32 devices in a mesh: seq: 8 (over y, x, core), head: 4 (over z).
Axes of the slice: x: 2, y: 2, z: 4, core: 2. Of those that a mesh axis runs over, the one named last changes fastest.
Arguments:
- inputs: bfloat16 [16384, 1024], P(('seq', 'head')), may hold values from -6 to 6
- norm1_gain: float32 [1024], replicated, may hold values from 0.1 to 1.9
- w_query: bfloat16 [1024, 1024], P(None, 'head'), may hold values from -0.1875 to 0.1875
- w_key: bfloat16 [1024, 1024], P(None, 'head'), may hold values from -0.1875 to 0.1875
- w_value: bfloat16 [1024, 1024], P(None, 'head'), may hold values from -0.1875 to 0.1875
- w_beta: bfloat16 [1024, 8], P(None, 'head'), may hold values from -0.1875 to 0.1875
- conv_weight: float32 [3, 4, 8, 128], P(None, None, 'head'), may hold values from -3 to 3
- head_gain: float32 [128], replicated, may hold values from 0.1 to 1.9
- w_out: bfloat16 [1024, 1024], P('head'), may hold values from -0.1875 to 0.1875
- norm2_gain: float32 [1024], replicated, may hold values from 0.1 to 1.9
- w_gate: bfloat16 [1024, 2816], P(None, 'head'), may hold values from -0.1875 to 0.1875
- w_up: bfloat16 [1024, 2816], P(None, 'head'), may hold values from -0.1875 to 0.1875
- w_down: bfloat16 [2816, 1024], P('head'), may hold values from -0.109375 to 0.109375
- seq_ids: int32 [16384], P('seq'), may hold values from 0 to 4, as said below
- cotangent: bfloat16 [16384, 1024], P('seq'), may hold values from -6 to 6
Outputs:
- output: bfloat16 [16384, 1024], P(('seq', 'head'))
- inputs_grad: float32 [16384, 1024], P(('seq', 'head'))
- norm1_gain_grad: float32 [1024], replicated
- w_query_grad: float32 [1024, 1024], P('seq', 'head')
- w_key_grad: float32 [1024, 1024], P('seq', 'head')
- w_value_grad: float32 [1024, 1024], P('seq', 'head')
- w_beta_grad: float32 [1024, 8], P('seq', 'head')
- conv_weight_grad: float32 [3, 4, 8, 128], P(None, None, 'head', 'seq')
- head_gain_grad: float32 [128], replicated
- w_out_grad: float32 [1024, 1024], P('head', 'seq')
- norm2_gain_grad: float32 [1024], replicated
- w_gate_grad: float32 [1024, 2816], P('seq', 'head')
- w_up_grad: float32 [1024, 2816], P('seq', 'head')
- w_down_grad: float32 [2816, 1024], P('head', 'seq')
The draws below stay inside these ranges and needn't reach their ends.
Inputs may be any that keep to these rules, and one draw needn't show every extreme that they name: `seq_ids`: sequence numbers never fall along the tokens and every number from 0 to 4 occurs; 4 marks the padding at the end, 1 to 512 tokens; one sequence, which one drawn from the seed, begins within the first 2048 tokens and ends within the last 2048 tokens; the others hold 1 to 256 tokens each.
All inputs are finite; a program needn't handle non-finite values.
Results may differ from the reference program's by a relative error of at most 0.023.
Values may be sent and summed in bfloat16 or wider, within the bound.
No kernel may reach another device: no remote copies, remote signals or barrier semaphores. Data moves between devices by JAX's collectives and lax.ppermute only.
A program may use at most 256 MiB of HBM per device.

```python
import jax
import jax.numpy as jnp
from jax import lax

D = 1024
H = 8
DK = 128
FF = 2816
CONV = 4
BLOCK = 64
SEQS = 4
SEQ_BLOCK = 2048
TOKENS = 16384


def sequence_numbers(key):
    pick_key, spread_key, tail_key = jax.random.split(key, 3)
    longest = jax.random.randint(pick_key, (), 0, SEQS)
    short_lens = jax.random.randint(spread_key, (SEQS,), 1, max(2, SEQ_BLOCK // 8 + 1))
    padding = jax.random.randint(tail_key, (), 1, max(2, SEQ_BLOCK // 4 + 1))
    slot_ids = jnp.arange(SEQS, dtype=jnp.int32)
    short_lens = jnp.where(slot_ids == longest, 0, short_lens)
    lengths = jnp.where(slot_ids == longest, TOKENS - padding - jnp.sum(short_lens), short_lens)
    seq_ends = jnp.cumsum(lengths).astype(jnp.int32)
    positions = jnp.arange(TOKENS, dtype=jnp.int32)
    return jnp.sum((positions[:, None] >= seq_ends[None, :]).astype(jnp.int32), axis=1).astype(jnp.int32)


def draw_seq_ids(key, part):
    key = jax.random.fold_in(key, 5)
    return sequence_numbers(key)


def with_spikes(result, key, source, target, shards_of, factor):
    def block_of(position):
        return (jnp.arange(result.shape[position]) // (result.shape[position] // shards_of)).reshape((-1,) + (1,) * (result.ndim - 1 - position))

    first = jax.random.permutation(key, shards_of)[block_of(target)]
    other_side = (block_of(target) + shards_of // 2) % shards_of
    return jnp.where((block_of(source) == first) | (block_of(source) == other_side), factor * result, result)


def steps_of(key, dims, cuts, smallest, largest):
    def one(axis_at, shards_of):
        heights = jax.random.uniform(jax.random.fold_in(jax.random.fold_in(key, 6), axis_at), (shards_of,), jnp.float32, smallest / len(cuts), largest / len(cuts))
        return jnp.repeat(jnp.exp(heights), dims[axis_at] // shards_of).reshape((-1,) + (1,) * (len(dims) - axis_at - 1))

    loudness = one(*cuts[0])
    for cut in cuts[1:]:
        loudness = loudness * one(*cut)
    return loudness


def scatter_about(key, shape, scale, bound, shards=(), kind=jnp.bfloat16):
    result = scale * jax.random.normal(key, shape, jnp.float32)
    if shards:
        result = result * steps_of(key, shape, shards, -0.22, 0.18)
    return jnp.clip(result, -bound, bound).astype(kind)


def noise_with(key, dims, deviation, limit, shards, heavy, kind=jnp.bfloat16):
    entries = deviation * jax.random.normal(key, dims, jnp.float32)
    if shards:
        entries = entries * steps_of(key, dims, shards, -0.22, 0.18)
    return jnp.clip(with_spikes(entries, jax.random.fold_in(key, 3), *heavy), -limit, limit).astype(kind)


def setup_inputs(seed: int = 0) -> dict:
    seeds = jax.random.split(jax.random.key(seed), 16)
    inputs = scatter_about(seeds[0], (TOKENS, D), 1.0, 6.0, ((0, 32),))
    norm1_gain = jnp.clip(1.0 + 0.18 * jax.random.normal(seeds[1], (D,), jnp.float32), 0.1, 1.9)
    w_query = scatter_about(seeds[2], (D, H * DK), D ** -0.5, 0.1875, ((1, 4),))
    w_key = scatter_about(seeds[3], (D, H * DK), D ** -0.5, 0.1875, ((1, 4),))
    w_value = scatter_about(seeds[4], (D, H * DK), D ** -0.5, 0.1875, ((1, 4),))
    w_beta = scatter_about(seeds[5], (D, H), D ** -0.5, 0.1875, ((1, 4),))
    conv_weight = scatter_about(seeds[6], (3, CONV, H, DK), 0.5, 3.0, ((2, 4),), jnp.float32)
    head_gain = jnp.clip(1.0 + 0.18 * jax.random.normal(seeds[7], (DK,), jnp.float32), 0.1, 1.9)
    w_out = scatter_about(seeds[8], (H * DK, D), (H * DK) ** -0.5, 0.1875, ((0, 4),))
    norm2_gain = jnp.clip(1.0 + 0.18 * jax.random.normal(seeds[9], (D,), jnp.float32), 0.1, 1.9)
    w_gate = scatter_about(seeds[10], (D, FF), D ** -0.5, 0.1875, ((1, 4),))
    w_up = scatter_about(seeds[11], (D, FF), D ** -0.5, 0.1875, ((1, 4),))
    w_down = scatter_about(seeds[12], (FF, D), FF ** -0.5, 0.109375, ((0, 4),))
    seq_ids = draw_seq_ids(jax.random.fold_in(seeds[15], 71), 0)
    cotangent = noise_with(seeds[14], (TOKENS, D), 1.0, 6.0, ((0, 8),), (0, 1, 8, 2.0))
    return dict(inputs=inputs, norm1_gain=norm1_gain, w_query=w_query, w_key=w_key, w_value=w_value, w_beta=w_beta, conv_weight=conv_weight, head_gain=head_gain, w_out=w_out, norm2_gain=norm2_gain, w_gate=w_gate, w_up=w_up, w_down=w_down, seq_ids=seq_ids, cotangent=cotangent)


precise = lax.Precision.HIGHEST
epsilon = 1e-06
beta_shift = 4.0

@jax.custom_vjp
def low(v):
    return lax.optimization_barrier(v.astype(jnp.bfloat16)).astype(jnp.float32)

@jax.custom_vjp
def low_back(v):
    return v

def low_keep(v):
    return (low(v), None)

def low_pass(kept, grad):
    return (grad,)

def back_keep(v):
    return (v, None)

def back_low(kept, grad):
    return (low(grad),)
low.defvjp(low_keep, low_pass)
low_back.defvjp(back_keep, back_low)

def rms_scale(values, scale_gain):
    return values * lax.rsqrt(lax.optimization_barrier(jnp.mean(values * values, -1, keepdims=True)) + epsilon) * scale_gain

def unit_rows(values):
    return values * lax.rsqrt(lax.optimization_barrier(jnp.sum(values * values, -1, keepdims=True)) + epsilon)

def matmul(left_side, right_hand):
    return jnp.dot(left_side, right_hand, precision=precise)

def prepare(queries, keys_in, values_in, beta_rate, block_ids, prev_ids):
    block_len = block_ids.shape[1]
    same_seq = (block_ids[:, :, None] == block_ids[:, None, :]).astype(jnp.float32)
    carry_in = (block_ids == prev_ids[:, None]).astype(jnp.float32)
    to_last = (block_ids == block_ids[:, -1:]).astype(jnp.float32)
    row_pos = lax.broadcasted_iota(jnp.int32, (block_len, block_len), 0)
    col_pos = lax.broadcasted_iota(jnp.int32, (block_len, block_len), 1)
    strict_mask = (row_pos > col_pos).astype(jnp.float32)[None] * same_seq
    causal_mask = (row_pos >= col_pos).astype(jnp.float32)[None] * same_seq
    queries_h = jnp.transpose(queries, (0, 2, 1, 3))
    keys_h = jnp.transpose(keys_in, (0, 2, 1, 3))
    values_h = jnp.transpose(values_in, (0, 2, 1, 3))
    beta_h = jnp.transpose(beta_rate, (0, 2, 1))[..., None]
    carry_h = carry_in[:, None, :, None]
    key_scores = jnp.einsum('chid,chjd->chij', keys_h, keys_h, precision=precise) * strict_mask[:, None]
    system = jnp.eye(block_len, dtype=jnp.float32) + beta_h * key_scores
    right_side = jnp.concatenate([beta_h * values_h, beta_h * carry_h * keys_h], axis=-1)
    solved = lax.linalg.triangular_solve(system, right_side, left_side=True, lower=True, unit_diagonal=True)
    value_width = values_in.shape[-1]
    key_width = keys_in.shape[-1]
    pseudo = solved[..., :value_width]
    erasers = solved[..., value_width:]
    scores = jnp.einsum('chid,chjd->chij', queries_h, keys_h, precision=precise) * causal_mask[:, None]
    base_out = jnp.einsum('chij,chjv->chiv', scores, pseudo, precision=precise)
    reach_q = carry_h * queries_h - jnp.einsum('chij,chjd->chid', scores, erasers, precision=precise)
    last_keys = keys_h * to_last[:, None, :, None]
    step_a = carry_in[:, -1][:, None, None, None] * jnp.eye(key_width, dtype=jnp.float32) - jnp.einsum('chid,chie->chde', erasers, last_keys, precision=precise)
    step_b = jnp.einsum('chiv,chie->chve', pseudo, last_keys, precision=precise)
    return (base_out, reach_q, step_a, step_b)

def delta_rule(queries, keys_in, values_in, beta_rate, seq_ids):
    token_count = seq_ids.shape[0]
    blocks = token_count // BLOCK
    head_count = queries.shape[1]
    shaped = [array_in.reshape(blocks, BLOCK, head_count, -1) for array_in in (queries, keys_in, values_in)]
    block_ids = seq_ids.reshape(blocks, BLOCK)
    prev_ids = jnp.concatenate([jnp.full((1,), -1, jnp.int32), block_ids[:-1, -1]])
    base_out, reach_q, step_a, step_b = prepare(shaped[0], shaped[1], shaped[2], beta_rate.reshape(blocks, BLOCK, head_count), block_ids, prev_ids)

    def advance(state_now, pieces):
        return (jnp.einsum('hvd,hde->hve', state_now, pieces[0], precision=precise) + pieces[1], state_now)
    initial = jnp.zeros((head_count, values_in.shape[-1], keys_in.shape[-1]), jnp.float32)
    final_state, starts = lax.scan(advance, initial, (step_a, step_b))
    outputs = base_out + jnp.einsum('chid,chvd->chiv', reach_q, starts, precision=precise)
    return jnp.transpose(outputs, (0, 2, 1, 3)).reshape(token_count, head_count, -1)

def convolve(projected, seq_ids, conv_weight):
    tap_count = conv_weight.shape[1]
    kernel = jnp.transpose(conv_weight, (1, 0, 2, 3)).reshape(tap_count, -1)
    summed = projected * kernel[0]
    for lag_step in range(1, tap_count):
        shifted = jnp.concatenate([jnp.zeros((lag_step, projected.shape[1]), jnp.float32), projected[:-lag_step]], 0)
        prior_ids = jnp.concatenate([jnp.full((lag_step,), -1, jnp.int32), seq_ids[:-lag_step]])
        summed = summed + shifted * kernel[lag_step] * (prior_ids == seq_ids).astype(jnp.float32)[:, None]
    return jax.nn.silu(summed)

def layer_forward(inputs, norm1_gain, w_query, w_key, w_value, w_beta, conv_weight, head_gain, w_out, norm2_gain, w_gate, w_up, w_down, seq_ids):
    token_count = inputs.shape[0]
    head_count = conv_weight.shape[2]
    mask_f = (seq_ids < SEQS).astype(jnp.float32)
    normed = low(rms_scale(inputs, norm1_gain))
    projected = low_back(jnp.concatenate([matmul(normed, w_query), matmul(normed, w_key), matmul(normed, w_value)], 1))
    logits = low_back(matmul(normed, w_beta))
    mixed_rows = convolve(projected, seq_ids, conv_weight).reshape(token_count, 3, head_count, -1)
    queries = low(unit_rows(mixed_rows[:, 0]))
    keys_in = low(unit_rows(mixed_rows[:, 1]))
    values_in = low(mixed_rows[:, 2])
    beta_rate = jax.nn.sigmoid(logits - beta_shift) * mask_f[:, None]
    attended = delta_rule(queries, keys_in, values_in, beta_rate, seq_ids)
    head_out = low((rms_scale(attended, head_gain) * mask_f[:, None, None]).reshape(token_count, -1))
    residual = inputs + low_back(matmul(head_out, w_out))
    normed_two = low(rms_scale(residual, norm2_gain))
    gate_proj = low_back(matmul(normed_two, w_gate))
    up_proj = low_back(matmul(normed_two, w_up))
    hidden = low(jax.nn.silu(gate_proj) * up_proj)
    return residual + low_back(matmul(hidden, w_down))

def reference(inputs, norm1_gain, w_query, w_key, w_value, w_beta, conv_weight, head_gain, w_out, norm2_gain, w_gate, w_up, w_down, seq_ids, cotangent):
    weights = [inputs, norm1_gain, w_query, w_key, w_value, w_beta, conv_weight, head_gain, w_out, norm2_gain, w_gate, w_up, w_down]
    floats = [array_in.astype(jnp.float32) for array_in in weights]

    def forward(*params):
        return layer_forward(*params, seq_ids)
    output, pullback = jax.vjp(forward, *floats)
    gradients = pullback(cotangent.astype(jnp.float32))
    return (output.astype(jnp.bfloat16), gradients[0], gradients[1], gradients[2], gradients[3], gradients[4], gradients[5], gradients[6], gradients[7], gradients[8], gradients[9], gradients[10], gradients[11], gradients[12])
```

```python
import functools

import jax
import jax.numpy as jnp
from jax import lax
from jax.experimental import pallas as pl
from jax.experimental.pallas import tpu as pltpu
from jax.sharding import PartitionSpec as P

SEQS = 4
CHUNK = 128
HALO = 8
epsilon = 1e-06
beta_shift = 4.0
f32 = jnp.float32
bf16 = jnp.bfloat16
WHOLE = ("seq", "head")
BY_HEAD = ("head", "seq")


def nn(a, b):
    return lax.dot_general(a, b, (((1,), (0,)), ((), ())), preferred_element_type=f32)


def nt(a, b):
    return lax.dot_general(a, b, (((1,), (1,)), ((), ())), preferred_element_type=f32)


def tn(a, b):
    return lax.dot_general(a, b, (((0,), (0,)), ((), ())), preferred_element_type=f32)


def params(mib=56, grid=1):
    return pltpu.CompilerParams(
        vmem_limit_bytes=mib << 20, dimension_semantics=("arbitrary",) * grid
    )


def lead(*shape):
    zeros = (0,) * len(shape)
    return pl.BlockSpec((None,) + shape, lambda i: (i,) + zeros)


def same(*shape):
    zeros = (0,) * len(shape)
    return pl.BlockSpec(shape, lambda i: zeros)


def sds(shape, kind):
    return jax.ShapeDtypeStruct(shape, kind)


def chunk_masks(idc_ref, idr_ref, c):
    base = HALO + c * CHUNK
    own = idc_ref[base : base + CHUNK, :]
    row = idr_ref[0:1, base : base + CHUNK]
    prev = idc_ref[base - 1 : base, :]
    last = idc_ref[base + CHUNK - 1 : base + CHUNK, :]
    equal = own == row
    carry = (own == prev).astype(f32)
    to_last = (own == last).astype(f32)
    carry_last = (last == prev).astype(f32)
    return equal, carry, to_last, carry_last


def positions():
    row = lax.broadcasted_iota(jnp.int32, (CHUNK, CHUNK), 0)
    col = lax.broadcasted_iota(jnp.int32, (CHUNK, CHUNK), 1)
    return row, col


def front_kernel(chunks, proj_ref, cw_ref, lgt_ref, idc_ref, idr_ref, qkv_ref, sum_ref, uw_ref, inv_ref, pre_ref, tot_ref):
    rows = CHUNK
    for b in range(6):
        part, hh = b // 2, b % 2
        cols = slice(b * 128, (b + 1) * 128)
        taps = [cw_ref[(part * 4 + j) * 2 + hh : (part * 4 + j) * 2 + hh + 1, :] for j in range(4)]
        for c in range(chunks):
            base = HALO + c * rows
            own = idc_ref[base : base + rows, :]
            acc = proj_ref[base : base + rows, cols] * taps[0]
            for j in range(1, 4):
                prior = idc_ref[base - j : base - j + rows, :]
                acc = acc + jnp.where(prior == own, proj_ref[base - j : base - j + rows, cols], 0.0) * taps[j]
            sum_ref[c * rows : (c + 1) * rows, cols] = acc
            mixed = acc / (1.0 + jnp.exp(-acc))
            if part < 2:
                mixed = mixed * lax.rsqrt(jnp.sum(mixed * mixed, -1, keepdims=True) + epsilon)
            qkv_ref[c * rows : (c + 1) * rows, cols] = mixed.astype(bf16)
    row, col = positions()
    differ = row ^ col
    strict = row > col
    units = [(hh, c) for c in range(chunks) for hh in range(2)]
    lower, inv, scaled = {}, {}, {}
    for hh, c in units:
        equal, carry, _, _ = chunk_masks(idc_ref, idr_ref, c)
        at = slice(c * CHUNK, (c + 1) * CHUNK)
        beta = jax.nn.sigmoid(lgt_ref[at, hh * 128 : (hh + 1) * 128] - beta_shift)
        beta = jnp.where(idc_ref[HALO + c * CHUNK : HALO + (c + 1) * CHUNK, :] < SEQS, beta, 0.0)
        keys = qkv_ref[at, 256 + hh * 128 : 256 + (hh + 1) * 128]
        values = qkv_ref[at, 512 + hh * 128 : 512 + (hh + 1) * 128]
        low = jnp.where(equal & strict, nt(keys, keys), 0.0) * beta
        lower[hh, c] = low
        inv[hh, c] = jnp.where(row == col, 1.0, 0.0) - jnp.where(differ == 1, low, 0.0)
        scaled[hh, c] = jnp.concatenate(
            [(values.astype(f32) * beta).astype(bf16), (keys.astype(f32) * (beta * carry)).astype(bf16)], axis=1
        )
    for k in range(1, 7):
        level = (differ >> k) == 1
        for u in units:
            off = jnp.where(level, lower[u], 0.0).astype(bf16)
            half = inv[u].astype(bf16)
            inv[u] = inv[u] - nn(half, nn(off, half).astype(bf16))
    for hh, c in units:
        at = slice(c * CHUNK, (c + 1) * CHUNK)
        half = inv[hh, c].astype(bf16)
        inv_ref[hh, at, :] = half
        uw_ref[hh, at, :] = nn(half, scaled[hh, c]).astype(bf16)
    eye = jnp.where(row == col, 1.0, 0.0)
    state = [[eye, jnp.zeros((CHUNK, CHUNK), f32)] for _ in range(2)]
    for c in range(chunks):
        at = slice(c * CHUNK, (c + 1) * CHUNK)
        _, _, to_last, carry_last = chunk_masks(idc_ref, idr_ref, c)
        for hh in range(2):
            packed = jnp.concatenate([state[hh][0].astype(bf16), state[hh][1].astype(bf16)], axis=1)
            pre_ref[hh, c] = packed
            moved = nn(uw_ref[hh, at, 128:256], packed)
            change = jnp.concatenate(
                [(-moved[:, :128]).astype(bf16), (uw_ref[hh, at, 0:128].astype(f32) - moved[:, 128:]).astype(bf16)], axis=1
            )
            keys = qkv_ref[at, 256 + hh * 128 : 256 + (hh + 1) * 128]
            kept = (keys.astype(f32) * to_last).astype(bf16)
            step = tn(kept, change)
            state[hh] = [state[hh][0] * carry_last + step[:, :128], state[hh][1] * carry_last + step[:, 128:]]
    for hh in range(2):
        tot_ref[hh] = jnp.concatenate([state[hh][0].astype(bf16), state[hh][1].astype(bf16)], axis=1)


def reach_kernel(chunks, qkv_ref, uw_ref, pre_ref, idc_ref, idr_ref, score_ref, reach_ref, base_ref, far_ref):
    row, col = positions()
    causal = row >= col
    for c in range(chunks):
        at = slice(c * CHUNK, (c + 1) * CHUNK)
        equal, carry, _, _ = chunk_masks(idc_ref, idr_ref, c)
        for hh in range(2):
            queries = qkv_ref[at, hh * 128 : (hh + 1) * 128]
            keys = qkv_ref[at, 256 + hh * 128 : 256 + (hh + 1) * 128]
            score = jnp.where(causal & equal, nt(queries, keys), 0.0).astype(bf16)
            score_ref[hh, at, :] = score
            both = nn(score, uw_ref[hh, at, :])
            reach = (queries.astype(f32) * carry - both[:, 128:]).astype(bf16)
            reach_ref[hh, at, :] = reach
            far = nn(reach, pre_ref[hh, c])
            far_ref[hh, at, :] = far[:, :128].astype(bf16)
            base_ref[hh, at, :] = both[:, :128] + far[:, 128:]


def attend_kernel(base_ref, far_ref, state_ref, gain_ref, idc_ref, out_ref, head_ref):
    rows = base_ref.shape[1]
    mask = (idc_ref[HALO : HALO + rows, :] < SEQS).astype(f32)
    for hh in range(2):
        out = base_ref[hh] + nn(far_ref[hh], state_ref[hh])
        out_ref[hh] = out
        rh = lax.rsqrt(jnp.mean(out * out, -1, keepdims=True) + epsilon)
        head_ref[:, hh * 128 : (hh + 1) * 128] = (out * rh * gain_ref[0:1, :] * mask).astype(bf16)


def ffn_kernel(normed_ref, dy_ref, wg_ref, wu_ref, wd_ref, out_ref, grad_ref, dg_ref, du_ref, dd_ref):
    step = pl.program_id(0)
    normed, dy = normed_ref[...], dy_ref[...]
    gate = nn(normed, wg_ref[...])
    up = nn(normed, wu_ref[...])
    sig = 1.0 / (1.0 + jnp.exp(-gate))
    act = gate * sig
    hidden = (act * up).astype(bf16)
    grad_hidden = nt(dy, wd_ref[...])
    grad_gate = (grad_hidden * up * (sig * (1.0 + gate * (1.0 - sig)))).astype(bf16)
    grad_up = (grad_hidden * act).astype(bf16)
    out = nn(hidden, wd_ref[...])
    back = nt(grad_gate, wg_ref[...]) + nt(grad_up, wu_ref[...])

    @pl.when(step == 0)
    def _():
        out_ref[...] = out
        grad_ref[...] = back

    @pl.when(step > 0)
    def _():
        out_ref[...] += out
        grad_ref[...] += back

    dd_ref[...] = tn(hidden, dy).astype(bf16)
    dg_ref[...] = tn(normed, grad_gate).astype(bf16)
    du_ref[...] = tn(normed, grad_up).astype(bf16)


def head_back_kernel(gho_ref, att_ref, far_ref, gain_ref, idc_ref, datt_ref, local_ref, gain_grad_ref):
    rows = att_ref.shape[1]
    mask = (idc_ref[HALO : HALO + rows, :] < SEQS).astype(f32)
    gain = gain_ref[0:1, :]
    total = jnp.zeros((1, 128), f32)
    for hh in range(2):
        out = att_ref[hh]
        go = gho_ref[:, hh * 128 : (hh + 1) * 128] * mask
        rh = lax.rsqrt(jnp.mean(out * out, -1, keepdims=True) + epsilon)
        total = total + jnp.sum(go * out * rh, 0, keepdims=True)
        inner = jnp.mean(out * gain * go, -1, keepdims=True)
        grad = (rh * gain * go - out * (rh * rh * rh) * inner).astype(bf16)
        datt_ref[hh] = grad
        local_ref[hh] = tn(far_ref[hh], grad).astype(bf16)
    gain_grad_ref[...] = jnp.broadcast_to(total, (8, 128))


def inner_back_kernel(chunks, qkv_ref, uw_ref, pre_ref, score_ref, datt_ref, state_ref, idc_ref, idr_ref, states_ref, pseudo_ref, dq_ref, dk_ref, dp_ref):
    row, col = positions()
    causal = row >= col
    for c in range(chunks):
        at = slice(c * CHUNK, (c + 1) * CHUNK)
        equal, carry, _, _ = chunk_masks(idc_ref, idr_ref, c)
        for hh in range(2):
            queries = qkv_ref[at, hh * 128 : (hh + 1) * 128]
            keys = qkv_ref[at, 256 + hh * 128 : 256 + (hh + 1) * 128]
            grad = datt_ref[hh, at, :]
            state = (nn(pre_ref[hh, c, :, 0:128], state_ref[hh]) + pre_ref[hh, c, :, 128:256].astype(f32)).astype(bf16)
            states_ref[hh, c] = state
            pseudo = (uw_ref[hh, at, 0:128].astype(f32) - nn(uw_ref[hh, at, 128:256], state)).astype(bf16)
            pseudo_ref[hh, at, :] = pseudo
            grad_score = jnp.where(causal & equal, nt(grad, pseudo), 0.0).astype(bf16)
            dq_ref[hh, at, :] = nt(grad, state) * carry + nn(grad_score, keys)
            dk_ref[hh, at, :] = tn(grad_score, queries)
            dp_ref[hh, at, :] = tn(score_ref[hh, at, :], grad)


def outer_back_kernel(
    chunks, qkv_ref, uw_ref, inv_ref, reach_ref, datt_ref, states_ref, pseudo_ref, dq_ref, dk_ref, dp_ref,
    sum_ref, proj_ref, lgt_ref, gout_ref, cw_ref, idc_ref, idr_ref,
    gp_ref, dcw_ref, dlgt_ref, dqkv, pad,
):
    row, col = positions()
    strict = row > col
    lane = lax.broadcasted_iota(jnp.int32, (CHUNK, 128), 1)
    grad_state = [gout_ref[hh].astype(f32) for hh in range(2)]
    for c in range(chunks - 1, -1, -1):
        at = slice(c * CHUNK, (c + 1) * CHUNK)
        equal, carry, to_last, carry_last = chunk_masks(idc_ref, idr_ref, c)
        own = idc_ref[HALO + c * CHUNK : HALO + (c + 1) * CHUNK, :]
        dlgt = jnp.zeros((CHUNK, 128), f32)
        for hh in range(2):
            keys = qkv_ref[at, 256 + hh * 128 : 256 + (hh + 1) * 128]
            keys_f = keys.astype(f32)
            values = qkv_ref[at, 512 + hh * 128 : 512 + (hh + 1) * 128]
            kept = (keys_f * to_last).astype(bf16)
            packed = grad_state[hh].astype(bf16)
            push = nn(kept, packed)
            grad_state[hh] = grad_state[hh] * carry_last + tn(reach_ref[hh, at, :], datt_ref[hh, at, :]) - tn(
                uw_ref[hh, at, 128:256], push.astype(bf16)
            )
            full = (dp_ref[hh, at, :] + push).astype(bf16)
            solved = tn(inv_ref[hh, at, :], full)
            solved_h = solved.astype(bf16)
            pseudo = pseudo_ref[hh, at, :]
            gate = jax.nn.sigmoid(lgt_ref[at, hh * 128 : (hh + 1) * 128] - beta_shift)
            mask = (own < SEQS).astype(f32)
            beta = gate * mask
            back = nt(solved_h, states_ref[hh, c]) * carry
            outer = jnp.where(equal & strict, nt(solved_h, pseudo), 0.0)
            overlap = nt(keys, keys)
            rate = jnp.sum(solved * values.astype(f32) - back * keys_f - outer * overlap, -1, keepdims=True)
            dlgt = jnp.where(lane == hh, rate * mask * gate * (1.0 - gate), dlgt)
            mixed = (outer * beta).astype(bf16)
            dqkv[at, 256 + hh * 128 : 256 + (hh + 1) * 128] = (
                dk_ref[hh, at, :] + nt(pseudo, packed) * to_last - beta * back - nn(mixed, keys) - tn(mixed, keys)
            )
            dqkv[at, 512 + hh * 128 : 512 + (hh + 1) * 128] = beta * solved
            dqkv[at, hh * 128 : (hh + 1) * 128] = dq_ref[hh, at, :]
        dlgt_ref[at, :] = dlgt
    rows = CHUNK
    length = chunks * CHUNK
    for b in range(6):
        part, hh = b // 2, b % 2
        cols = slice(b * 128, (b + 1) * 128)
        taps = [cw_ref[(part * 4 + j) * 2 + hh : (part * 4 + j) * 2 + hh + 1, :] for j in range(4)]
        pad[0:HALO, :] = jnp.zeros((HALO, 128), f32)
        pad[HALO + length : 2 * HALO + length, :] = jnp.zeros((HALO, 128), f32)
        sums = [jnp.zeros((1, 128), f32) for _ in range(4)]
        for c in range(chunks):
            at = slice(c * rows, (c + 1) * rows)
            base = HALO + c * rows
            u = sum_ref[at, cols]
            sig = 1.0 / (1.0 + jnp.exp(-u))
            grad = dqkv[at, cols]
            if part < 2:
                mixed = u * sig
                r = lax.rsqrt(jnp.sum(mixed * mixed, -1, keepdims=True) + epsilon)
                grad = r * grad - mixed * ((r * r * r) * jnp.sum(mixed * grad, -1, keepdims=True))
            grad = grad * (sig * (1.0 + u * (1.0 - sig)))
            pad[base : base + rows, :] = grad
            own = idc_ref[base : base + rows, :]
            sums[0] = sums[0] + jnp.sum(grad * proj_ref[base : base + rows, cols], 0, keepdims=True)
            for j in range(1, 4):
                prior = idc_ref[base - j : base - j + rows, :]
                sums[j] = sums[j] + jnp.sum(
                    jnp.where(prior == own, proj_ref[base - j : base - j + rows, cols], 0.0) * grad, 0, keepdims=True
                )
        for j in range(4):
            dcw_ref[(part * 4 + j) * 2 + hh : (part * 4 + j) * 2 + hh + 1, :] = sums[j]
        for start, size in [(0, HALO)] + [(HALO + c * rows, rows) for c in range(chunks)]:
            own = idc_ref[start : start + size, :]
            acc = pad[start : start + size, :] * taps[0]
            for j in range(1, 4):
                later = idc_ref[start + j : start + j + size, :]
                acc = acc + jnp.where(later == own, pad[start + j : start + j + size, :], 0.0) * taps[j]
            gp_ref[start : start + size, cols] = acc


def exchange_forward(tot, n_seq, s):
    groups = tot.shape[0]
    got = lax.all_to_all(tot, "head", 0, 0, tiled=True)

    def apply(a, x):
        return jnp.einsum("hij,hjk->hik", a.astype(bf16), x.astype(bf16), preferred_element_type=f32)

    def after(second, first):
        moved = apply(second[..., :128], first)
        return jnp.concatenate([moved[..., :128], moved[..., 128:] + second[..., 128:].astype(f32)], -1)

    whole = got[0].astype(f32)
    for j in range(1, groups):
        whole = after(got[j], whole)
    eye = jnp.broadcast_to(jnp.eye(128, dtype=f32), (2, 128, 128))
    prefix = jnp.concatenate([eye, jnp.zeros((2, 128, 128), f32)], -1)
    suffix = eye
    kept = []
    k = 1
    while k < n_seq:
        mine = whole.astype(bf16)
        other = lax.ppermute(mine, "seq", [(i, i ^ k) for i in range(n_seq)])
        upper = (s & k) != 0
        first = jnp.where(upper, other, mine)
        second = jnp.where(upper, mine, other)
        kept.append((first[..., :128], suffix.astype(bf16)))
        prefix = jnp.where(upper, after(prefix, other), prefix)
        suffix = jnp.where(upper, suffix, apply(other[..., :128], suffix))
        whole = after(second, first)
        k *= 2
    state = prefix[..., 128:]
    states = [state.astype(bf16)]
    for j in range(groups - 1):
        state = apply(got[j][..., :128], state) + got[j][..., 128:].astype(f32)
        states.append(state.astype(bf16))
    back = lax.all_to_all(jnp.stack(states), "head", 0, 0, tiled=True)
    return back, got, kept


def exchange_backward(local, got, kept, n_seq, s):
    groups = local.shape[0]
    grads = lax.all_to_all(local, "head", 0, 0, tiled=True)

    def pull(a, g):
        return jnp.einsum("hij,hik->hjk", a.astype(bf16), g.astype(bf16), preferred_element_type=f32)

    whole = grads[groups - 1].astype(f32)
    for j in range(groups - 2, -1, -1):
        whole = pull(got[j][..., :128], whole) + grads[j].astype(f32)
    later = jnp.zeros_like(whole)
    k = 1
    for first_a, suffix in kept:
        mine = whole.astype(bf16)
        other = lax.ppermute(mine, "seq", [(i, i ^ k) for i in range(n_seq)])
        upper = (s & k) != 0
        later = jnp.where(upper, later, pull(suffix, other) + later)
        first = jnp.where(upper, other, mine)
        second = jnp.where(upper, mine, other)
        whole = pull(first_a, second) + first.astype(f32)
        k *= 2
    outs = [later.astype(bf16)]
    for j in range(groups - 1, 0, -1):
        later = pull(got[j][..., :128], later) + grads[j].astype(f32)
        outs.append(later.astype(bf16))
    return lax.all_to_all(jnp.stack(outs[::-1]), "head", 0, 0, tiled=True)


def local(
    inputs, norm1_gain, w_query, w_key, w_value, w_beta, conv_weight, head_gain, w_out, norm2_gain, w_gate, w_up, w_down,
    seq_ids, cotangent,
):
    n_seq, n_head = lax.axis_size("seq"), lax.axis_size("head")
    s, z = lax.axis_index("seq"), lax.axis_index("head")
    rows, width = inputs.shape
    ff = w_gate.shape[1]
    chunks = rows // CHUNK
    ext = rows + HALO
    count = n_seq * n_head
    part = width // n_seq

    def slice_of(array, size):
        return lax.dynamic_slice_in_dim(array, s * size, size, 0)

    def gathered(array):
        piece = slice_of(array, array.shape[0] // n_seq)
        full = lax.all_gather(piece, BY_HEAD, axis=0, tiled=True)
        return full.reshape((n_head,) + array.shape)

    w_proj = gathered(jnp.concatenate([w_query, w_key, w_value], 1))
    small = jnp.concatenate([conv_weight.reshape(-1, 128), w_beta.astype(f32).T.reshape(-1, 128)], 0)
    small = lax.all_gather(small, "head", axis=0)
    taps = small[:, : 24, :]
    w_beta_all = small[:, 24:, :].reshape(n_head * 2, width).astype(bf16)
    w_out_all = gathered(w_out).reshape(-1, width)
    w_gate_all = gathered(w_gate)
    w_up_all = gathered(w_up)
    w_down_all = gathered(w_down)

    before = lax.ppermute(inputs[-HALO:], WHOLE, [(i, i + 1) for i in range(count - 1)])
    ids_before = lax.ppermute(seq_ids[-HALO:], "seq", [(i, i + 1) for i in range(n_seq - 1)])
    ids_before = jnp.where(s == 0, -1, ids_before)
    ids = lax.dynamic_slice_in_dim(jnp.concatenate([ids_before, seq_ids]), z * rows, ext)
    ids_pad = jnp.concatenate([ids, jnp.full((HALO,), -2, jnp.int32)])
    idc = jnp.broadcast_to(ids_pad[:, None], (ext + HALO, 128))
    idr = jnp.broadcast_to(ids[None, :], (8, ext))
    dy = lax.dynamic_slice_in_dim(cotangent, z * rows, rows, 0)

    x_ext = jnp.concatenate([before, inputs], 0).astype(f32)
    r1_ext = lax.rsqrt(jnp.mean(x_ext * x_ext, -1, keepdims=True) + epsilon)
    normed_ext = (x_ext * r1_ext * norm1_gain).astype(bf16)
    normed = normed_ext[HALO:]
    x, r1 = x_ext[HALO:], r1_ext[HALO:]
    projected = jnp.stack([jnp.dot(normed_ext, w_proj[g], preferred_element_type=f32) for g in range(n_head)])
    beta_wide = jnp.broadcast_to(w_beta_all.reshape(n_head, 2, 1, width), (n_head, 2, 128, width)).reshape(n_head, 256, width)
    logits = jnp.einsum("td,gcd->gtc", normed, beta_wide, preferred_element_type=f32)

    idc_spec, idr_spec = same(ext + HALO, 128), same(8, ext)
    qkv, summed, uw, inverse, prefixes, totals = pl.pallas_call(
        functools.partial(front_kernel, chunks),
        grid=(n_head,),
        in_specs=[lead(ext, 768), lead(24, 128), lead(rows, 256), idc_spec, idr_spec],
        out_specs=[
            lead(rows, 768), lead(rows, 768), lead(2, rows, 256), lead(2, rows, 128), lead(2, chunks, 128, 256),
            lead(2, 128, 256),
        ],
        out_shape=[
            sds((n_head, rows, 768), bf16), sds((n_head, rows, 768), f32), sds((n_head, 2, rows, 256), bf16),
            sds((n_head, 2, rows, 128), bf16), sds((n_head, 2, chunks, 128, 256), bf16), sds((n_head, 2, 128, 256), bf16),
        ],
        compiler_params=params(),
        name="front",
    )(projected, taps, logits, idc, idr)
    state_in, got, kept = exchange_forward(totals, n_seq, s)
    score, reach, base, far = pl.pallas_call(
        functools.partial(reach_kernel, chunks),
        grid=(n_head,),
        in_specs=[lead(rows, 768), lead(2, rows, 256), lead(2, chunks, 128, 256), idc_spec, idr_spec],
        out_specs=[lead(2, rows, 128)] * 4,
        out_shape=[sds((n_head, 2, rows, 128), kind) for kind in (bf16, bf16, f32, bf16)],
        compiler_params=params(),
        name="reach",
    )(qkv, uw, prefixes, idc, idr)
    gain_rows = jnp.broadcast_to(head_gain[None, :], (8, 128))
    attended, head_out = pl.pallas_call(
        attend_kernel,
        grid=(n_head,),
        in_specs=[lead(2, rows, 128), lead(2, rows, 128), lead(2, 128, 128), same(8, 128), idc_spec],
        out_specs=[lead(2, rows, 128), pl.BlockSpec((rows, 256), lambda i: (0, i))],
        out_shape=[sds((n_head, 2, rows, 128), f32), sds((rows, n_head * 256), bf16)],
        compiler_params=params(),
        name="attend",
    )(base, far, state_in, gain_rows, idc)

    residual = x + jnp.dot(head_out, w_out_all, preferred_element_type=f32)
    r2 = lax.rsqrt(jnp.mean(residual * residual, -1, keepdims=True) + epsilon)
    normed_two = (residual * r2 * norm2_gain).astype(bf16)
    ffn_out, grad_two, grad_gate, grad_up, grad_down = pl.pallas_call(
        ffn_kernel,
        grid=(n_head,),
        in_specs=[same(rows, width), same(rows, width), lead(width, ff), lead(width, ff), lead(ff, width)],
        out_specs=[same(rows, width), same(rows, width), lead(width, ff), lead(width, ff), lead(ff, width)],
        out_shape=[
            sds((rows, width), f32), sds((rows, width), f32), sds((n_head, width, ff), bf16), sds((n_head, width, ff), bf16),
            sds((n_head, ff, width), bf16),
        ],
        compiler_params=params(60),
        name="ffn",
    )(normed_two, dy, w_gate_all, w_up_all, w_down_all)
    output = (residual + ffn_out).astype(bf16)

    grad_norm_two = jnp.sum(grad_two * residual * r2, 0)
    scaled_two = norm2_gain * grad_two
    grad_residual = dy.astype(f32) + r2 * scaled_two - residual * (r2 * r2 * r2) * jnp.mean(residual * scaled_two, -1, keepdims=True)
    grad_mixer = grad_residual.astype(bf16)
    grad_out = jnp.einsum("tc,td->cd", head_out, grad_mixer, preferred_element_type=f32).astype(bf16)
    grad_head_out = jnp.einsum("td,cd->tc", grad_mixer, w_out_all, preferred_element_type=f32)

    datt, local_grad, gain_part = pl.pallas_call(
        head_back_kernel,
        grid=(n_head,),
        in_specs=[
            pl.BlockSpec((rows, 256), lambda i: (0, i)), lead(2, rows, 128), lead(2, rows, 128), same(8, 128), idc_spec,
        ],
        out_specs=[lead(2, rows, 128), lead(2, 128, 128), lead(8, 128)],
        out_shape=[sds((n_head, 2, rows, 128), bf16), sds((n_head, 2, 128, 128), bf16), sds((n_head, 8, 128), f32)],
        compiler_params=params(),
        name="head_back",
    )(grad_head_out, attended, far, gain_rows, idc)
    grad_out_state = exchange_backward(local_grad, got, kept, n_seq, s)
    states, pseudo, dq, dk, dp = pl.pallas_call(
        functools.partial(inner_back_kernel, chunks),
        grid=(n_head,),
        in_specs=[
            lead(rows, 768), lead(2, rows, 256), lead(2, chunks, 128, 256), lead(2, rows, 128), lead(2, rows, 128),
            lead(2, 128, 128), idc_spec, idr_spec,
        ],
        out_specs=[lead(2, chunks, 128, 128)] + [lead(2, rows, 128)] * 4,
        out_shape=[sds((n_head, 2, chunks, 128, 128), bf16)]
        + [sds((n_head, 2, rows, 128), kind) for kind in (bf16, f32, f32, f32)],
        compiler_params=params(),
        name="inner_back",
    )(qkv, uw, prefixes, score, datt, state_in, idc, idr)
    gp_ext, grad_taps, grad_logits = pl.pallas_call(
        functools.partial(outer_back_kernel, chunks),
        grid=(n_head,),
        in_specs=[
            lead(rows, 768), lead(2, rows, 256), lead(2, rows, 128), lead(2, rows, 128), lead(2, rows, 128),
            lead(2, chunks, 128, 128), lead(2, rows, 128), lead(2, rows, 128), lead(2, rows, 128), lead(2, rows, 128),
            lead(rows, 768), lead(ext, 768), lead(rows, 256), lead(2, 128, 128), lead(24, 128), idc_spec, idr_spec,
        ],
        out_specs=[lead(ext, 768), lead(24, 128), lead(rows, 128)],
        out_shape=[sds((n_head, ext, 768), f32), sds((n_head, 24, 128), f32), sds((n_head, rows, 128), f32)],
        scratch_shapes=[pltpu.VMEM((rows, 768), f32), pltpu.VMEM((rows + 2 * HALO, 128), f32)],
        compiler_params=params(),
        name="outer_back",
    )(
        qkv, uw, inverse, reach, datt, states, pseudo, dq, dk, dp, summed, projected, logits, grad_out_state, taps, idc, idr,
    )

    from_next = lax.ppermute(gp_ext[:, :HALO], WHOLE, [(i + 1, i) for i in range(count - 1)])
    grad_proj = jnp.concatenate([gp_ext[:, HALO:rows], gp_ext[:, rows:] + from_next], 1).astype(bf16)
    grad_logits = jnp.concatenate([grad_logits[g, :, :2] for g in range(n_head)], 1).astype(bf16)
    grad_w = jnp.stack([
        jnp.einsum("td,tc->dc", normed, grad_proj[g], preferred_element_type=f32).astype(bf16) for g in range(n_head)
    ])
    grad_beta_w = jnp.einsum("td,th->hd", normed, grad_logits, preferred_element_type=f32)
    grad_normed = jnp.dot(grad_logits, w_beta_all, preferred_element_type=f32)
    for g in range(n_head):
        grad_normed = grad_normed + jnp.einsum("tc,dc->td", grad_proj[g], w_proj[g], preferred_element_type=f32)

    def scattered(array):
        return lax.psum_scatter(array.reshape((-1,) + array.shape[3:]), BY_HEAD, scatter_dimension=0, tiled=True).astype(f32)

    tap_pieces = grad_taps.reshape(n_head, 24, n_seq, 128 // n_seq).transpose(0, 2, 1, 3).reshape(n_head, n_seq, -1)
    beta_pieces = grad_beta_w.reshape(n_head, 2, n_seq, part).transpose(0, 2, 1, 3).reshape(n_head, n_seq, -1)
    extra = jnp.concatenate([tap_pieces, beta_pieces], -1).astype(bf16)
    extra_size = extra.shape[-1]
    extra_rows = -(-extra_size // 768)
    extra_rows = -(-extra_rows // 8) * 8
    extra = jnp.pad(extra, ((0, 0), (0, 0), (0, extra_rows * 768 - extra_size))).reshape(n_head, n_seq, extra_rows, 768)
    sum_w = scattered(jnp.concatenate([grad_w.reshape(n_head, n_seq, part, 768), extra], 2))
    sum_gate = scattered(grad_gate.reshape(n_head, n_seq, part, ff))
    sum_up = scattered(grad_up.reshape(n_head, n_seq, part, ff))
    sum_down = scattered(grad_down.reshape(n_head, ff, n_seq, part).transpose(0, 2, 1, 3))
    sum_out = scattered(grad_out.reshape(n_head, 256, n_seq, part).transpose(0, 2, 1, 3))
    flat = sum_w[part:].reshape(-1)
    tap_size = 24 * (128 // n_seq)
    sum_taps = flat[:tap_size].reshape(3, 4, 2, 128 // n_seq)
    sum_beta = flat[tap_size : tap_size + 2 * part].reshape(2, part).T

    grad_norm_one = jnp.sum(grad_normed * x * r1, 0)
    scaled_one = norm1_gain * grad_normed
    inputs_grad = grad_residual + r1 * scaled_one - x * (r1 * r1 * r1) * jnp.mean(x * scaled_one, -1, keepdims=True)
    gains = lax.psum((grad_norm_one, grad_norm_two, jnp.sum(gain_part[:, 0], 0)), WHOLE)
    return (
        output, inputs_grad, gains[0], sum_w[:part, :256], sum_w[:part, 256:512], sum_w[:part, 512:], sum_beta, sum_taps, gains[2],
        sum_out, gains[1], sum_gate, sum_up, sum_down,
    )


def solution(mesh):
    return jax.shard_map(
        local,
        mesh=mesh,
        in_specs=(
            P(("seq", "head"), None),
            P(),
            P(None, "head"),
            P(None, "head"),
            P(None, "head"),
            P(None, "head"),
            P(None, None, "head", None),
            P(),
            P("head", None),
            P(),
            P(None, "head"),
            P(None, "head"),
            P("head", None),
            P("seq"),
            P("seq", None),
        ),
        out_specs=(
            P(("seq", "head"), None),
            P(("seq", "head"), None),
            P(),
            P("seq", "head"),
            P("seq", "head"),
            P("seq", "head"),
            P("seq", "head"),
            P(None, None, "head", "seq"),
            P(),
            P("head", "seq"),
            P(),
            P("seq", "head"),
            P("seq", "head"),
            P("head", "seq"),
        ),
        check_vma=False,
    )
```

```python
import functools

import jax
import jax.numpy as jnp
from jax import lax
from jax.experimental import pallas as pl
from jax.experimental.pallas import tpu as pltpu
from jax.sharding import PartitionSpec as P

SEQS = 4
CHUNK = 128
HALO = 8
FFP = 768
epsilon = 1e-06
beta_shift = 4.0
f32 = jnp.float32
bf16 = jnp.bfloat16
WHOLE = ("seq", "head")
BY_HEAD = ("head", "seq")


def nn(a, b):
    return lax.dot_general(a, b, (((1,), (0,)), ((), ())), preferred_element_type=f32)


def nt(a, b):
    return lax.dot_general(a, b, (((1,), (1,)), ((), ())), preferred_element_type=f32)


def tn(a, b):
    return lax.dot_general(a, b, (((0,), (0,)), ((), ())), preferred_element_type=f32)


def params(mib=56, grid=1):
    return pltpu.CompilerParams(
        vmem_limit_bytes=mib << 20, dimension_semantics=("arbitrary",) * grid
    )


def lead(*shape):
    zeros = (0,) * len(shape)
    return pl.BlockSpec((None,) + shape, lambda i: (i,) + zeros)


def same(*shape):
    zeros = (0,) * len(shape)
    return pl.BlockSpec(shape, lambda i: zeros)


def cost(us):
    return pl.CostEstimate(flops=int(us * 1.1e9), bytes_accessed=int(us * 1e6), transcendentals=0)


def sds(shape, kind):
    return jax.ShapeDtypeStruct(shape, kind)


def pack_proj_kernel(table_ref, q_ref, k_ref, v_ref, more_ref, out_ref):
    out_ref[:, 0:256] = q_ref[...]
    out_ref[:, 256:512] = k_ref[...]
    out_ref[:, 512:768] = v_ref[...]
    out_ref[:, 768:896] = more_ref[...]


def pack_ffn_kernel(table_ref, gate_ref, up_ref, down_ref, out_w_ref, out_ref, tall):
    ff = gate_ref.shape[1]
    blank = jnp.zeros((gate_ref.shape[0], FFP - ff), bf16)
    out_ref[:, 0:FFP] = jnp.concatenate([gate_ref[...], blank], 1)
    out_ref[:, FFP : 2 * FFP] = jnp.concatenate([up_ref[...], blank], 1)
    tall[0:ff, :] = down_ref[...].astype(f32)
    tall[ff:FFP, :] = jnp.zeros((FFP - ff, 128), f32)
    out_ref[:, 2 * FFP : 3 * FFP] = jnp.transpose(tall[...]).astype(bf16)
    out_ref[:, 3 * FFP : 3 * FFP + 256] = jnp.transpose(out_w_ref[...].astype(f32)).astype(bf16)


def prep_kernel(table_ref, halo_ref, x_ref, gain_ref, normed_ref, turned_ref, wide):
    rows = x_ref.shape[0]
    wide[0:HALO, :] = halo_ref[...]
    wide[HALO : HALO + rows, :] = x_ref[...].astype(f32)
    full = wide[...]
    wide[...] = full * lax.rsqrt(jnp.mean(full * full, -1, keepdims=True) + epsilon) * gain_ref[...]
    for i in range(8):
        at = slice(i * 128, (i + 1) * 128)
        here = pl.ds(pl.multiple_of(table_ref[i] * 128, 128), 128)
        block = wide[:, here]
        normed_ref[:, at] = block.astype(bf16)
        turned_ref[at, :] = jnp.transpose(block[HALO:, :]).astype(bf16)


def mix_kernel(groups, order_ref, head_ref, x_ref, gain_ref, weight_ref, res_ref, normed_ref):
    step = pl.program_id(0)
    part = nt(head_ref[...], weight_ref[...])

    @pl.when(step == 0)
    def _():
        res_ref[...] = x_ref[...].astype(f32) + part

    @pl.when(step > 0)
    def _():
        res_ref[...] += part

    @pl.when(step == groups - 1)
    def _():
        full = res_ref[...]
        normed = full * lax.rsqrt(jnp.mean(full * full, -1, keepdims=True) + epsilon) * gain_ref[...]
        normed_ref[...] = normed.astype(bf16)


def turn_kernel(
    table_ref, order_ref, ffn_ref, two_ref, res_ref, dy_ref, gain_two_ref, head_ref, weight_ref, att_ref, far_ref, gain_ref, idc_ref,
    _, __, out_ref, gres_ref, gtwo_ref, own_ref, other_ref, datt_ref, local_grad_ref, gain_grad_ref, mixer, turned,
):
    step = pl.program_id(0)
    rows = att_ref.shape[1]

    @pl.when(step == 0)
    def _():
        res = res_ref[...]
        two = two_ref[...]
        r2 = lax.rsqrt(jnp.mean(res * res, -1, keepdims=True) + epsilon)
        scaled = gain_two_ref[...] * two
        grad = dy_ref[...].astype(f32) + r2 * scaled - res * ((r2 * r2 * r2) * jnp.mean(res * scaled, -1, keepdims=True))
        gres_ref[...] = grad
        mixer[...] = grad.astype(bf16)
        for i in range(8):
            here = pl.ds(pl.multiple_of(table_ref[i] * 128, 128), 128)
            turned[i * 128 : (i + 1) * 128, :] = jnp.transpose(gres_ref[:, here]).astype(bf16)
        gtwo_ref[...] = jnp.broadcast_to(jnp.sum(two * res * r2, 0, keepdims=True), gtwo_ref.shape)
        out_ref[...] = (res + ffn_ref[...]).astype(bf16)

    gho = nn(mixer[...], weight_ref[...])
    mask = (idc_ref[HALO : HALO + rows, :] < SEQS).astype(f32)
    gain = gain_ref[0:1, :]
    total = jnp.zeros((1, 128), f32)
    for hh in range(2):
        out = att_ref[hh]
        go = gho[:, hh * 128 : (hh + 1) * 128] * mask
        rh = lax.rsqrt(jnp.mean(out * out, -1, keepdims=True) + epsilon)
        total = total + jnp.sum(go * out * rh, 0, keepdims=True)
        inner = jnp.mean(out * gain * go, -1, keepdims=True)
        grad = (rh * gain * go - out * (rh * rh * rh) * inner).astype(bf16)
        datt_ref[hh] = grad
        local_grad_ref[hh] = tn(far_ref[hh], grad).astype(bf16)
    gain_grad_ref[...] = jnp.broadcast_to(total, (8, 128))
    half = own_ref.shape[0]
    own_ref[...] = nn(turned[0:half, :], head_ref[...]).astype(bf16)
    other_ref[...] = nn(turned[half : 2 * half, :], head_ref[...]).astype(bf16)


def chunk_masks(idc_ref, idr_ref, c):
    base = HALO + c * CHUNK
    own = idc_ref[base : base + CHUNK, :]
    row = idr_ref[0:1, base : base + CHUNK]
    prev = idc_ref[base - 1 : base, :]
    last = idc_ref[base + CHUNK - 1 : base + CHUNK, :]
    equal = own == row
    carry = (own == prev).astype(f32)
    to_last = (own == last).astype(f32)
    carry_last = (last == prev).astype(f32)
    return equal, carry, to_last, carry_last


def positions():
    row = lax.broadcasted_iota(jnp.int32, (CHUNK, CHUNK), 0)
    col = lax.broadcasted_iota(jnp.int32, (CHUNK, CHUNK), 1)
    return row, col


def front_kernel(chunks, skip, normed_ref, w0, w1, w2, w3, idc_ref, idr_ref, *rest):
    proj_ref, lgt_ref, cw_ref, qkv_ref, sum_ref, uw_ref, inv_ref, pre_ref, tot_ref = rest[skip:]
    rows = CHUNK
    quarter = w0.shape[0]
    wide = nn(normed_ref[:, 0:quarter], w0[...])
    for i, w in enumerate((w1, w2, w3)):
        wide = wide + nn(normed_ref[:, (i + 1) * quarter : (i + 2) * quarter], w[...])
    proj_ref[...] = wide[:, :768]
    lgt_ref[...] = wide[HALO:, 768:896]
    turned = jnp.transpose(w0[0:128, 768:896].astype(f32))
    for j in range(24):
        cw_ref[j : j + 1, :] = turned[2 + 3 * j : 3 + 3 * j] + turned[3 + 3 * j : 4 + 3 * j] + turned[4 + 3 * j : 5 + 3 * j]
    for b in range(6):
        part, hh = b // 2, b % 2
        cols = slice(b * 128, (b + 1) * 128)
        taps = [cw_ref[(part * 4 + j) * 2 + hh : (part * 4 + j) * 2 + hh + 1, :] for j in range(4)]
        for c in range(chunks):
            base = HALO + c * rows
            own = idc_ref[base : base + rows, :]
            acc = proj_ref[base : base + rows, cols] * taps[0]
            for j in range(1, 4):
                prior = idc_ref[base - j : base - j + rows, :]
                acc = acc + jnp.where(prior == own, proj_ref[base - j : base - j + rows, cols], 0.0) * taps[j]
            sum_ref[c * rows : (c + 1) * rows, cols] = acc
            mixed = acc / (1.0 + jnp.exp(-acc))
            if part < 2:
                mixed = mixed * lax.rsqrt(jnp.sum(mixed * mixed, -1, keepdims=True) + epsilon)
            qkv_ref[c * rows : (c + 1) * rows, cols] = mixed.astype(bf16)
    row, col = positions()
    differ = row ^ col
    strict = row > col
    units = [(hh, c) for c in range(chunks) for hh in range(2)]
    lower, inv, scaled = {}, {}, {}
    for hh, c in units:
        equal, carry, _, _ = chunk_masks(idc_ref, idr_ref, c)
        at = slice(c * CHUNK, (c + 1) * CHUNK)
        beta = jax.nn.sigmoid(jnp.broadcast_to(lgt_ref[at, hh : hh + 1], (CHUNK, 128)) - beta_shift)
        beta = jnp.where(idc_ref[HALO + c * CHUNK : HALO + (c + 1) * CHUNK, :] < SEQS, beta, 0.0)
        keys = qkv_ref[at, 256 + hh * 128 : 256 + (hh + 1) * 128]
        values = qkv_ref[at, 512 + hh * 128 : 512 + (hh + 1) * 128]
        low = jnp.where(equal & strict, nt(keys, keys), 0.0) * beta
        lower[hh, c] = low
        inv[hh, c] = jnp.where(row == col, 1.0, 0.0) - jnp.where(differ == 1, low, 0.0)
        scaled[hh, c] = jnp.concatenate(
            [(values.astype(f32) * beta).astype(bf16), (keys.astype(f32) * (beta * carry)).astype(bf16)], axis=1
        )
    for k in range(1, 7):
        level = (differ >> k) == 1
        for u in units:
            off = jnp.where(level, lower[u], 0.0).astype(bf16)
            half = inv[u].astype(bf16)
            inv[u] = inv[u] - nn(half, nn(off, half).astype(bf16))
    for hh, c in units:
        at = slice(c * CHUNK, (c + 1) * CHUNK)
        half = inv[hh, c].astype(bf16)
        inv_ref[hh, at, :] = half
        uw_ref[hh, at, :] = nn(half, scaled[hh, c]).astype(bf16)
    eye = jnp.where(row == col, 1.0, 0.0)
    state = [[eye, jnp.zeros((CHUNK, CHUNK), f32)] for _ in range(2)]
    for c in range(chunks):
        at = slice(c * CHUNK, (c + 1) * CHUNK)
        _, _, to_last, carry_last = chunk_masks(idc_ref, idr_ref, c)
        for hh in range(2):
            packed = jnp.concatenate([state[hh][0].astype(bf16), state[hh][1].astype(bf16)], axis=1)
            pre_ref[hh, c] = packed
            moved = nn(uw_ref[hh, at, 128:256], packed)
            change = jnp.concatenate(
                [(-moved[:, :128]).astype(bf16), (uw_ref[hh, at, 0:128].astype(f32) - moved[:, 128:]).astype(bf16)], axis=1
            )
            keys = qkv_ref[at, 256 + hh * 128 : 256 + (hh + 1) * 128]
            kept = (keys.astype(f32) * to_last).astype(bf16)
            step = tn(kept, change)
            state[hh] = [state[hh][0] * carry_last + step[:, :128], state[hh][1] * carry_last + step[:, 128:]]
    for hh in range(2):
        tot_ref[hh] = jnp.concatenate([state[hh][0].astype(bf16), state[hh][1].astype(bf16)], axis=1)


def reach_kernel(chunks, qkv_ref, uw_ref, pre_ref, idc_ref, idr_ref, score_ref, reach_ref, base_ref, far_ref):
    row, col = positions()
    causal = row >= col
    for c in range(chunks):
        at = slice(c * CHUNK, (c + 1) * CHUNK)
        equal, carry, _, _ = chunk_masks(idc_ref, idr_ref, c)
        for hh in range(2):
            queries = qkv_ref[at, hh * 128 : (hh + 1) * 128]
            keys = qkv_ref[at, 256 + hh * 128 : 256 + (hh + 1) * 128]
            score = jnp.where(causal & equal, nt(queries, keys), 0.0).astype(bf16)
            score_ref[hh, at, :] = score
            both = nn(score, uw_ref[hh, at, :])
            reach = (queries.astype(f32) * carry - both[:, 128:]).astype(bf16)
            reach_ref[hh, at, :] = reach
            far = nn(reach, pre_ref[hh, c])
            far_ref[hh, at, :] = far[:, :128].astype(bf16)
            base_ref[hh, at, :] = both[:, :128] + far[:, 128:]


def attend_kernel(base_ref, far_ref, state_ref, gain_ref, idc_ref, out_ref, head_ref):
    rows = base_ref.shape[1]
    mask = (idc_ref[HALO : HALO + rows, :] < SEQS).astype(f32)
    for hh in range(2):
        out = base_ref[hh] + nn(far_ref[hh], state_ref[hh])
        out_ref[hh] = out
        rh = lax.rsqrt(jnp.mean(out * out, -1, keepdims=True) + epsilon)
        head_ref[:, hh * 128 : (hh + 1) * 128] = (out * rh * gain_ref[0:1, :] * mask).astype(bf16)


def ffn_kernel(
    table_ref, order_ref, normed_ref, dy_ref, gate_ref, up_ref, down_ref, out_ref, grad_ref, own_ref, other_ref, nturned, dturned
):
    step = pl.program_id(0)
    span = FFP

    @pl.when(step == 0)
    def _():
        for i in range(8):
            at = slice(i * 128, (i + 1) * 128)
            here = pl.ds(pl.multiple_of(table_ref[i] * 128, 128), 128)
            nturned[at, :] = jnp.transpose(normed_ref[:, here].astype(f32)).astype(bf16)
            dturned[at, :] = jnp.transpose(dy_ref[:, here].astype(f32)).astype(bf16)

    gate = nn(normed_ref[...], gate_ref[...])
    up = nn(normed_ref[...], up_ref[...])
    sig = 1.0 / (1.0 + jnp.exp(-gate))
    act = gate * sig
    hidden = (act * up).astype(bf16)
    grad_hidden = nn(dy_ref[...], down_ref[...])
    grad_gate = (grad_hidden * up * (sig * (1.0 + gate * (1.0 - sig)))).astype(bf16)
    grad_up = (grad_hidden * act).astype(bf16)
    out = nt(hidden, down_ref[...])
    back = nt(grad_gate, gate_ref[...]) + nt(grad_up, up_ref[...])

    @pl.when(step == 0)
    def _():
        out_ref[...] = out
        grad_ref[...] = back

    @pl.when(step > 0)
    def _():
        out_ref[...] += out
        grad_ref[...] += back

    half = own_ref.shape[0]
    for target, into in ((own_ref, slice(0, half)), (other_ref, slice(half, 2 * half))):
        target[:, 0:span] = nn(nturned[into, :], grad_gate).astype(bf16)
        target[:, span : 2 * span] = nn(nturned[into, :], grad_up).astype(bf16)
        target[:, 2 * span : 3 * span] = nn(dturned[into, :], hidden).astype(bf16)


def inner_back_kernel(chunks, skip, qkv_ref, uw_ref, pre_ref, score_ref, datt_ref, state_ref, idc_ref, idr_ref, *rest):
    states_ref, pseudo_ref, dq_ref, dk_ref, dp_ref = rest[skip:]
    row, col = positions()
    causal = row >= col
    for c in range(chunks):
        at = slice(c * CHUNK, (c + 1) * CHUNK)
        equal, carry, _, _ = chunk_masks(idc_ref, idr_ref, c)
        for hh in range(2):
            queries = qkv_ref[at, hh * 128 : (hh + 1) * 128]
            keys = qkv_ref[at, 256 + hh * 128 : 256 + (hh + 1) * 128]
            grad = datt_ref[hh, at, :]
            state = (nn(pre_ref[hh, c, :, 0:128], state_ref[hh]) + pre_ref[hh, c, :, 128:256].astype(f32)).astype(bf16)
            states_ref[hh, c] = state
            pseudo = (uw_ref[hh, at, 0:128].astype(f32) - nn(uw_ref[hh, at, 128:256], state)).astype(bf16)
            pseudo_ref[hh, at, :] = pseudo
            grad_score = jnp.where(causal & equal, nt(grad, pseudo), 0.0).astype(bf16)
            dq_ref[hh, at, :] = nt(grad, state) * carry + nn(grad_score, keys)
            dk_ref[hh, at, :] = tn(grad_score, queries)
            dp_ref[hh, at, :] = tn(score_ref[hh, at, :], grad)


def outer_back_kernel(
    chunks, qkv_ref, uw_ref, inv_ref, reach_ref, datt_ref, states_ref, pseudo_ref, dq_ref, dk_ref, dp_ref,
    sum_ref, proj_ref, lgt_ref, gout_ref, cw_ref, idc_ref, idr_ref,
    gp_ref, dcw_ref, first_ref, last_ref, dqkv, pad,
):
    row, col = positions()
    strict = row > col
    lane = lax.broadcasted_iota(jnp.int32, (CHUNK, 128), 1)
    grad_state = [gout_ref[hh].astype(f32) for hh in range(2)]
    for c in range(chunks - 1, -1, -1):
        at = slice(c * CHUNK, (c + 1) * CHUNK)
        equal, carry, to_last, carry_last = chunk_masks(idc_ref, idr_ref, c)
        own = idc_ref[HALO + c * CHUNK : HALO + (c + 1) * CHUNK, :]
        dlgt = jnp.zeros((CHUNK, 128), f32)
        for hh in range(2):
            keys = qkv_ref[at, 256 + hh * 128 : 256 + (hh + 1) * 128]
            keys_f = keys.astype(f32)
            values = qkv_ref[at, 512 + hh * 128 : 512 + (hh + 1) * 128]
            kept = (keys_f * to_last).astype(bf16)
            packed = grad_state[hh].astype(bf16)
            push = nn(kept, packed)
            grad_state[hh] = grad_state[hh] * carry_last + tn(reach_ref[hh, at, :], datt_ref[hh, at, :]) - tn(
                uw_ref[hh, at, 128:256], push.astype(bf16)
            )
            full = (dp_ref[hh, at, :] + push).astype(bf16)
            solved = tn(inv_ref[hh, at, :], full)
            solved_h = solved.astype(bf16)
            pseudo = pseudo_ref[hh, at, :]
            gate = jax.nn.sigmoid(jnp.broadcast_to(lgt_ref[at, hh : hh + 1], (CHUNK, 128)) - beta_shift)
            mask = (own < SEQS).astype(f32)
            beta = gate * mask
            back = nt(solved_h, states_ref[hh, c]) * carry
            outer = jnp.where(equal & strict, nt(solved_h, pseudo), 0.0)
            overlap = nt(keys, keys)
            rate = jnp.sum(solved * values.astype(f32) - back * keys_f - outer * overlap, -1, keepdims=True)
            dlgt = jnp.where(lane == hh, rate * mask * gate * (1.0 - gate), dlgt)
            mixed = (outer * beta).astype(bf16)
            dqkv[at, 256 + hh * 128 : 256 + (hh + 1) * 128] = (
                dk_ref[hh, at, :] + nt(pseudo, packed) * to_last - beta * back - nn(mixed, keys) - tn(mixed, keys)
            )
            dqkv[at, 512 + hh * 128 : 512 + (hh + 1) * 128] = beta * solved
            dqkv[at, hh * 128 : (hh + 1) * 128] = dq_ref[hh, at, :]
        gp_ref[at, 768:896] = dlgt.astype(bf16)
    rows = CHUNK
    length = chunks * CHUNK
    for b in range(6):
        part, hh = b // 2, b % 2
        cols = slice(b * 128, (b + 1) * 128)
        taps = [cw_ref[(part * 4 + j) * 2 + hh : (part * 4 + j) * 2 + hh + 1, :] for j in range(4)]
        pad[0:HALO, :] = jnp.zeros((HALO, 128), f32)
        pad[HALO + length : 2 * HALO + length, :] = jnp.zeros((HALO, 128), f32)
        sums = [jnp.zeros((1, 128), f32) for _ in range(4)]
        for c in range(chunks):
            at = slice(c * rows, (c + 1) * rows)
            base = HALO + c * rows
            u = sum_ref[at, cols]
            sig = 1.0 / (1.0 + jnp.exp(-u))
            grad = dqkv[at, cols]
            if part < 2:
                mixed = u * sig
                r = lax.rsqrt(jnp.sum(mixed * mixed, -1, keepdims=True) + epsilon)
                grad = r * grad - mixed * ((r * r * r) * jnp.sum(mixed * grad, -1, keepdims=True))
            grad = grad * (sig * (1.0 + u * (1.0 - sig)))
            pad[base : base + rows, :] = grad
            own = idc_ref[base : base + rows, :]
            sums[0] = sums[0] + jnp.sum(grad * proj_ref[base : base + rows, cols], 0, keepdims=True)
            for j in range(1, 4):
                prior = idc_ref[base - j : base - j + rows, :]
                sums[j] = sums[j] + jnp.sum(
                    jnp.where(prior == own, proj_ref[base - j : base - j + rows, cols], 0.0) * grad, 0, keepdims=True
                )
        for j in range(4):
            dcw_ref[(part * 4 + j) * 2 + hh : (part * 4 + j) * 2 + hh + 1, :] = sums[j]
        for start, size in [(0, HALO)] + [(HALO + c * rows, rows) for c in range(chunks)]:
            own = idc_ref[start : start + size, :]
            acc = pad[start : start + size, :] * taps[0]
            for j in range(1, 4):
                later = idc_ref[start + j : start + j + size, :]
                acc = acc + jnp.where(later == own, pad[start + j : start + j + size, :], 0.0) * taps[j]
            if start == 0:
                first_ref[:, cols] = acc
            else:
                gp_ref[start - HALO : start - HALO + size, cols] = acc.astype(bf16)
            if start + size == HALO + length:
                last_ref[:, cols] = acc[size - 16 :, :]


def proj_back_kernel(groups, table_ref, turned_ref, gp_ref, last_ref, recv_ref, extra_ref, x_ref, gain_ref, gres_ref, *rest):
    near_w, one_w, far_w, (in_ref, gone_ref, own_ref, other_ref, gp, grad) = rest[:4], rest[4:8], rest[8:12], rest[12:]
    step = pl.program_id(0)
    rows = gp_ref.shape[0]
    half = own_ref.shape[0]
    gp[...] = gp_ref[...]
    fixed = jnp.concatenate([last_ref[0:HALO, :], last_ref[HALO:16, :] + recv_ref[...]], 0)
    gp[rows - 16 : rows, 0:768] = fixed.astype(bf16)
    grads = gp[...]

    def back(pieces):
        return nt(grads, jnp.concatenate([w[...] for w in pieces], 0))

    @pl.when(step == 0)
    def _():
        grad[...] = back(near_w)

    @pl.when(step == 1)
    def _():
        grad[...] += back(one_w)

    @pl.when(step > 1)
    def _():
        grad[...] += back(far_w)

    for target, into in ((own_ref, slice(0, half)), (other_ref, slice(half, 2 * half))):
        total = nn(turned_ref[into, :], grads)
        target[:, 0:768] = total[:, :768].astype(bf16)
        target[:, 768:896] = (total[:, 768:] + extra_ref[into, :]).astype(bf16)

    @pl.when(step == groups - 1)
    def _():
        for i in range(8):
            here = pl.ds(pl.multiple_of(table_ref[i] * 128, 128), 128)
            in_ref[:, here] = grad[:, i * 128 : (i + 1) * 128]
        x = x_ref[...].astype(f32)
        normed_grad = in_ref[...]
        r1 = lax.rsqrt(jnp.mean(x * x, -1, keepdims=True) + epsilon)
        scaled = gain_ref[...] * normed_grad
        gone_ref[...] = jnp.broadcast_to(jnp.sum(normed_grad * x * r1, 0, keepdims=True), gone_ref.shape)
        in_ref[...] = gres_ref[...] + r1 * scaled - x * ((r1 * r1 * r1) * jnp.mean(x * scaled, -1, keepdims=True))


def core_first(n_seq):
    return [2 if i % 2 == 0 else 4 for i in range(n_seq)], [4 if i % 2 == 0 else 2 for i in range(n_seq)]


def seq_permute(array, steps):
    return lax.ppermute(array, "seq", [(i, i ^ k) for i, k in enumerate(steps)])


def ring(array, by=1):
    count = lax.axis_size("head")
    return lax.ppermute(array, "head", [(i, (i + by) % count) for i in range(count)])


def slot_table(s, n_seq):
    if n_seq != 8:
        return jnp.arange(8, dtype=jnp.int32)
    odd = s & 1
    f = jnp.where(odd == 0, 2, 4)
    g = 6 - f
    masks = jnp.stack([0 * f, f, g, 0 * f + 6, 0 * f + 1, 1 ^ g, 1 ^ f, 0 * f + 7])
    return (s ^ masks).astype(jnp.int32)


def gather_plane(pieces, n_seq):
    if n_seq != 8:
        full = lax.all_gather(pieces, "seq", axis=1, tiled=True)
        quarter = full.shape[1] // 4
        return [full[:, i * quarter : (i + 1) * quarter] for i in range(4)]
    near, wide = core_first(n_seq)
    pair = jnp.concatenate([pieces, seq_permute(pieces, near)], 1)
    pair_two = seq_permute(pair, wide)
    swap = [1] * n_seq
    return [pair, pair_two, seq_permute(pair, swap), seq_permute(pair_two, swap)]


def plus(a, b):
    return (a.astype(f32) + b.astype(f32)).astype(bf16)


def tie(value, *others):
    return lax.optimization_barrier((value,) + others)[0]


def after_core(own, got):
    return plus(own[:, own.shape[1] // 2 :], got[:, own.shape[1] // 2 :])


def after_wide(own, got, more):
    quarter = own.shape[1] // 4
    at = slice(quarter, 2 * quarter)
    return (own[:, at].astype(f32) + got[:, at].astype(f32) + more[:, quarter:].astype(f32)).astype(bf16)


def after_near(own, got, more, last):
    quarter = own.shape[1] // 4
    total = own[:, :quarter].astype(f32) + got[:, :quarter].astype(f32) + more[:, :quarter].astype(f32)
    return (total + last.astype(f32)).astype(bf16)


def reduce_whole(own, other):
    return lax.psum_scatter(jnp.concatenate([own, other], 1), "seq", scatter_dimension=1, tiled=True)


def reduce_ring(parts):
    groups = parts.shape[0]
    moving = parts[1]
    for k in range(2, groups + 1):
        moving = ring(moving).astype(f32) + parts[k % groups].astype(f32)
        if k < groups:
            moving = moving.astype(bf16)
    return moving


def apply(a, x):
    return jnp.einsum("hij,hjk->hik", a.astype(bf16), x.astype(bf16), preferred_element_type=f32)


def pull(a, g):
    return jnp.einsum("hij,hik->hjk", a.astype(bf16), g.astype(bf16), preferred_element_type=f32)


def to_groups(slots, z):
    groups = len(slots)
    arrived = jnp.stack([slots[0]] + [ring(slots[k], -k) for k in range(1, groups)])
    return lax.dynamic_slice_in_dim(jnp.concatenate([arrived, arrived], 0), (groups - z) % groups, groups, 0)


def from_groups(blocks, z):
    groups = len(blocks)
    stacked = jnp.stack(blocks)
    turned = lax.dynamic_slice_in_dim(jnp.concatenate([stacked, stacked], 0), z, groups, 0)
    return jnp.stack([turned[0]] + [ring(turned[k], k) for k in range(1, groups)])


def exchange_forward(tot, n_seq, s, z):
    groups = len(tot)
    got = to_groups(tot, z)

    def after(second, first):
        moved = apply(second[..., :128], first)
        return jnp.concatenate([moved[..., :128], moved[..., 128:] + second[..., 128:].astype(f32)], -1)

    whole = got[0].astype(f32)
    for j in range(1, groups):
        whole = after(got[j], whole)
    eye = jnp.broadcast_to(jnp.eye(128, dtype=f32), (2, 128, 128))
    prefix = jnp.concatenate([eye, jnp.zeros((2, 128, 128), f32)], -1)
    suffix = eye
    kept = []
    k = 1
    while k < n_seq:
        mine = whole.astype(bf16)
        other = lax.ppermute(mine, "seq", [(i, i ^ k) for i in range(n_seq)])
        upper = (s & k) != 0
        first = jnp.where(upper, other, mine)
        second = jnp.where(upper, mine, other)
        kept.append((first[..., :128], suffix.astype(bf16)))
        prefix = jnp.where(upper, after(prefix, other), prefix)
        suffix = jnp.where(upper, suffix, apply(other[..., :128], suffix))
        whole = after(second, first)
        k *= 2
    state = prefix[..., 128:]
    states = [state.astype(bf16)]
    for j in range(groups - 1):
        state = apply(got[j][..., :128], state) + got[j][..., 128:].astype(f32)
        states.append(state.astype(bf16))
    return from_groups(states, z), got, kept


def exchange_backward(local, got, kept, n_seq, s, z):
    groups = len(local)
    grads = to_groups(local, z)
    whole = grads[groups - 1].astype(f32)
    for j in range(groups - 2, -1, -1):
        whole = pull(got[j][..., :128], whole) + grads[j].astype(f32)
    later = jnp.zeros_like(whole)
    k = 1
    for first_a, suffix in kept:
        mine = whole.astype(bf16)
        other = lax.ppermute(mine, "seq", [(i, i ^ k) for i in range(n_seq)])
        upper = (s & k) != 0
        later = jnp.where(upper, later, pull(suffix, other) + later)
        first = jnp.where(upper, other, mine)
        second = jnp.where(upper, mine, other)
        whole = pull(first_a, second) + first.astype(f32)
        k *= 2
    outs = [later.astype(bf16)]
    for j in range(groups - 1, 0, -1):
        later = pull(got[j][..., :128], later) + grads[j].astype(f32)
        outs.append(later.astype(bf16))
    return from_groups(outs[::-1], z)


def sum_everywhere(array, n_seq, n_head):
    count = n_seq * n_head
    k = 1
    while k < count:
        array = array + lax.ppermute(array, WHOLE, [(i, i ^ k) for i in range(count)])
        k *= 2
    return array


def local(
    inputs, norm1_gain, w_query, w_key, w_value, w_beta, conv_weight, head_gain, w_out, norm2_gain, w_gate, w_up, w_down,
    seq_ids, cotangent,
):
    n_seq, n_head = lax.axis_size("seq"), lax.axis_size("head")
    s, z = lax.axis_index("seq"), lax.axis_index("head")
    rows, width = inputs.shape
    ff = w_gate.shape[1]
    chunks = rows // CHUNK
    ext = rows + HALO
    count = n_seq * n_head
    part = width // n_seq
    quarter = width // 4
    table = slot_table(s, n_seq)
    smem = pl.BlockSpec(memory_space=pltpu.SMEM)

    before = lax.ppermute(inputs[-HALO:], WHOLE, [(i, i + 1) for i in range(count - 1)])
    ids_before = lax.ppermute(seq_ids[-HALO:], "seq", [(i, i + 1) for i in range(n_seq - 1)])
    taps = conv_weight.reshape(24, 128).T
    high = lax.reduce_precision(taps, 8, 7)
    middle = lax.reduce_precision(taps - high, 8, 7)
    coded = jnp.stack([high, middle, taps - high - middle], -1).reshape(128, 72).astype(bf16)
    coded = jnp.tile(coded, (width // 128, 1))
    more = jnp.concatenate([w_beta, coded, jnp.zeros((width, 54), bf16)], 1)

    def by_row(columns):
        return pl.BlockSpec((128, columns), lambda i, table: (table[i], 0))

    def by_column(size):
        return pl.BlockSpec((size, 128), lambda i, table: (0, table[i]))

    columns = 3 * FFP + 256

    def packed_proj(blocks, name):
        return pl.pallas_call(
            pack_proj_kernel,
            grid_spec=pltpu.PrefetchScalarGridSpec(
                num_scalar_prefetch=1,
                grid=(blocks,),
                in_specs=[by_row(256)] * 3 + [by_row(128)],
                out_specs=pl.BlockSpec((128, 896), lambda i, table: (i, 0)),
            ),
            out_shape=sds((blocks * 128, 896), bf16),
            compiler_params=params(),
            cost_estimate=cost(0.8 * blocks),
            name=name,
        )(table, w_query, w_key, w_value, more)

    proj_local = packed_proj(8, "pack_proj")
    if n_seq == 8:
        own_proj = packed_proj(1, "pack_proj_own")
        own_ffn = pl.pallas_call(
            pack_ffn_kernel,
            grid_spec=pltpu.PrefetchScalarGridSpec(
                num_scalar_prefetch=1,
                grid=(1,),
                in_specs=[by_row(ff), by_row(ff), by_column(ff), by_column(256)],
                out_specs=pl.BlockSpec((128, columns), lambda i, table: (i, 0)),
                scratch_shapes=[pltpu.VMEM((FFP, 128), f32)],
            ),
            out_shape=sds((128, columns), bf16),
            compiler_params=params(),
            cost_estimate=cost(2),
            name="pack_ffn",
        )(table, w_gate, w_up, w_down, w_out)
    else:
        own_proj = lax.dynamic_slice_in_dim(proj_local, s * part, part, 0)

        def padded(array):
            return jnp.pad(array, ((0, 0), (0, FFP - ff)))

        whole_ffn = jnp.concatenate([padded(w_gate), padded(w_up), padded(w_down.T), w_out.T], 1)
        own_ffn = lax.dynamic_slice_in_dim(whole_ffn, s * part, part, 0)
    ffn_all = lax.all_gather(own_ffn, BY_HEAD, axis=0, tiled=True).reshape(n_head, width, columns)
    ring_pieces = [own_proj]
    for _ in range(n_head - 1):
        ring_pieces.append(ring(ring_pieces[-1]))
    proj_one = gather_plane(ring_pieces[1][None], n_seq)
    proj_far = gather_plane(jnp.stack(ring_pieces[2:]), n_seq)

    ids_before = jnp.where(s == 0, -1, ids_before)
    ids = lax.dynamic_slice_in_dim(jnp.concatenate([ids_before, seq_ids]), z * rows, ext)
    ids_pad = jnp.concatenate([ids, jnp.full((HALO,), -2, jnp.int32)])
    idc = jnp.broadcast_to(ids_pad[:, None], (ext + HALO, 128))
    idr = jnp.broadcast_to(ids[None, :], (8, ext))
    normed_ext, turned = pl.pallas_call(
        prep_kernel,
        grid=(1,),
        in_specs=[smem, same(HALO, width), same(rows, width), same(1, width)],
        out_specs=[same(ext, width), same(width, rows)],
        out_shape=[sds((ext, width), bf16), sds((width, rows), bf16)],
        scratch_shapes=[pltpu.VMEM((ext, width), f32)],
        compiler_params=params(),
        cost_estimate=cost(5),
        name="prep",
    )(table, before.astype(f32), inputs, norm1_gain[None])

    idc_spec, idr_spec = same(ext + HALO, 128), same(8, ext)
    hidden_spec = pl.BlockSpec(memory_space=pl.ANY)
    shapes = [
        ((ext, 768), f32), ((rows, 128), f32), ((24, 128), f32), ((rows, 768), bf16), ((rows, 768), f32), ((2, rows, 256), bf16),
        ((2, rows, 128), bf16), ((2, chunks, 128, 256), bf16),
    ]

    def shifted(by, *shape):
        zeros = (0,) * len(shape)
        return pl.BlockSpec((None,) + shape, lambda i: (i + by,) + zeros)

    def local_pieces(columns, at=0):
        return [pl.BlockSpec((quarter, columns), lambda k, i=i: (i, at)) for i in range(4)]

    first = pl.pallas_call(
        functools.partial(front_kernel, chunks, 0),
        grid=(1,),
        in_specs=[same(ext, width)] + local_pieces(896) + [idc_spec, idr_spec],
        out_specs=[lead(*shape) for shape, _ in shapes] + [lead(2, 128, 256)],
        out_shape=[sds((n_head,) + shape, kind) for shape, kind in shapes] + [sds((1, 2, 128, 256), bf16)],
        compiler_params=params(),
        cost_estimate=cost(9),
        name="front_near",
    )(normed_ext, *[proj_local] * 4, idc, idr)
    def front_more(pieces, by, before_it, name):
        size = pieces[0].shape[0]
        return pl.pallas_call(
            functools.partial(front_kernel, chunks, len(shapes)),
            grid=(size,),
            in_specs=[same(ext, width)] + [lead(quarter, 896)] * 4 + [idc_spec, idr_spec] + [hidden_spec] * len(shapes),
            out_specs=[shifted(by, *shape) for shape, _ in shapes] + [lead(2, 128, 256)],
            out_shape=[sds((n_head,) + shape, kind) for shape, kind in shapes] + [sds((size, 2, 128, 256), bf16)],
            input_output_aliases={7 + i: i for i in range(len(shapes))},
            compiler_params=params(),
            cost_estimate=cost(7 * size + 1),
            name=name,
        )(normed_ext, *pieces, idc, idr, *before_it[:-1])

    second = front_more(proj_one, 1, first, "front_one")
    filled = front_more(proj_far, 2, second, "front_far")
    projected, logits, taps_all, qkv, summed, uw, inverse, prefixes, totals = filled
    every_total = [first[-1][0], second[-1][0]] + [totals[k] for k in range(n_head - 2)]
    state_in, got, kept = exchange_forward(every_total, n_seq, s, z)
    score, reach, base, far = pl.pallas_call(
        functools.partial(reach_kernel, chunks),
        grid=(n_head,),
        in_specs=[lead(rows, 768), lead(2, rows, 256), lead(2, chunks, 128, 256), idc_spec, idr_spec],
        out_specs=[lead(2, rows, 128)] * 4,
        out_shape=[sds((n_head, 2, rows, 128), kind) for kind in (bf16, bf16, f32, bf16)],
        compiler_params=params(),
        cost_estimate=cost(9),
        name="reach",
    )(qkv, uw, prefixes, idc, idr)
    gain_rows = jnp.broadcast_to(head_gain[None, :], (8, 128))
    attended, head_out = pl.pallas_call(
        attend_kernel,
        grid=(n_head,),
        in_specs=[lead(2, rows, 128), lead(2, rows, 128), lead(2, 128, 128), same(8, 128), idc_spec],
        out_specs=[lead(2, rows, 128), pl.BlockSpec((rows, 256), lambda i: (0, i))],
        out_shape=[sds((n_head, 2, rows, 128), f32), sds((rows, n_head * 256), bf16)],
        compiler_params=params(),
        cost_estimate=cost(5),
        name="attend",
    )(base, far, state_in, gain_rows, idc)

    order = ((z - jnp.arange(n_head)) % n_head).astype(jnp.int32)

    def by_slot(columns, at):
        return pl.BlockSpec((None, width, columns), lambda k, order: (order[k], 0, at))

    def fixed(*shape):
        zeros = (0,) * len(shape)
        return pl.BlockSpec(shape, lambda k, *scalars: zeros)

    def led(*shape):
        zeros = (0,) * len(shape)
        return pl.BlockSpec((None,) + shape, lambda k, *scalars: (k,) + zeros)

    head_columns = pl.BlockSpec((rows, 256), lambda k, *scalars: (0, k))
    residual, normed_two = pl.pallas_call(
        functools.partial(mix_kernel, n_head),
        grid_spec=pltpu.PrefetchScalarGridSpec(
            num_scalar_prefetch=1,
            grid=(n_head,),
            in_specs=[head_columns, fixed(rows, width), fixed(1, width), by_slot(256, 3 * FFP // 256)],
            out_specs=[fixed(rows, width), fixed(rows, width)],
        ),
        out_shape=[sds((rows, width), f32), sds((rows, width), bf16)],
        compiler_params=params(),
        cost_estimate=cost(5),
        name="mix",
    )(order, head_out, inputs, norm2_gain[None], ffn_all)
    dy_block = pl.BlockSpec((rows, width), lambda k, table, order: (order[0], 0))

    def ffn_part(at):
        return pl.BlockSpec((None, width, FFP), lambda k, table, order: (order[k], 0, at))

    grads_shape = sds((n_head, width // 2, columns), bf16)
    ffn_out, grad_two, ffn_own, ffn_other = pl.pallas_call(
        ffn_kernel,
        grid_spec=pltpu.PrefetchScalarGridSpec(
            num_scalar_prefetch=2,
            grid=(n_head,),
            in_specs=[fixed(rows, width), dy_block] + [ffn_part(i) for i in range(3)],
            out_specs=[fixed(rows, width), fixed(rows, width)] + [led(width // 2, 3 * FFP)] * 2,
            scratch_shapes=[pltpu.VMEM((width, rows), bf16)] * 2,
        ),
        out_shape=[sds((rows, width), f32), sds((rows, width), f32), grads_shape, grads_shape],
        compiler_params=params(60),
        cost_estimate=cost(38),
        name="ffn",
    )(table, order, normed_two, cotangent, ffn_all, ffn_all, ffn_all)
    output, grad_residual, grad_norm_two, ffn_own, ffn_other, datt, local_grad, gain_part = pl.pallas_call(
        turn_kernel,
        grid_spec=pltpu.PrefetchScalarGridSpec(
            num_scalar_prefetch=2,
            grid=(n_head,),
            in_specs=[
                fixed(rows, width), fixed(rows, width), fixed(rows, width),
                pl.BlockSpec((rows, width), lambda k, table, order: (order[0], 0)), fixed(1, width), head_columns,
                pl.BlockSpec((None, width, 256), lambda k, table, order: (order[k], 0, 3 * FFP // 256)), led(2, rows, 128),
                led(2, rows, 128), fixed(8, 128), fixed(ext + HALO, 128), hidden_spec, hidden_spec,
            ],
            out_specs=[
                fixed(rows, width), fixed(rows, width), fixed(8, width),
                pl.BlockSpec((None, width // 2, 256), lambda k, *scalars: (k, 0, 3 * FFP // 256)),
                pl.BlockSpec((None, width // 2, 256), lambda k, *scalars: (k, 0, 3 * FFP // 256)), led(2, rows, 128),
                led(2, 128, 128), led(8, 128),
            ],
            scratch_shapes=[pltpu.VMEM((rows, width), bf16), pltpu.VMEM((width, rows), bf16)],
        ),
        out_shape=[
            sds((rows, width), bf16), sds((rows, width), f32), sds((8, width), f32), grads_shape, grads_shape,
            sds((n_head, 2, rows, 128), bf16), sds((n_head, 2, 128, 128), bf16), sds((n_head, 8, 128), f32),
        ],
        input_output_aliases={13: 3, 14: 4},
        compiler_params=params(),
        cost_estimate=cost(12),
        name="turn",
    )(
        table, order, ffn_out, grad_two, residual, cotangent, norm2_gain[None], head_out, ffn_all, attended, far, gain_rows, idc,
        ffn_own, ffn_other,
    )
    if n_seq == 8:
        ffn_got = seq_permute(ffn_other, [1] * n_seq)
        ffn_send = after_core(ffn_own, ffn_got)
    grad_out_state = exchange_backward([local_grad[k] for k in range(n_head)], got, kept, n_seq, s, z)
    inner_shapes = [((2, chunks, 128, 128), bf16)] + [((2, rows, 128), kind) for kind in (bf16, f32, f32, f32)]
    inner = []
    for k in range(n_head):

        def at_slot(*shape, k=k):
            zeros = (0,) * len(shape)
            return pl.BlockSpec((None,) + shape, lambda i: (k,) + zeros)

        inner = pl.pallas_call(
            functools.partial(inner_back_kernel, chunks, len(inner)),
            grid=(1,),
            in_specs=[
                at_slot(rows, 768), at_slot(2, rows, 256), at_slot(2, chunks, 128, 256), at_slot(2, rows, 128), at_slot(2, rows, 128),
                at_slot(2, 128, 128), idc_spec, idr_spec,
            ]
            + [hidden_spec] * len(inner),
            out_specs=[at_slot(*shape) for shape, _ in inner_shapes],
            out_shape=[sds((n_head,) + shape, kind) for shape, kind in inner_shapes],
            input_output_aliases={8 + i: i for i in range(len(inner))},
            compiler_params=params(),
            cost_estimate=cost(5.5),
            name="inner_back",
        )(qkv, uw, prefixes, score, datt, state_in, idc, idr, *inner)
    states, pseudo, dq, dk, dp = inner
    if n_seq == 8:
        states = tie(states, ffn_send)
    grad_proj, grad_taps, to_previous, last_rows = pl.pallas_call(
        functools.partial(outer_back_kernel, chunks),
        grid=(n_head,),
        in_specs=[
            lead(rows, 768), lead(2, rows, 256), lead(2, rows, 128), lead(2, rows, 128), lead(2, rows, 128),
            lead(2, chunks, 128, 128), lead(2, rows, 128), lead(2, rows, 128), lead(2, rows, 128), lead(2, rows, 128),
            lead(rows, 768), lead(ext, 768), lead(rows, 128), lead(2, 128, 128), lead(24, 128), idc_spec, idr_spec,
        ],
        out_specs=[lead(rows, 896), lead(24, 128), lead(HALO, 768), lead(16, 768)],
        out_shape=[
            sds((n_head, rows, 896), bf16), sds((n_head, 24, 128), f32), sds((n_head, HALO, 768), f32),
            sds((n_head, 16, 768), f32),
        ],
        scratch_shapes=[pltpu.VMEM((rows, 768), f32), pltpu.VMEM((rows + 2 * HALO, 128), f32)],
        compiler_params=params(),
        cost_estimate=cost(26),
        name="outer_back",
    )(
        qkv, uw, inverse, reach, datt, states, pseudo, dq, dk, dp, summed, projected, logits, grad_out_state, taps_all, idc, idr,
    )

    to_previous = jnp.take(to_previous, order, axis=0)
    from_next = lax.ppermute(to_previous, WHOLE, [(i + 1, i) for i in range(count - 1)])
    from_next = jnp.take(from_next, order, axis=0)
    lanes = 128 // n_seq
    extra = grad_taps.reshape(n_head, 24, n_seq, lanes).transpose(0, 2, 3, 1)
    if n_seq == 8:
        extra = jnp.take(extra, table, axis=1)
    extra = jnp.pad(extra, ((0, 0), (0, 0), (0, part - lanes), (2, 102))).reshape(n_head, width, 128)
    if n_seq == 8:
        near, wide = core_first(n_seq)
        ffn_more = seq_permute(ffn_send, wide)
        ffn_send = after_wide(ffn_own, ffn_got, ffn_more)
        grad_proj = tie(grad_proj, ffn_send)

    def far_block(by):
        return pl.BlockSpec((None, quarter, 896), lambda k: (jnp.maximum(k - by, 0), 0, 0))

    inputs_grad, grad_norm_one, proj_own, proj_other = pl.pallas_call(
        functools.partial(proj_back_kernel, n_head),
        grid=(n_head,),
        in_specs=[
            smem, same(width, rows), lead(rows, 896), lead(16, 768), lead(HALO, 768), lead(width, 128), same(rows, width),
            same(1, width), same(rows, width),
        ]
        + local_pieces(896)
        + [pl.BlockSpec((None, quarter, 896), lambda k: (0, 0, 0))] * 4
        + [far_block(2)] * 4,
        out_specs=[same(rows, width), same(8, width), lead(width // 2, 896), lead(width // 2, 896)],
        out_shape=[sds((rows, width), f32), sds((8, width), f32)] + [sds((n_head, width // 2, 896), bf16)] * 2,
        scratch_shapes=[pltpu.VMEM((rows, 896), bf16), pltpu.VMEM((rows, width), f32)],
        compiler_params=params(),
        cost_estimate=cost(15),
        name="proj_back",
    )(
        table, turned, grad_proj, last_rows, from_next, extra, inputs, norm1_gain[None], grad_residual, *[proj_local] * 4, *proj_one,
        *proj_far,
    )
    if n_seq == 8:
        ffn_last = seq_permute(ffn_send, near)
        proj_got = tie(seq_permute(proj_other, [1] * n_seq), ffn_last)
        proj_more = seq_permute(after_core(proj_own, proj_got), wide)
        ffn_sum = after_near(ffn_own, ffn_got, ffn_more, ffn_last)
        proj_last = seq_permute(after_wide(proj_own, proj_got, proj_more), near)
        proj_sum = after_near(proj_own, proj_got, proj_more, proj_last)
    else:
        proj_sum, ffn_sum = reduce_whole(proj_own, proj_other), reduce_whole(ffn_own, ffn_other)
    sum_proj, sum_ffn = reduce_ring(proj_sum), reduce_ring(ffn_sum)

    gains = jnp.concatenate([grad_norm_one[0], grad_norm_two[0], jnp.sum(gain_part[:, 0], 0)]).reshape(-1, 128)
    gains = sum_everywhere(gains, n_seq, n_head).reshape(-1)
    return (
        output, inputs_grad, gains[:width], sum_proj[:, :256], sum_proj[:, 256:512], sum_proj[:, 512:768], sum_proj[:, 768:770],
        sum_proj[:lanes, 770:794].T.reshape(3, 4, 2, lanes), gains[2 * width :], sum_ffn[:, 3 * FFP :].T, gains[width : 2 * width],
        sum_ffn[:, :ff], sum_ffn[:, FFP : FFP + ff], sum_ffn[:, 2 * FFP : 2 * FFP + ff].T,
    )


def solution(mesh):
    return jax.shard_map(
        local,
        mesh=mesh,
        in_specs=(
            P(("seq", "head"), None),
            P(),
            P(None, "head"),
            P(None, "head"),
            P(None, "head"),
            P(None, "head"),
            P(None, None, "head", None),
            P(),
            P("head", None),
            P(),
            P(None, "head"),
            P(None, "head"),
            P("head", None),
            P("seq"),
            P("seq", None),
        ),
        out_specs=(
            P(("seq", "head"), None),
            P(("seq", "head"), None),
            P(),
            P("seq", "head"),
            P("seq", "head"),
            P("seq", "head"),
            P("seq", "head"),
            P(None, None, "head", "seq"),
            P(),
            P("head", "seq"),
            P(),
            P("seq", "head"),
            P("seq", "head"),
            P("head", "seq"),
        ),
        check_vma=False,
    )
```

```python
import functools

import jax
import jax.numpy as jnp
from jax import lax
from jax.experimental import pallas as pl
from jax.experimental.pallas import tpu as pltpu
from jax.sharding import PartitionSpec as P

SEQS = 4
CHUNK = 128
HALO = 8
FFP = 768
epsilon = 1e-06
beta_shift = 4.0
f32 = jnp.float32
bf16 = jnp.bfloat16
WHOLE = ("seq", "head")
BY_HEAD = ("head", "seq")


def nn(a, b):
    return lax.dot_general(a, b, (((1,), (0,)), ((), ())), preferred_element_type=f32)


def nt(a, b):
    return lax.dot_general(a, b, (((1,), (1,)), ((), ())), preferred_element_type=f32)


def tn(a, b):
    return lax.dot_general(a, b, (((0,), (0,)), ((), ())), preferred_element_type=f32)


def params(mib=56, grid=1):
    return pltpu.CompilerParams(
        vmem_limit_bytes=mib << 20, dimension_semantics=("arbitrary",) * grid
    )


def lead(*shape):
    zeros = (0,) * len(shape)
    return pl.BlockSpec((None,) + shape, lambda i: (i,) + zeros)


def same(*shape):
    zeros = (0,) * len(shape)
    return pl.BlockSpec(shape, lambda i: zeros)


def cost(us):
    return pl.CostEstimate(flops=int(us * 1.1e9), bytes_accessed=int(us * 1e6), transcendentals=0)


def sds(shape, kind):
    return jax.ShapeDtypeStruct(shape, kind)


def pack_proj_kernel(table_ref, q_ref, k_ref, v_ref, more_ref, out_ref):
    out_ref[:, 0:256] = q_ref[...]
    out_ref[:, 256:512] = k_ref[...]
    out_ref[:, 512:768] = v_ref[...]
    out_ref[:, 768:896] = more_ref[...]


def pack_ffn_kernel(table_ref, gate_ref, up_ref, down_ref, out_w_ref, out_ref, tall):
    ff = gate_ref.shape[0]
    tall[ff:FFP, :] = jnp.zeros((FFP - ff, 128), f32)
    for i, ref in enumerate((gate_ref, up_ref, down_ref)):
        tall[0:ff, :] = ref[...].astype(f32)
        out_ref[:, i * FFP : (i + 1) * FFP] = jnp.transpose(tall[...]).astype(bf16)
    out_ref[:, 3 * FFP : 3 * FFP + 256] = jnp.transpose(out_w_ref[...].astype(f32)).astype(bf16)


def prep_kernel(table_ref, halo_ref, x_ref, gain_ref, normed_ref, turned_ref, wide):
    rows = x_ref.shape[0]
    wide[0:HALO, :] = halo_ref[...]
    wide[HALO : HALO + rows, :] = x_ref[...].astype(f32)
    full = wide[...]
    wide[...] = full * lax.rsqrt(jnp.mean(full * full, -1, keepdims=True) + epsilon) * gain_ref[...]
    for i in range(8):
        at = slice(i * 128, (i + 1) * 128)
        here = pl.ds(pl.multiple_of(table_ref[i] * 128, 128), 128)
        block = wide[:, here]
        normed_ref[:, at] = block.astype(bf16)
        turned_ref[at, :] = jnp.transpose(block[HALO:, :]).astype(bf16)


def mix_kernel(groups, order_ref, head_ref, x_ref, gain_ref, weight_ref, res_ref, normed_ref):
    step = pl.program_id(0)
    part = nt(head_ref[...], weight_ref[...])

    @pl.when(step == 0)
    def _():
        res_ref[...] = x_ref[...].astype(f32) + part

    @pl.when(step > 0)
    def _():
        res_ref[...] += part

    @pl.when(step == groups - 1)
    def _():
        full = res_ref[...]
        normed = full * lax.rsqrt(jnp.mean(full * full, -1, keepdims=True) + epsilon) * gain_ref[...]
        normed_ref[...] = normed.astype(bf16)


def turn_kernel(
    table_ref, order_ref, ffn_ref, two_ref, res_ref, dy_ref, gain_two_ref, head_ref, weight_ref, att_ref, far_ref, gain_ref, idc_ref,
    out_ref, gres_ref, gtwo_ref, own_ref, other_ref, datt_ref, local_grad_ref, gain_grad_ref, mixer, turned,
):
    step = pl.program_id(0)
    rows = att_ref.shape[1]

    @pl.when(step == 0)
    def _():
        res = res_ref[...]
        two = two_ref[...]
        r2 = lax.rsqrt(jnp.mean(res * res, -1, keepdims=True) + epsilon)
        scaled = gain_two_ref[...] * two
        grad = dy_ref[...].astype(f32) + r2 * scaled - res * ((r2 * r2 * r2) * jnp.mean(res * scaled, -1, keepdims=True))
        gres_ref[...] = grad
        mixer[...] = grad.astype(bf16)
        for i in range(8):
            here = pl.ds(pl.multiple_of(table_ref[i] * 128, 128), 128)
            turned[i * 128 : (i + 1) * 128, :] = jnp.transpose(gres_ref[:, here]).astype(bf16)
        gtwo_ref[...] = jnp.broadcast_to(jnp.sum(two * res * r2, 0, keepdims=True), gtwo_ref.shape)
        out_ref[...] = (res + ffn_ref[...]).astype(bf16)

    gho = nn(mixer[...], weight_ref[...])
    mask = (idc_ref[HALO : HALO + rows, :] < SEQS).astype(f32)
    gain = gain_ref[0:1, :]
    total = jnp.zeros((1, 128), f32)
    for hh in range(2):
        out = att_ref[hh]
        go = gho[:, hh * 128 : (hh + 1) * 128] * mask
        rh = lax.rsqrt(jnp.mean(out * out, -1, keepdims=True) + epsilon)
        total = total + jnp.sum(go * out * rh, 0, keepdims=True)
        inner = jnp.mean(out * gain * go, -1, keepdims=True)
        grad = (rh * gain * go - out * (rh * rh * rh) * inner).astype(bf16)
        datt_ref[hh] = grad
        local_grad_ref[hh] = tn(far_ref[hh], grad).astype(bf16)
    gain_grad_ref[...] = jnp.broadcast_to(total, (8, 128))
    half = own_ref.shape[0]
    own_ref[...] = nn(turned[0:half, :], head_ref[...]).astype(bf16)
    other_ref[...] = nn(turned[half : 2 * half, :], head_ref[...]).astype(bf16)


def chunk_masks(idc_ref, idr_ref, c):
    base = HALO + c * CHUNK
    own = idc_ref[base : base + CHUNK, :]
    row = idr_ref[0:1, base : base + CHUNK]
    prev = idc_ref[base - 1 : base, :]
    last = idc_ref[base + CHUNK - 1 : base + CHUNK, :]
    equal = own == row
    carry = (own == prev).astype(f32)
    to_last = (own == last).astype(f32)
    carry_last = (last == prev).astype(f32)
    return equal, carry, to_last, carry_last


def positions():
    row = lax.broadcasted_iota(jnp.int32, (CHUNK, CHUNK), 0)
    col = lax.broadcasted_iota(jnp.int32, (CHUNK, CHUNK), 1)
    return row, col


def front_kernel(chunks, skip, normed_ref, w0, w1, w2, w3, idc_ref, idr_ref, *rest):
    proj_ref, lgt_ref, cw_ref, qkv_ref, sum_ref, uw_ref, inv_ref, pre_ref, tot_ref = rest[skip:]
    rows = CHUNK
    quarter = w0.shape[0]
    wide = nn(normed_ref[:, 0:quarter], w0[...])
    for i, w in enumerate((w1, w2, w3)):
        wide = wide + nn(normed_ref[:, (i + 1) * quarter : (i + 2) * quarter], w[...])
    proj_ref[...] = wide[:, :768]
    lgt_ref[...] = wide[HALO:, 768:896]
    turned = jnp.transpose(w0[0:128, 768:896].astype(f32))
    for j in range(24):
        cw_ref[j : j + 1, :] = turned[2 + 3 * j : 3 + 3 * j] + turned[3 + 3 * j : 4 + 3 * j] + turned[4 + 3 * j : 5 + 3 * j]
    for b in range(6):
        part, hh = b // 2, b % 2
        cols = slice(b * 128, (b + 1) * 128)
        taps = [cw_ref[(part * 4 + j) * 2 + hh : (part * 4 + j) * 2 + hh + 1, :] for j in range(4)]
        for c in range(chunks):
            base = HALO + c * rows
            own = idc_ref[base : base + rows, :]
            acc = proj_ref[base : base + rows, cols] * taps[0]
            for j in range(1, 4):
                prior = idc_ref[base - j : base - j + rows, :]
                acc = acc + jnp.where(prior == own, proj_ref[base - j : base - j + rows, cols], 0.0) * taps[j]
            sum_ref[c * rows : (c + 1) * rows, cols] = acc
            mixed = acc / (1.0 + jnp.exp(-acc))
            if part < 2:
                mixed = mixed * lax.rsqrt(jnp.sum(mixed * mixed, -1, keepdims=True) + epsilon)
            qkv_ref[c * rows : (c + 1) * rows, cols] = mixed.astype(bf16)
    row, col = positions()
    differ = row ^ col
    strict = row > col
    units = [(hh, c) for c in range(chunks) for hh in range(2)]
    lower, inv, scaled = {}, {}, {}
    for hh, c in units:
        equal, carry, _, _ = chunk_masks(idc_ref, idr_ref, c)
        at = slice(c * CHUNK, (c + 1) * CHUNK)
        beta = jax.nn.sigmoid(jnp.broadcast_to(lgt_ref[at, hh : hh + 1], (CHUNK, 128)) - beta_shift)
        beta = jnp.where(idc_ref[HALO + c * CHUNK : HALO + (c + 1) * CHUNK, :] < SEQS, beta, 0.0)
        keys = qkv_ref[at, 256 + hh * 128 : 256 + (hh + 1) * 128]
        values = qkv_ref[at, 512 + hh * 128 : 512 + (hh + 1) * 128]
        low = jnp.where(equal & strict, nt(keys, keys), 0.0) * beta
        lower[hh, c] = low
        inv[hh, c] = jnp.where(row == col, 1.0, 0.0) - jnp.where(differ == 1, low, 0.0)
        scaled[hh, c] = jnp.concatenate(
            [(values.astype(f32) * beta).astype(bf16), (keys.astype(f32) * (beta * carry)).astype(bf16)], axis=1
        )
    for k in range(1, 7):
        level = (differ >> k) == 1
        for u in units:
            off = jnp.where(level, lower[u], 0.0).astype(bf16)
            half = inv[u].astype(bf16)
            inv[u] = inv[u] - nn(half, nn(off, half).astype(bf16))
    for hh, c in units:
        at = slice(c * CHUNK, (c + 1) * CHUNK)
        half = inv[hh, c].astype(bf16)
        inv_ref[hh, at, :] = half
        uw_ref[hh, at, :] = nn(half, scaled[hh, c]).astype(bf16)
    eye = jnp.where(row == col, 1.0, 0.0)
    state = [[eye, jnp.zeros((CHUNK, CHUNK), f32)] for _ in range(2)]
    for c in range(chunks):
        at = slice(c * CHUNK, (c + 1) * CHUNK)
        _, _, to_last, carry_last = chunk_masks(idc_ref, idr_ref, c)
        for hh in range(2):
            packed = jnp.concatenate([state[hh][0].astype(bf16), state[hh][1].astype(bf16)], axis=1)
            pre_ref[hh, c] = packed
            moved = nn(uw_ref[hh, at, 128:256], packed)
            change = jnp.concatenate(
                [(-moved[:, :128]).astype(bf16), (uw_ref[hh, at, 0:128].astype(f32) - moved[:, 128:]).astype(bf16)], axis=1
            )
            keys = qkv_ref[at, 256 + hh * 128 : 256 + (hh + 1) * 128]
            kept = (keys.astype(f32) * to_last).astype(bf16)
            step = tn(kept, change)
            state[hh] = [state[hh][0] * carry_last + step[:, :128], state[hh][1] * carry_last + step[:, 128:]]
    for hh in range(2):
        tot_ref[hh] = jnp.concatenate([state[hh][0].astype(bf16), state[hh][1].astype(bf16)], axis=1)


def reach_kernel(chunks, qkv_ref, uw_ref, pre_ref, idc_ref, idr_ref, score_ref, reach_ref, base_ref, far_ref):
    row, col = positions()
    causal = row >= col
    for c in range(chunks):
        at = slice(c * CHUNK, (c + 1) * CHUNK)
        equal, carry, _, _ = chunk_masks(idc_ref, idr_ref, c)
        for hh in range(2):
            queries = qkv_ref[at, hh * 128 : (hh + 1) * 128]
            keys = qkv_ref[at, 256 + hh * 128 : 256 + (hh + 1) * 128]
            score = jnp.where(causal & equal, nt(queries, keys), 0.0).astype(bf16)
            score_ref[hh, at, :] = score
            both = nn(score, uw_ref[hh, at, :])
            reach = (queries.astype(f32) * carry - both[:, 128:]).astype(bf16)
            reach_ref[hh, at, :] = reach
            far = nn(reach, pre_ref[hh, c])
            far_ref[hh, at, :] = far[:, :128].astype(bf16)
            base_ref[hh, at, :] = both[:, :128] + far[:, 128:]


def attend_kernel(base_ref, far_ref, state_ref, gain_ref, idc_ref, out_ref, head_ref):
    rows = base_ref.shape[1]
    mask = (idc_ref[HALO : HALO + rows, :] < SEQS).astype(f32)
    for hh in range(2):
        out = base_ref[hh] + nn(far_ref[hh], state_ref[hh])
        out_ref[hh] = out
        rh = lax.rsqrt(jnp.mean(out * out, -1, keepdims=True) + epsilon)
        head_ref[:, hh * 128 : (hh + 1) * 128] = (out * rh * gain_ref[0:1, :] * mask).astype(bf16)


def ffn_kernel(later, table_ref, order_ref, normed_ref, dy_ref, gate_ref, up_ref, down_ref, *rest):
    given, (out_ref, grad_ref, own_ref, other_ref, nturned, dturned) = rest[:later], rest[later:]
    step = pl.program_id(0)
    span = FFP

    @pl.when(step == 0)
    def _():
        for i in range(8):
            at = slice(i * 128, (i + 1) * 128)
            here = pl.ds(pl.multiple_of(table_ref[i] * 128, 128), 128)
            nturned[at, :] = jnp.transpose(normed_ref[:, here].astype(f32)).astype(bf16)
            dturned[at, :] = jnp.transpose(dy_ref[:, here].astype(f32)).astype(bf16)

    gate = nn(normed_ref[...], gate_ref[...])
    up = nn(normed_ref[...], up_ref[...])
    sig = 1.0 / (1.0 + jnp.exp(-gate))
    act = gate * sig
    hidden = (act * up).astype(bf16)
    grad_hidden = nn(dy_ref[...], down_ref[...])
    grad_gate = (grad_hidden * up * (sig * (1.0 + gate * (1.0 - sig)))).astype(bf16)
    grad_up = (grad_hidden * act).astype(bf16)
    out = nt(hidden, down_ref[...])
    back = nt(grad_gate, gate_ref[...]) + nt(grad_up, up_ref[...])

    @pl.when(step == 0)
    def _():
        out_ref[...] = given[0][...] + out if later else out
        grad_ref[...] = given[1][...] + back if later else back

    @pl.when(step > 0)
    def _():
        out_ref[...] += out
        grad_ref[...] += back

    half = own_ref.shape[0]
    for target, into in ((own_ref, slice(0, half)), (other_ref, slice(half, 2 * half))):
        target[:, 0:span] = nn(nturned[into, :], grad_gate).astype(bf16)
        target[:, span : 2 * span] = nn(nturned[into, :], grad_up).astype(bf16)
        target[:, 2 * span : 3 * span] = nn(dturned[into, :], hidden).astype(bf16)


def inner_back_kernel(chunks, skip, qkv_ref, uw_ref, pre_ref, score_ref, datt_ref, state_ref, idc_ref, idr_ref, *rest):
    states_ref, pseudo_ref, dq_ref, dk_ref, dp_ref = rest[skip:]
    row, col = positions()
    causal = row >= col
    for c in range(chunks):
        at = slice(c * CHUNK, (c + 1) * CHUNK)
        equal, carry, _, _ = chunk_masks(idc_ref, idr_ref, c)
        for hh in range(2):
            queries = qkv_ref[at, hh * 128 : (hh + 1) * 128]
            keys = qkv_ref[at, 256 + hh * 128 : 256 + (hh + 1) * 128]
            grad = datt_ref[hh, at, :]
            state = (nn(pre_ref[hh, c, :, 0:128], state_ref[hh]) + pre_ref[hh, c, :, 128:256].astype(f32)).astype(bf16)
            states_ref[hh, c] = state
            pseudo = (uw_ref[hh, at, 0:128].astype(f32) - nn(uw_ref[hh, at, 128:256], state)).astype(bf16)
            pseudo_ref[hh, at, :] = pseudo
            grad_score = jnp.where(causal & equal, nt(grad, pseudo), 0.0).astype(bf16)
            dq_ref[hh, at, :] = nt(grad, state) * carry + nn(grad_score, keys)
            dk_ref[hh, at, :] = tn(grad_score, queries)
            dp_ref[hh, at, :] = tn(score_ref[hh, at, :], grad)


def tail_kernel(
    chunks, n_seq, last, table_ref, qkv_ref, uw_ref, inv_ref, reach_ref, datt_ref, states_ref, pseudo_ref, dq_ref, dk_ref, dp_ref,
    sum_ref, proj_ref, lgt_ref, gout_ref, cw_ref, idc_ref, idr_ref,
    turned_ref, edge_ref, *rest,
):
    first_w, second_w, rest = rest[:4], rest[4:8], rest[8:]
    if last:
        gn_in, gh_in, x_ref, halo_ref, gain_ref, gres_ref = rest[:6]
        in_ref, hin_ref, gone_ref, own_ref, other_ref, gp_ref, first_ref, dqkv, pad, spread, extra, gn_ref, gh_ref = rest[6:]
    else:
        outs_w, (gn_ref, gh_ref, own_ref, other_ref, gp_ref, first_ref, dqkv, pad, spread, extra) = rest[:4], rest[4:]
    step = pl.program_id(0)
    row, col = positions()
    strict = row > col
    lane = lax.broadcasted_iota(jnp.int32, (CHUNK, 128), 1)
    grad_state = [gout_ref[hh].astype(f32) for hh in range(2)]
    for c in range(chunks - 1, -1, -1):
        at = slice(c * CHUNK, (c + 1) * CHUNK)
        equal, carry, to_last, carry_last = chunk_masks(idc_ref, idr_ref, c)
        own = idc_ref[HALO + c * CHUNK : HALO + (c + 1) * CHUNK, :]
        dlgt = jnp.zeros((CHUNK, 128), f32)
        for hh in range(2):
            keys = qkv_ref[at, 256 + hh * 128 : 256 + (hh + 1) * 128]
            keys_f = keys.astype(f32)
            values = qkv_ref[at, 512 + hh * 128 : 512 + (hh + 1) * 128]
            kept = (keys_f * to_last).astype(bf16)
            packed = grad_state[hh].astype(bf16)
            push = nn(kept, packed)
            grad_state[hh] = grad_state[hh] * carry_last + tn(reach_ref[hh, at, :], datt_ref[hh, at, :]) - tn(
                uw_ref[hh, at, 128:256], push.astype(bf16)
            )
            full = (dp_ref[hh, at, :] + push).astype(bf16)
            solved = tn(inv_ref[hh, at, :], full)
            solved_h = solved.astype(bf16)
            pseudo = pseudo_ref[hh, at, :]
            gate = jax.nn.sigmoid(jnp.broadcast_to(lgt_ref[at, hh : hh + 1], (CHUNK, 128)) - beta_shift)
            mask = (own < SEQS).astype(f32)
            beta = gate * mask
            back = nt(solved_h, states_ref[hh, c]) * carry
            outer = jnp.where(equal & strict, nt(solved_h, pseudo), 0.0)
            overlap = nt(keys, keys)
            rate = jnp.sum(solved * values.astype(f32) - back * keys_f - outer * overlap, -1, keepdims=True)
            dlgt = jnp.where(lane == hh, rate * mask * gate * (1.0 - gate), dlgt)
            mixed = (outer * beta).astype(bf16)
            dqkv[at, 256 + hh * 128 : 256 + (hh + 1) * 128] = (
                dk_ref[hh, at, :] + nt(pseudo, packed) * to_last - beta * back - nn(mixed, keys) - tn(mixed, keys)
            )
            dqkv[at, 512 + hh * 128 : 512 + (hh + 1) * 128] = beta * solved
            dqkv[at, hh * 128 : (hh + 1) * 128] = dq_ref[hh, at, :]
        gp_ref[at, 768:896] = dlgt.astype(bf16)
    rows = CHUNK
    length = chunks * CHUNK
    for b in range(6):
        part, hh = b // 2, b % 2
        cols = slice(b * 128, (b + 1) * 128)
        taps = [cw_ref[(part * 4 + j) * 2 + hh : (part * 4 + j) * 2 + hh + 1, :] for j in range(4)]
        pad[0:HALO, :] = jnp.zeros((HALO, 128), f32)
        pad[HALO + length : 2 * HALO + length, :] = jnp.zeros((HALO, 128), f32)
        sums = [jnp.zeros((1, 128), f32) for _ in range(4)]
        for c in range(chunks):
            at = slice(c * rows, (c + 1) * rows)
            base = HALO + c * rows
            u = sum_ref[at, cols]
            sig = 1.0 / (1.0 + jnp.exp(-u))
            grad = dqkv[at, cols]
            if part < 2:
                mixed = u * sig
                r = lax.rsqrt(jnp.sum(mixed * mixed, -1, keepdims=True) + epsilon)
                grad = r * grad - mixed * ((r * r * r) * jnp.sum(mixed * grad, -1, keepdims=True))
            grad = grad * (sig * (1.0 + u * (1.0 - sig)))
            pad[base : base + rows, :] = grad
            own = idc_ref[base : base + rows, :]
            sums[0] = sums[0] + jnp.sum(grad * proj_ref[base : base + rows, cols], 0, keepdims=True)
            for j in range(1, 4):
                prior = idc_ref[base - j : base - j + rows, :]
                sums[j] = sums[j] + jnp.sum(
                    jnp.where(prior == own, proj_ref[base - j : base - j + rows, cols], 0.0) * grad, 0, keepdims=True
                )
        for j in range(4):
            spot = 2 + (part * 4 + j) * 2 + hh
            spread[spot : spot + 1, :] = sums[j]
        for start, size in [(0, HALO)] + [(HALO + c * rows, rows) for c in range(chunks)]:
            own = idc_ref[start : start + size, :]
            acc = pad[start : start + size, :] * taps[0]
            for j in range(1, 4):
                later = idc_ref[start + j : start + j + size, :]
                acc = acc + jnp.where(later == own, pad[start + j : start + j + size, :], 0.0) * taps[j]
            if start == 0:
                first_ref[:, cols] = jnp.concatenate([acc, jnp.zeros((HALO, 128), f32)], 0).astype(bf16)
            else:
                gp_ref[start - HALO : start - HALO + size, cols] = acc.astype(bf16)
    first_ref[:, 768:896] = jnp.zeros((2 * HALO, 128), bf16)

    @pl.when(step == 0)
    def _():
        spread[0:2, :] = jnp.zeros((2, 128), f32)
        spread[26:128, :] = jnp.zeros((102, 128), f32)
        extra[...] = jnp.zeros(extra.shape, f32)

    pad[0:128, :] = jnp.transpose(spread[...])
    part, lanes = 1024 // n_seq, 128 // n_seq
    for i in range(n_seq):
        if n_seq == 8:
            piece = pad[pl.ds(pl.multiple_of(table_ref[i] * lanes, lanes), lanes), :]
        else:
            piece = pad[i * lanes : (i + 1) * lanes, :]
        extra[i * part : i * part + lanes, :] = piece
    grads, edge = gp_ref[...], first_ref[...]

    def back(pieces, fresh):
        weights = jnp.concatenate([w[...] for w in pieces], 0)
        if fresh:
            gn_ref[...] = nt(grads, weights)
            gh_ref[...] = nt(edge, weights)
        else:
            gn_ref[...] += nt(grads, weights)
            gh_ref[...] += nt(edge, weights)

    @pl.when(step == 0)
    def _():
        if last:
            gn_ref[...] = gn_in[...]
            gh_ref[...] = gh_in[...]
        back(first_w, not last)

    @pl.when(step == 1)
    def _():
        back(second_w, False)

    half = own_ref.shape[0]
    for target, into in ((own_ref, slice(0, half)), (other_ref, slice(half, 2 * half))):
        total = nn(turned_ref[into, :], grads) + tn(edge_ref[:, into], edge)
        target[:, 0:768] = total[:, :768].astype(bf16)
        target[:, 768:896] = (total[:, 768:] + extra[into, :]).astype(bf16)

    if not last:
        for i, target in enumerate((own_ref, other_ref)):
            target[:, 896:1152] = outs_w[i][...]
            target[:, 1152:1408] = outs_w[2 + i][...]

    if last:

        @pl.when(step == 1)
        def _():
            for i in range(8):
                here = pl.ds(pl.multiple_of(table_ref[i] * 128, 128), 128)
                in_ref[:, here] = gn_ref[:, i * 128 : (i + 1) * 128]
                hin_ref[:, here] = gh_ref[0:HALO, i * 128 : (i + 1) * 128]

            def through(x, normed_grad):
                r1 = lax.rsqrt(jnp.mean(x * x, -1, keepdims=True) + epsilon)
                scaled = gain_ref[...] * normed_grad
                moved = r1 * scaled - x * ((r1 * r1 * r1) * jnp.mean(x * scaled, -1, keepdims=True))
                return moved, jnp.sum(normed_grad * x * r1, 0, keepdims=True)

            moved, sums_one = through(x_ref[...].astype(f32), in_ref[...])
            in_ref[...] = gres_ref[...] + moved
            moved, sums_two = through(halo_ref[...], hin_ref[...])
            hin_ref[...] = moved
            gone_ref[...] = jnp.broadcast_to(sums_one + sums_two, gone_ref.shape)


def core_first(n_seq):
    return [2 if i % 2 == 0 else 4 for i in range(n_seq)], [4 if i % 2 == 0 else 2 for i in range(n_seq)]


def seq_permute(array, steps):
    return lax.ppermute(array, "seq", [(i, i ^ k) for i, k in enumerate(steps)])


def ring(array, by=1):
    count = lax.axis_size("head")
    return lax.ppermute(array, "head", [(i, (i + by) % count) for i in range(count)])


def slot_table(s, n_seq):
    if n_seq != 8:
        return jnp.arange(8, dtype=jnp.int32)
    odd = s & 1
    f = jnp.where(odd == 0, 2, 4)
    g = 6 - f
    masks = jnp.stack([0 * f, f, g, 0 * f + 6, 0 * f + 1, 1 ^ g, 1 ^ f, 0 * f + 7])
    return (s ^ masks).astype(jnp.int32)


def gather_plane(pieces, n_seq):
    if n_seq != 8:
        full = lax.all_gather(pieces, "seq", axis=1, tiled=True)
        quarter = full.shape[1] // 4
        return [full[:, i * quarter : (i + 1) * quarter] for i in range(4)]
    near, wide = core_first(n_seq)
    pair = jnp.concatenate([pieces, seq_permute(pieces, near)], 1)
    pair_two = seq_permute(pair, wide)
    swap = [1] * n_seq
    return [pair, pair_two, seq_permute(pair, swap), seq_permute(pair_two, swap)]


def plus(a, b):
    return (a.astype(f32) + b.astype(f32)).astype(bf16)


def tie(value, *others):
    return lax.optimization_barrier((value,) + others)[0]


def after_core(own, got):
    return plus(own[:, own.shape[1] // 2 :], got[:, own.shape[1] // 2 :])


def after_wide(own, got, more):
    quarter = own.shape[1] // 4
    at = slice(quarter, 2 * quarter)
    return (own[:, at].astype(f32) + got[:, at].astype(f32) + more[:, quarter:].astype(f32)).astype(bf16)


def after_near(own, got, more, last):
    quarter = own.shape[1] // 4
    total = own[:, :quarter].astype(f32) + got[:, :quarter].astype(f32) + more[:, :quarter].astype(f32)
    return (total + last.astype(f32)).astype(bf16)


def reduce_whole(own, other):
    return lax.psum_scatter(jnp.concatenate([own, other], 1), "seq", scatter_dimension=1, tiled=True)


def reduce_ring(parts):
    groups = len(parts)
    moving = parts[1]
    for k in range(2, groups + 1):
        moving = ring(moving).astype(f32) + parts[k % groups].astype(f32)
        if k < groups:
            moving = moving.astype(bf16)
    return moving


def apply(a, x):
    return jnp.einsum("hij,hjk->hik", a.astype(bf16), x.astype(bf16), preferred_element_type=f32)


def pull(a, g):
    return jnp.einsum("hij,hik->hjk", a.astype(bf16), g.astype(bf16), preferred_element_type=f32)


def to_groups(slots, z):
    groups = len(slots)
    arrived = jnp.stack([slots[0]] + [ring(slots[k], -k) for k in range(1, groups)])
    return lax.dynamic_slice_in_dim(jnp.concatenate([arrived, arrived], 0), (groups - z) % groups, groups, 0)


def from_groups(blocks, z):
    groups = len(blocks)
    stacked = jnp.stack(blocks)
    turned = lax.dynamic_slice_in_dim(jnp.concatenate([stacked, stacked], 0), z, groups, 0)
    return jnp.stack([turned[0]] + [ring(turned[k], k) for k in range(1, groups)])


def exchange_forward(tot, n_seq, s, z):
    groups = len(tot)
    got = to_groups(tot, z)

    def after(second, first):
        moved = apply(second[..., :128], first)
        return jnp.concatenate([moved[..., :128], moved[..., 128:] + second[..., 128:].astype(f32)], -1)

    whole = got[0].astype(f32)
    for j in range(1, groups):
        whole = after(got[j], whole)
    eye = jnp.broadcast_to(jnp.eye(128, dtype=f32), (2, 128, 128))
    prefix = jnp.concatenate([eye, jnp.zeros((2, 128, 128), f32)], -1)
    suffix = eye
    kept = []
    k = 1
    while k < n_seq:
        mine = whole.astype(bf16)
        other = lax.ppermute(mine, "seq", [(i, i ^ k) for i in range(n_seq)])
        upper = (s & k) != 0
        first = jnp.where(upper, other, mine)
        second = jnp.where(upper, mine, other)
        kept.append((first[..., :128], suffix.astype(bf16)))
        prefix = jnp.where(upper, after(prefix, other), prefix)
        suffix = jnp.where(upper, suffix, apply(other[..., :128], suffix))
        whole = after(second, first)
        k *= 2
    state = prefix[..., 128:]
    states = [state.astype(bf16)]
    for j in range(groups - 1):
        state = apply(got[j][..., :128], state) + got[j][..., 128:].astype(f32)
        states.append(state.astype(bf16))
    return from_groups(states, z), got, kept


def exchange_backward(local, got, kept, n_seq, s, z):
    groups = len(local)
    grads = to_groups(local, z)
    whole = grads[groups - 1].astype(f32)
    for j in range(groups - 2, -1, -1):
        whole = pull(got[j][..., :128], whole) + grads[j].astype(f32)
    later = jnp.zeros_like(whole)
    k = 1
    for first_a, suffix in kept:
        mine = whole.astype(bf16)
        other = lax.ppermute(mine, "seq", [(i, i ^ k) for i in range(n_seq)])
        upper = (s & k) != 0
        later = jnp.where(upper, later, pull(suffix, other) + later)
        first = jnp.where(upper, other, mine)
        second = jnp.where(upper, mine, other)
        whole = pull(first_a, second) + first.astype(f32)
        k *= 2
    outs = [later.astype(bf16)]
    for j in range(groups - 1, 0, -1):
        later = pull(got[j][..., :128], later) + grads[j].astype(f32)
        outs.append(later.astype(bf16))
    return from_groups(outs[::-1], z)


def gain_steps(n_seq, n_head):
    if n_seq == 8:
        near, wide = core_first(n_seq)
        steps = [("seq", [1] * n_seq), ("seq", wide), ("seq", near)]
    else:
        steps = [("seq", [1 << i] * n_seq) for i in range(n_seq.bit_length() - 1)]
    return [("head", [1 << i] * n_head) for i in range(n_head.bit_length() - 1)] + steps


def swap_add(array, step):
    axis, partner = step
    return array + lax.ppermute(array, axis, [(i, i ^ k) for i, k in enumerate(partner)])


def local(
    inputs, norm1_gain, w_query, w_key, w_value, w_beta, conv_weight, head_gain, w_out, norm2_gain, w_gate, w_up, w_down,
    seq_ids, cotangent,
):
    n_seq, n_head = lax.axis_size("seq"), lax.axis_size("head")
    s, z = lax.axis_index("seq"), lax.axis_index("head")
    rows, width = inputs.shape
    ff = w_gate.shape[1]
    chunks = rows // CHUNK
    ext = rows + HALO
    count = n_seq * n_head
    part = width // n_seq
    quarter = width // 4
    table = slot_table(s, n_seq)
    smem = pl.BlockSpec(memory_space=pltpu.SMEM)

    before = lax.ppermute(inputs[-HALO:], WHOLE, [(i, i + 1) for i in range(count - 1)])
    ids_before = lax.ppermute(seq_ids[-HALO:], "seq", [(i, i + 1) for i in range(n_seq - 1)])
    taps = conv_weight.reshape(24, 128).T
    high = lax.reduce_precision(taps, 8, 7)
    middle = lax.reduce_precision(taps - high, 8, 7)
    coded = jnp.stack([high, middle, taps - high - middle], -1).reshape(128, 72).astype(bf16)
    coded = jnp.tile(coded, (width // 128, 1))
    more = jnp.concatenate([w_beta, coded, jnp.zeros((width, 54), bf16)], 1)

    def by_row(columns):
        return pl.BlockSpec((128, columns), lambda i, table: (table[i], 0))

    def by_column(size):
        return pl.BlockSpec((size, 128), lambda i, table: (0, table[i]))

    columns = 3 * FFP + 256

    def packed_proj(blocks, name):
        return pl.pallas_call(
            pack_proj_kernel,
            grid_spec=pltpu.PrefetchScalarGridSpec(
                num_scalar_prefetch=1,
                grid=(blocks,),
                in_specs=[by_row(256)] * 3 + [by_row(128)],
                out_specs=pl.BlockSpec((128, 896), lambda i, table: (i, 0)),
            ),
            out_shape=sds((blocks * 128, 896), bf16),
            compiler_params=params(),
            cost_estimate=cost(0.8 * blocks),
            name=name,
        )(table, w_query, w_key, w_value, more)

    proj_local = packed_proj(8, "pack_proj")
    if n_seq == 8:
        own_proj = packed_proj(1, "pack_proj_own")
        own_ffn = pl.pallas_call(
            pack_ffn_kernel,
            grid_spec=pltpu.PrefetchScalarGridSpec(
                num_scalar_prefetch=1,
                grid=(1,),
                in_specs=[by_column(ff), by_column(ff), by_column(ff), by_column(256)],
                out_specs=pl.BlockSpec((128, columns), lambda i, table: (i, 0)),
                scratch_shapes=[pltpu.VMEM((FFP, 128), f32)],
            ),
            out_shape=sds((128, columns), bf16),
            compiler_params=params(),
            cost_estimate=cost(2),
            name="pack_ffn",
        )(table, w_gate.T, w_up.T, w_down, w_out)
    else:
        own_proj = lax.dynamic_slice_in_dim(proj_local, s * part, part, 0)

        def padded(array):
            return jnp.pad(array, ((0, 0), (0, FFP - ff)))

        whole_ffn = jnp.concatenate([padded(w_gate), padded(w_up), padded(w_down.T), w_out.T], 1)
        own_ffn = lax.dynamic_slice_in_dim(whole_ffn, s * part, part, 0)
    ffn_all = lax.all_gather(own_ffn, BY_HEAD, axis=0, tiled=True).reshape(n_head, width, columns)
    ring_pieces = [own_proj]
    for _ in range(n_head - 1):
        ring_pieces.append(ring(ring_pieces[-1]))
    proj_one = gather_plane(ring_pieces[1][None], n_seq)
    proj_far = gather_plane(jnp.stack(ring_pieces[2:]), n_seq)

    ids_before = jnp.where(s == 0, -1, ids_before)
    ids = lax.dynamic_slice_in_dim(jnp.concatenate([ids_before, seq_ids]), z * rows, ext)
    ids_pad = jnp.concatenate([ids, jnp.full((HALO,), -2, jnp.int32)])
    idc = jnp.broadcast_to(ids_pad[:, None], (ext + HALO, 128))
    idr = jnp.broadcast_to(ids[None, :], (8, ext))
    halo = before.astype(f32)
    normed_ext, turned = pl.pallas_call(
        prep_kernel,
        grid=(1,),
        in_specs=[smem, same(HALO, width), same(rows, width), same(1, width)],
        out_specs=[same(ext, width), same(width, rows)],
        out_shape=[sds((ext, width), bf16), sds((width, rows), bf16)],
        scratch_shapes=[pltpu.VMEM((ext, width), f32)],
        compiler_params=params(),
        cost_estimate=cost(5),
        name="prep",
    )(table, halo, inputs, norm1_gain[None])

    idc_spec, idr_spec = same(ext + HALO, 128), same(8, ext)
    hidden_spec = pl.BlockSpec(memory_space=pl.ANY)
    shapes = [
        ((ext, 768), f32), ((rows, 128), f32), ((24, 128), f32), ((rows, 768), bf16), ((rows, 768), f32), ((2, rows, 256), bf16),
        ((2, rows, 128), bf16), ((2, chunks, 128, 256), bf16),
    ]

    def shifted(by, *shape):
        zeros = (0,) * len(shape)
        return pl.BlockSpec((None,) + shape, lambda i: (i + by,) + zeros)

    def local_pieces(columns, at=0):
        return [pl.BlockSpec((quarter, columns), lambda k, i=i: (i, at)) for i in range(4)]

    first = pl.pallas_call(
        functools.partial(front_kernel, chunks, 0),
        grid=(1,),
        in_specs=[same(ext, width)] + local_pieces(896) + [idc_spec, idr_spec],
        out_specs=[lead(*shape) for shape, _ in shapes] + [lead(2, 128, 256)],
        out_shape=[sds((n_head,) + shape, kind) for shape, kind in shapes] + [sds((1, 2, 128, 256), bf16)],
        compiler_params=params(),
        cost_estimate=cost(9),
        name="front_near",
    )(normed_ext, *[proj_local] * 4, idc, idr)
    def front_more(pieces, by, before_it, name):
        size = pieces[0].shape[0]
        return pl.pallas_call(
            functools.partial(front_kernel, chunks, len(shapes)),
            grid=(size,),
            in_specs=[same(ext, width)] + [lead(quarter, 896)] * 4 + [idc_spec, idr_spec] + [hidden_spec] * len(shapes),
            out_specs=[shifted(by, *shape) for shape, _ in shapes] + [lead(2, 128, 256)],
            out_shape=[sds((n_head,) + shape, kind) for shape, kind in shapes] + [sds((size, 2, 128, 256), bf16)],
            input_output_aliases={7 + i: i for i in range(len(shapes))},
            compiler_params=params(),
            cost_estimate=cost(7 * size + 1),
            name=name,
        )(normed_ext, *pieces, idc, idr, *before_it[:-1])

    second = front_more(proj_one, 1, first, "front_one")
    filled = front_more(proj_far, 2, second, "front_far")
    projected, logits, taps_all, qkv, summed, uw, inverse, prefixes, totals = filled
    every_total = [first[-1][0], second[-1][0]] + [totals[k] for k in range(n_head - 2)]
    state_in, got, kept = exchange_forward(every_total, n_seq, s, z)
    score, reach, base, far = pl.pallas_call(
        functools.partial(reach_kernel, chunks),
        grid=(n_head,),
        in_specs=[lead(rows, 768), lead(2, rows, 256), lead(2, chunks, 128, 256), idc_spec, idr_spec],
        out_specs=[lead(2, rows, 128)] * 4,
        out_shape=[sds((n_head, 2, rows, 128), kind) for kind in (bf16, bf16, f32, bf16)],
        compiler_params=params(),
        cost_estimate=cost(9),
        name="reach",
    )(qkv, uw, prefixes, idc, idr)
    gain_rows = jnp.broadcast_to(head_gain[None, :], (8, 128))
    attended, head_out = pl.pallas_call(
        attend_kernel,
        grid=(n_head,),
        in_specs=[lead(2, rows, 128), lead(2, rows, 128), lead(2, 128, 128), same(8, 128), idc_spec],
        out_specs=[lead(2, rows, 128), pl.BlockSpec((rows, 256), lambda i: (0, i))],
        out_shape=[sds((n_head, 2, rows, 128), f32), sds((rows, n_head * 256), bf16)],
        compiler_params=params(),
        cost_estimate=cost(5),
        name="attend",
    )(base, far, state_in, gain_rows, idc)

    order = ((z - jnp.arange(n_head)) % n_head).astype(jnp.int32)

    def by_slot(columns, at):
        return pl.BlockSpec((None, width, columns), lambda k, order: (order[k], 0, at))

    def fixed(*shape):
        zeros = (0,) * len(shape)
        return pl.BlockSpec(shape, lambda k, *scalars: zeros)

    def led(*shape):
        zeros = (0,) * len(shape)
        return pl.BlockSpec((None,) + shape, lambda k, *scalars: (k,) + zeros)

    head_columns = pl.BlockSpec((rows, 256), lambda k, *scalars: (0, k))
    residual, normed_two = pl.pallas_call(
        functools.partial(mix_kernel, n_head),
        grid_spec=pltpu.PrefetchScalarGridSpec(
            num_scalar_prefetch=1,
            grid=(n_head,),
            in_specs=[head_columns, fixed(rows, width), fixed(1, width), by_slot(256, 3 * FFP // 256)],
            out_specs=[fixed(rows, width), fixed(rows, width)],
        ),
        out_shape=[sds((rows, width), f32), sds((rows, width), bf16)],
        compiler_params=params(),
        cost_estimate=cost(5),
        name="mix",
    )(order, head_out, inputs, norm2_gain[None], ffn_all)
    near, wide = core_first(n_seq)
    swap = [1] * n_seq

    def ffn_weight(at):
        return pl.BlockSpec((None, width, FFP), lambda k, table, order: (order[k], 0, at))

    ffn_grads = sds((n_head, width // 2, 3 * FFP), bf16)
    ffn_out, grad_two, *ffn_a = pl.pallas_call(
        functools.partial(ffn_kernel, 0),
        grid_spec=pltpu.PrefetchScalarGridSpec(
            num_scalar_prefetch=2,
            grid=(n_head,),
            in_specs=[fixed(rows, width), pl.BlockSpec((rows, width), lambda k, table, order: (order[0], 0))]
            + [ffn_weight(i) for i in range(3)],
            out_specs=[fixed(rows, width), fixed(rows, width)] + [led(width // 2, 3 * FFP)] * 2,
            scratch_shapes=[pltpu.VMEM((width, rows), bf16)] * 2,
        ),
        out_shape=[sds((rows, width), f32), sds((rows, width), f32), ffn_grads, ffn_grads],
        compiler_params=params(60),
        cost_estimate=cost(2),
        name="ffn",
    )(table, order, normed_two, cotangent, ffn_all, ffn_all, ffn_all)
    if n_seq == 8:
        ffn_a = [ffn_a[0], seq_permute(ffn_a[1], swap)]
        send_a = after_core(*ffn_a)

    output, grad_residual, grad_norm_two, out_own, out_other, datt, local_grad, gain_part = pl.pallas_call(
        turn_kernel,
        grid_spec=pltpu.PrefetchScalarGridSpec(
            num_scalar_prefetch=2,
            grid=(n_head,),
            in_specs=[
                fixed(rows, width), fixed(rows, width), fixed(rows, width),
                pl.BlockSpec((rows, width), lambda k, table, order: (order[0], 0)), fixed(1, width), head_columns,
                pl.BlockSpec((None, width, 256), lambda k, table, order: (order[k], 0, 3 * FFP // 256)), led(2, rows, 128),
                led(2, rows, 128), fixed(8, 128), fixed(ext + HALO, 128),
            ],
            out_specs=[
                fixed(rows, width), fixed(rows, width), fixed(8, width),
                led(width // 2, 256), led(width // 2, 256), led(2, rows, 128),
                led(2, 128, 128), led(8, 128),
            ],
            scratch_shapes=[pltpu.VMEM((rows, width), bf16), pltpu.VMEM((width, rows), bf16)],
        ),
        out_shape=[
            sds((rows, width), bf16), sds((rows, width), f32), sds((8, width), f32), sds((n_head, width // 2, 256), bf16),
            sds((n_head, width // 2, 256), bf16), sds((n_head, 2, rows, 128), bf16), sds((n_head, 2, 128, 128), bf16), sds((n_head, 8, 128), f32),
        ],
        compiler_params=params(),
        cost_estimate=cost(0.6),
        name="turn",
    )(
        table, order, ffn_out, grad_two, residual, cotangent, norm2_gain[None], head_out, ffn_all, attended, far, gain_rows, idc,
    )
    grad_out_state = exchange_backward([local_grad[k] for k in range(n_head)], got, kept, n_seq, s, z)
    if n_seq == 8:
        datt = tie(datt, send_a)
        more_a = seq_permute(send_a, wide)
    inner_shapes = [((2, chunks, 128, 128), bf16)] + [((2, rows, 128), kind) for kind in (bf16, f32, f32, f32)]
    states, pseudo, dq, dk, dp = pl.pallas_call(
        functools.partial(inner_back_kernel, chunks, 0),
        grid=(n_head,),
        in_specs=[
            lead(rows, 768), lead(2, rows, 256), lead(2, chunks, 128, 256), lead(2, rows, 128), lead(2, rows, 128),
            lead(2, 128, 128), idc_spec, idr_spec,
        ],
        out_specs=[lead(*shape) for shape, _ in inner_shapes],
        out_shape=[sds((n_head,) + shape, kind) for shape, kind in inner_shapes],
        compiler_params=params(),
        cost_estimate=cost(1),
        name="inner_back",
    )(qkv, uw, prefixes, score, datt, state_in, idc, idr)
    def tail(slot, pieces, before_it, name):
        last = bool(before_it)
        size = 896 if last else 1408
        grad_size = sds((2, width // 2, size), bf16)

        def at(*shape):
            zeros = (0,) * len(shape)
            return pl.BlockSpec((None,) + shape, lambda i: (slot(i),) + zeros)

        sums = [same(rows, width), same(2 * HALO, width)]
        sum_shapes = [sds((rows, width), f32), sds((2 * HALO, width), f32)]
        given = [out_own, out_other, out_own, out_other]
        given_specs = [pl.BlockSpec((None, width // 2, 256), lambda i: (i + 1, 0, 0))] * 2
        given_specs += [pl.BlockSpec((None, width // 2, 256), lambda i: (3 - 3 * i, 0, 0))] * 2
        outs, out_specs = sum_shapes, sums
        if last:
            given = [*before_it, inputs, halo, norm1_gain[None], grad_residual]
            given_specs = sums + [same(rows, width), same(HALO, width), same(1, width), same(rows, width)]
            outs = [sds((rows, width), f32), sds((HALO, width), f32), sds((8, width), f32)]
            out_specs = [same(rows, width), same(HALO, width), same(8, width)]
        return pl.pallas_call(
            functools.partial(tail_kernel, chunks, n_seq, last),
            grid=(2,),
            in_specs=[
                smem, at(rows, 768), at(2, rows, 256), at(2, rows, 128), at(2, rows, 128), at(2, rows, 128),
                at(2, chunks, 128, 128), at(2, rows, 128), at(2, rows, 128), at(2, rows, 128), at(2, rows, 128),
                at(rows, 768), at(ext, 768), at(rows, 128), at(2, 128, 128), at(24, 128), idc_spec, idr_spec,
                same(width, rows), same(2 * HALO, width),
            ]
            + [spec for spec, _ in pieces]
            + given_specs,
            out_specs=out_specs + [lead(width // 2, size)] * 2,
            out_shape=outs + [grad_size] * 2,
            scratch_shapes=[
                pltpu.VMEM((rows, 896), bf16), pltpu.VMEM((2 * HALO, 896), bf16), pltpu.VMEM((rows, 768), f32),
                pltpu.VMEM((rows + 2 * HALO, 128), f32), pltpu.VMEM((128, 128), f32), pltpu.VMEM((width, 128), f32),
            ]
            + ([pltpu.VMEM((rows, width), f32), pltpu.VMEM((2 * HALO, width), f32)] if last else []),
            compiler_params=params(60),
            cost_estimate=cost(1),
            name=name,
        )(
            table, qkv, uw, inverse, reach, datt, states, pseudo, dq, dk, dp, summed, projected, logits, grad_out_state, taps_all, idc,
            idr, turned, normed_ext, *[piece for _, piece in pieces], *given,
        )

    def picked(arrays, k):
        return [(pl.BlockSpec((None, quarter, 896), lambda i: (k, 0, 0)), array) for array in arrays]

    here = list(zip(local_pieces(896), [proj_local] * 4))
    *partial, one_own, one_other = tail(lambda i: i + 1, picked(proj_one, 0) + picked(proj_far, 0), [], "tail_one")
    if n_seq == 8:
        one_got = seq_permute(one_other, swap)
        one_send = after_core(one_own, one_got)
        next_a = after_wide(*ffn_a, more_a)
        partial[0] = tie(partial[0], next_a, one_send)
        last_a = seq_permute(next_a, near)
        one_more = seq_permute(one_send, wide)
    inputs_grad, halo_grad, grad_norm_one, two_own, two_other = tail(
        lambda i: 3 - 3 * i, picked(proj_far, 1) + here, partial, "tail_two"
    )
    from_next = lax.ppermute(halo_grad, WHOLE, [(i + 1, i) for i in range(count - 1)])
    gains = jnp.concatenate([grad_norm_one[0], grad_norm_two[0], jnp.sum(gain_part[:, 0], 0)]).reshape(-1, 128)
    steps = gain_steps(n_seq, n_head)
    if n_seq == 8:
        two_got = seq_permute(two_other, swap)
        for step in steps[:2]:
            gains = swap_add(gains, step)
        sum_a = after_near(*ffn_a, more_a, last_a)
        moved = ring(tie(sum_a[1], gains))
        two_send = after_core(two_own, tie(two_got, sum_a))
        two_more = seq_permute(two_send, wide)
        one_send = after_wide(one_own, one_got, tie(one_more, two_other))
        one_last = seq_permute(one_send, near)
        moved = ring(plus(moved, sum_a[2]))
        two_send = after_wide(two_own, two_got, two_more)
        two_last = seq_permute(two_send, near)
        one_sum = after_near(one_own, one_got, one_more, one_last)
        gains = tie(gains, two_send)
        two_sum = after_near(two_own, two_got, two_more, two_last)
        for step in steps[2:]:
            gains = swap_add(gains, step)
        from_next = tie(from_next, two_sum)
        sum_ffn = ring(plus(moved, sum_a[3])).astype(f32) + sum_a[0].astype(f32)
    else:
        one_sum, two_sum, sum_a = (reduce_whole(*pair) for pair in ((one_own, one_other), (two_own, two_other), ffn_a))
        for step in steps:
            gains = swap_add(gains, step)
        sum_ffn = reduce_ring([sum_a[k] for k in range(n_head)])
    third = jnp.concatenate([two_sum[0], one_sum[0, :, 1152:]], 1)
    fourth = jnp.concatenate([two_sum[1], one_sum[1, :, 1152:]], 1)
    sum_proj = reduce_ring([fourth, one_sum[0, :, :1152], one_sum[1, :, :1152], third])
    inputs_grad = inputs_grad.at[rows - HALO :].add(from_next)
    lanes = 128 // n_seq
    gains = gains.reshape(-1)
    return (
        output, inputs_grad, gains[:width], sum_proj[:, :256], sum_proj[:, 256:512], sum_proj[:, 512:768], sum_proj[:, 768:770],
        sum_proj[:lanes, 770:794].T.reshape(3, 4, 2, lanes), gains[2 * width :], sum_proj[:, 896:].T, gains[width : 2 * width],
        sum_ffn[:, :ff], sum_ffn[:, FFP : FFP + ff], sum_ffn[:, 2 * FFP : 2 * FFP + ff].T,
    )


def solution(mesh):
    return jax.shard_map(
        local,
        mesh=mesh,
        in_specs=(
            P(("seq", "head"), None),
            P(),
            P(None, "head"),
            P(None, "head"),
            P(None, "head"),
            P(None, "head"),
            P(None, None, "head", None),
            P(),
            P("head", None),
            P(),
            P(None, "head"),
            P(None, "head"),
            P("head", None),
            P("seq"),
            P("seq", None),
        ),
        out_specs=(
            P(("seq", "head"), None),
            P(("seq", "head"), None),
            P(),
            P("seq", "head"),
            P("seq", "head"),
            P("seq", "head"),
            P("seq", "head"),
            P(None, None, "head", "seq"),
            P(),
            P("head", "seq"),
            P(),
            P("seq", "head"),
            P("seq", "head"),
            P("head", "seq"),
        ),
        check_vma=False,
    )
```

```python
import functools

import jax
import jax.numpy as jnp
from jax import lax
from jax.experimental import pallas as pl
from jax.experimental.pallas import tpu as pltpu
from jax.sharding import PartitionSpec as P

SEQS = 4
CHUNK = 128
HALO = 8
FFP = 768
epsilon = 1e-06
beta_shift = 4.0
f32 = jnp.float32
bf16 = jnp.bfloat16
WHOLE = ("seq", "head")
BY_HEAD = ("head", "seq")


def nn(a, b):
    return lax.dot_general(a, b, (((1,), (0,)), ((), ())), preferred_element_type=f32)


def nt(a, b):
    return lax.dot_general(a, b, (((1,), (1,)), ((), ())), preferred_element_type=f32)


def tn(a, b):
    return lax.dot_general(a, b, (((0,), (0,)), ((), ())), preferred_element_type=f32)


def params(mib=56, grid=1):
    return pltpu.CompilerParams(
        vmem_limit_bytes=mib << 20, dimension_semantics=("arbitrary",) * grid
    )


def lead(*shape):
    zeros = (0,) * len(shape)
    return pl.BlockSpec((None,) + shape, lambda i: (i,) + zeros)


def same(*shape):
    zeros = (0,) * len(shape)
    return pl.BlockSpec(shape, lambda i: zeros)


def cost(us):
    return pl.CostEstimate(flops=int(us * 1.1e9), bytes_accessed=int(us * 1e6), transcendentals=0)


def sds(shape, kind):
    return jax.ShapeDtypeStruct(shape, kind)


def pack_proj_kernel(table_ref, q_ref, k_ref, v_ref, more_ref, out_ref):
    out_ref[:, 0:256] = q_ref[...]
    out_ref[:, 256:512] = k_ref[...]
    out_ref[:, 512:768] = v_ref[...]
    out_ref[:, 768:896] = more_ref[...]


def pack_ffn_kernel(table_ref, gate_ref, up_ref, down_ref, out_w_ref, out_ref, tall):
    ff = gate_ref.shape[0]
    tall[ff:FFP, :] = jnp.zeros((FFP - ff, 128), f32)
    for i, ref in enumerate((gate_ref, up_ref, down_ref)):
        tall[0:ff, :] = ref[...].astype(f32)
        out_ref[:, i * FFP : (i + 1) * FFP] = jnp.transpose(tall[...]).astype(bf16)
    out_ref[:, 3 * FFP : 3 * FFP + 256] = jnp.transpose(out_w_ref[...].astype(f32)).astype(bf16)


def prep_kernel(table_ref, halo_ref, x_ref, gain_ref, normed_ref, turned_ref, wide):
    rows = x_ref.shape[0]
    wide[0:HALO, :] = halo_ref[...]
    wide[HALO : HALO + rows, :] = x_ref[...].astype(f32)
    full = wide[...]
    wide[...] = full * lax.rsqrt(jnp.mean(full * full, -1, keepdims=True) + epsilon) * gain_ref[...]
    for i in range(8):
        at = slice(i * 128, (i + 1) * 128)
        here = pl.ds(pl.multiple_of(table_ref[i] * 128, 128), 128)
        block = wide[:, here]
        normed_ref[:, at] = block.astype(bf16)
        turned_ref[at, :] = jnp.transpose(block[HALO:, :]).astype(bf16)


def mix_kernel(groups, order_ref, head_ref, x_ref, gain_ref, weight_ref, res_ref, normed_ref):
    step = pl.program_id(0)
    part = nt(head_ref[...], weight_ref[...])

    @pl.when(step == 0)
    def _():
        res_ref[...] = x_ref[...].astype(f32) + part

    @pl.when(step > 0)
    def _():
        res_ref[...] += part

    @pl.when(step == groups - 1)
    def _():
        full = res_ref[...]
        normed = full * lax.rsqrt(jnp.mean(full * full, -1, keepdims=True) + epsilon) * gain_ref[...]
        normed_ref[...] = normed.astype(bf16)


def turn_kernel(
    table_ref, order_ref, ffn_ref, two_ref, res_ref, dy_ref, gain_two_ref, head_ref, weight_ref, att_ref, far_ref, gain_ref, idc_ref,
    out_ref, gres_ref, gtwo_ref, own_ref, other_ref, datt_ref, local_grad_ref, gain_grad_ref, mixer, turned,
):
    step = pl.program_id(0)
    rows = att_ref.shape[1]

    @pl.when(step == 0)
    def _():
        res = res_ref[...]
        two = two_ref[...]
        r2 = lax.rsqrt(jnp.mean(res * res, -1, keepdims=True) + epsilon)
        scaled = gain_two_ref[...] * two
        grad = dy_ref[...].astype(f32) + r2 * scaled - res * ((r2 * r2 * r2) * jnp.mean(res * scaled, -1, keepdims=True))
        gres_ref[...] = grad
        mixer[...] = grad.astype(bf16)
        for i in range(8):
            here = pl.ds(pl.multiple_of(table_ref[i] * 128, 128), 128)
            turned[i * 128 : (i + 1) * 128, :] = jnp.transpose(gres_ref[:, here]).astype(bf16)
        gtwo_ref[...] = jnp.broadcast_to(jnp.sum(two * res * r2, 0, keepdims=True), gtwo_ref.shape)
        out_ref[...] = (res + ffn_ref[...]).astype(bf16)

    gho = nn(mixer[...], weight_ref[...])
    mask = (idc_ref[HALO : HALO + rows, :] < SEQS).astype(f32)
    gain = gain_ref[0:1, :]
    total = jnp.zeros((1, 128), f32)
    for hh in range(2):
        out = att_ref[hh]
        go = gho[:, hh * 128 : (hh + 1) * 128] * mask
        rh = lax.rsqrt(jnp.mean(out * out, -1, keepdims=True) + epsilon)
        total = total + jnp.sum(go * out * rh, 0, keepdims=True)
        inner = jnp.mean(out * gain * go, -1, keepdims=True)
        grad = (rh * gain * go - out * (rh * rh * rh) * inner).astype(bf16)
        datt_ref[hh] = grad
        local_grad_ref[hh] = tn(far_ref[hh], grad).astype(bf16)
    gain_grad_ref[...] = jnp.broadcast_to(total, (8, 128))
    half = own_ref.shape[0]
    own_ref[...] = nn(turned[0:half, :], head_ref[...]).astype(bf16)
    other_ref[...] = nn(turned[half : 2 * half, :], head_ref[...]).astype(bf16)


def chunk_masks(idc_ref, idr_ref, c):
    base = HALO + c * CHUNK
    own = idc_ref[base : base + CHUNK, :]
    row = idr_ref[0:1, base : base + CHUNK]
    prev = idc_ref[base - 1 : base, :]
    last = idc_ref[base + CHUNK - 1 : base + CHUNK, :]
    equal = own == row
    carry = (own == prev).astype(f32)
    to_last = (own == last).astype(f32)
    carry_last = (last == prev).astype(f32)
    return equal, carry, to_last, carry_last


def positions():
    row = lax.broadcasted_iota(jnp.int32, (CHUNK, CHUNK), 0)
    col = lax.broadcasted_iota(jnp.int32, (CHUNK, CHUNK), 1)
    return row, col


def front_kernel(chunks, skip, normed_ref, w0, w1, w2, w3, idc_ref, idr_ref, *rest):
    proj_ref, lgt_ref, cw_ref, qkv_ref, sum_ref, uw_ref, inv_ref, pre_ref, tot_ref = rest[skip:]
    rows = CHUNK
    quarter = w0.shape[0]
    wide = nn(normed_ref[:, 0:quarter], w0[...])
    for i, w in enumerate((w1, w2, w3)):
        wide = wide + nn(normed_ref[:, (i + 1) * quarter : (i + 2) * quarter], w[...])
    proj_ref[...] = wide[:, :768]
    lgt_ref[...] = wide[HALO:, 768:896]
    turned = jnp.transpose(w0[0:128, 768:896].astype(f32))
    for j in range(24):
        cw_ref[j : j + 1, :] = turned[2 + 3 * j : 3 + 3 * j] + turned[3 + 3 * j : 4 + 3 * j] + turned[4 + 3 * j : 5 + 3 * j]
    for b in range(6):
        part, hh = b // 2, b % 2
        cols = slice(b * 128, (b + 1) * 128)
        taps = [cw_ref[(part * 4 + j) * 2 + hh : (part * 4 + j) * 2 + hh + 1, :] for j in range(4)]
        for c in range(chunks):
            base = HALO + c * rows
            own = idc_ref[base : base + rows, :]
            acc = proj_ref[base : base + rows, cols] * taps[0]
            for j in range(1, 4):
                prior = idc_ref[base - j : base - j + rows, :]
                acc = acc + jnp.where(prior == own, proj_ref[base - j : base - j + rows, cols], 0.0) * taps[j]
            sum_ref[c * rows : (c + 1) * rows, cols] = acc
            mixed = acc / (1.0 + jnp.exp(-acc))
            if part < 2:
                mixed = mixed * lax.rsqrt(jnp.sum(mixed * mixed, -1, keepdims=True) + epsilon)
            qkv_ref[c * rows : (c + 1) * rows, cols] = mixed.astype(bf16)
    row, col = positions()
    differ = row ^ col
    strict = row > col
    units = [(hh, c) for c in range(chunks) for hh in range(2)]
    lower, inv, scaled = {}, {}, {}
    for hh, c in units:
        equal, carry, _, _ = chunk_masks(idc_ref, idr_ref, c)
        at = slice(c * CHUNK, (c + 1) * CHUNK)
        beta = jax.nn.sigmoid(jnp.broadcast_to(lgt_ref[at, hh : hh + 1], (CHUNK, 128)) - beta_shift)
        beta = jnp.where(idc_ref[HALO + c * CHUNK : HALO + (c + 1) * CHUNK, :] < SEQS, beta, 0.0)
        keys = qkv_ref[at, 256 + hh * 128 : 256 + (hh + 1) * 128]
        values = qkv_ref[at, 512 + hh * 128 : 512 + (hh + 1) * 128]
        low = jnp.where(equal & strict, nt(keys, keys), 0.0) * beta
        lower[hh, c] = low
        inv[hh, c] = jnp.where(row == col, 1.0, 0.0) - jnp.where(differ == 1, low, 0.0)
        scaled[hh, c] = jnp.concatenate(
            [(values.astype(f32) * beta).astype(bf16), (keys.astype(f32) * (beta * carry)).astype(bf16)], axis=1
        )
    for k in range(1, 7):
        level = (differ >> k) == 1
        for u in units:
            off = jnp.where(level, lower[u], 0.0).astype(bf16)
            half = inv[u].astype(bf16)
            inv[u] = inv[u] - nn(half, nn(off, half).astype(bf16))
    for hh, c in units:
        at = slice(c * CHUNK, (c + 1) * CHUNK)
        half = inv[hh, c].astype(bf16)
        inv_ref[hh, at, :] = half
        uw_ref[hh, at, :] = nn(half, scaled[hh, c]).astype(bf16)
    eye = jnp.where(row == col, 1.0, 0.0)
    state = [[eye, jnp.zeros((CHUNK, CHUNK), f32)] for _ in range(2)]
    for c in range(chunks):
        at = slice(c * CHUNK, (c + 1) * CHUNK)
        _, _, to_last, carry_last = chunk_masks(idc_ref, idr_ref, c)
        for hh in range(2):
            packed = jnp.concatenate([state[hh][0].astype(bf16), state[hh][1].astype(bf16)], axis=1)
            pre_ref[hh, c] = packed
            moved = nn(uw_ref[hh, at, 128:256], packed)
            change = jnp.concatenate(
                [(-moved[:, :128]).astype(bf16), (uw_ref[hh, at, 0:128].astype(f32) - moved[:, 128:]).astype(bf16)], axis=1
            )
            keys = qkv_ref[at, 256 + hh * 128 : 256 + (hh + 1) * 128]
            kept = (keys.astype(f32) * to_last).astype(bf16)
            step = tn(kept, change)
            state[hh] = [state[hh][0] * carry_last + step[:, :128], state[hh][1] * carry_last + step[:, 128:]]
    for hh in range(2):
        tot_ref[hh] = jnp.concatenate([state[hh][0].astype(bf16), state[hh][1].astype(bf16)], axis=1)


def reach_kernel(chunks, qkv_ref, uw_ref, pre_ref, idc_ref, idr_ref, score_ref, reach_ref, base_ref, far_ref):
    row, col = positions()
    causal = row >= col
    for c in range(chunks):
        at = slice(c * CHUNK, (c + 1) * CHUNK)
        equal, carry, _, _ = chunk_masks(idc_ref, idr_ref, c)
        for hh in range(2):
            queries = qkv_ref[at, hh * 128 : (hh + 1) * 128]
            keys = qkv_ref[at, 256 + hh * 128 : 256 + (hh + 1) * 128]
            score = jnp.where(causal & equal, nt(queries, keys), 0.0).astype(bf16)
            score_ref[hh, at, :] = score
            both = nn(score, uw_ref[hh, at, :])
            reach = (queries.astype(f32) * carry - both[:, 128:]).astype(bf16)
            reach_ref[hh, at, :] = reach
            far = nn(reach, pre_ref[hh, c])
            far_ref[hh, at, :] = far[:, :128].astype(bf16)
            base_ref[hh, at, :] = both[:, :128] + far[:, 128:]


def attend_kernel(base_ref, far_ref, state_ref, gain_ref, idc_ref, out_ref, head_ref):
    rows = base_ref.shape[1]
    mask = (idc_ref[HALO : HALO + rows, :] < SEQS).astype(f32)
    for hh in range(2):
        out = base_ref[hh] + nn(far_ref[hh], state_ref[hh])
        out_ref[hh] = out
        rh = lax.rsqrt(jnp.mean(out * out, -1, keepdims=True) + epsilon)
        head_ref[:, hh * 128 : (hh + 1) * 128] = (out * rh * gain_ref[0:1, :] * mask).astype(bf16)


def ffn_kernel(later, table_ref, order_ref, normed_ref, dy_ref, gate_ref, up_ref, down_ref, *rest):
    given, (out_ref, grad_ref, own_ref, other_ref, nturned, dturned) = rest[:later], rest[later:]
    step = pl.program_id(0)
    span = FFP

    @pl.when(step == 0)
    def _():
        for i in range(8):
            at = slice(i * 128, (i + 1) * 128)
            here = pl.ds(pl.multiple_of(table_ref[i] * 128, 128), 128)
            nturned[at, :] = jnp.transpose(normed_ref[:, here].astype(f32)).astype(bf16)
            dturned[at, :] = jnp.transpose(dy_ref[:, here].astype(f32)).astype(bf16)

    gate = nn(normed_ref[...], gate_ref[...])
    up = nn(normed_ref[...], up_ref[...])
    sig = 1.0 / (1.0 + jnp.exp(-gate))
    act = gate * sig
    hidden = (act * up).astype(bf16)
    grad_hidden = nn(dy_ref[...], down_ref[...])
    grad_gate = (grad_hidden * up * (sig * (1.0 + gate * (1.0 - sig)))).astype(bf16)
    grad_up = (grad_hidden * act).astype(bf16)
    out = nt(hidden, down_ref[...])
    back = nt(grad_gate, gate_ref[...]) + nt(grad_up, up_ref[...])

    @pl.when(step == 0)
    def _():
        out_ref[...] = given[0][...] + out if later else out
        grad_ref[...] = given[1][...] + back if later else back

    @pl.when(step > 0)
    def _():
        out_ref[...] += out
        grad_ref[...] += back

    half = own_ref.shape[0]
    for target, into in ((own_ref, slice(0, half)), (other_ref, slice(half, 2 * half))):
        target[:, 0:span] = nn(nturned[into, :], grad_gate).astype(bf16)
        target[:, span : 2 * span] = nn(nturned[into, :], grad_up).astype(bf16)
        target[:, 2 * span : 3 * span] = nn(dturned[into, :], hidden).astype(bf16)


def inner_back_kernel(chunks, skip, qkv_ref, uw_ref, pre_ref, score_ref, datt_ref, state_ref, idc_ref, idr_ref, *rest):
    states_ref, pseudo_ref, dq_ref, dk_ref, dp_ref = rest[skip:]
    row, col = positions()
    causal = row >= col
    for c in range(chunks):
        at = slice(c * CHUNK, (c + 1) * CHUNK)
        equal, carry, _, _ = chunk_masks(idc_ref, idr_ref, c)
        for hh in range(2):
            queries = qkv_ref[at, hh * 128 : (hh + 1) * 128]
            keys = qkv_ref[at, 256 + hh * 128 : 256 + (hh + 1) * 128]
            grad = datt_ref[hh, at, :]
            state = (nn(pre_ref[hh, c, :, 0:128], state_ref[hh]) + pre_ref[hh, c, :, 128:256].astype(f32)).astype(bf16)
            states_ref[hh, c] = state
            pseudo = (uw_ref[hh, at, 0:128].astype(f32) - nn(uw_ref[hh, at, 128:256], state)).astype(bf16)
            pseudo_ref[hh, at, :] = pseudo
            grad_score = jnp.where(causal & equal, nt(grad, pseudo), 0.0).astype(bf16)
            dq_ref[hh, at, :] = nt(grad, state) * carry + nn(grad_score, keys)
            dk_ref[hh, at, :] = tn(grad_score, queries)
            dp_ref[hh, at, :] = tn(score_ref[hh, at, :], grad)


def tail_kernel(
    chunks, n_seq, last, table_ref, qkv_ref, uw_ref, inv_ref, reach_ref, datt_ref, states_ref, pseudo_ref, dq_ref, dk_ref, dp_ref,
    sum_ref, proj_ref, lgt_ref, gout_ref, cw_ref, idc_ref, idr_ref,
    turned_ref, edge_ref, *rest,
):
    first_w, second_w, rest = rest[:4], rest[4:8], rest[8:]
    if last:
        gn_in, gh_in, x_ref, halo_ref, gain_ref, gres_ref = rest[:6]
        in_ref, hin_ref, gone_ref, own_ref, other_ref, gp_ref, first_ref, dqkv, pad, spread, extra, gn_ref, gh_ref = rest[6:]
    else:
        outs_w, (gn_ref, gh_ref, own_ref, other_ref, gp_ref, first_ref, dqkv, pad, spread, extra) = rest[:4], rest[4:]
    step = pl.program_id(0)
    row, col = positions()
    strict = row > col
    lane = lax.broadcasted_iota(jnp.int32, (CHUNK, 128), 1)
    grad_state = [gout_ref[hh].astype(f32) for hh in range(2)]
    for c in range(chunks - 1, -1, -1):
        at = slice(c * CHUNK, (c + 1) * CHUNK)
        equal, carry, to_last, carry_last = chunk_masks(idc_ref, idr_ref, c)
        own = idc_ref[HALO + c * CHUNK : HALO + (c + 1) * CHUNK, :]
        dlgt = jnp.zeros((CHUNK, 128), f32)
        for hh in range(2):
            keys = qkv_ref[at, 256 + hh * 128 : 256 + (hh + 1) * 128]
            keys_f = keys.astype(f32)
            values = qkv_ref[at, 512 + hh * 128 : 512 + (hh + 1) * 128]
            kept = (keys_f * to_last).astype(bf16)
            packed = grad_state[hh].astype(bf16)
            push = nn(kept, packed)
            grad_state[hh] = grad_state[hh] * carry_last + tn(reach_ref[hh, at, :], datt_ref[hh, at, :]) - tn(
                uw_ref[hh, at, 128:256], push.astype(bf16)
            )
            full = (dp_ref[hh, at, :] + push).astype(bf16)
            solved = tn(inv_ref[hh, at, :], full)
            solved_h = solved.astype(bf16)
            pseudo = pseudo_ref[hh, at, :]
            gate = jax.nn.sigmoid(jnp.broadcast_to(lgt_ref[at, hh : hh + 1], (CHUNK, 128)) - beta_shift)
            mask = (own < SEQS).astype(f32)
            beta = gate * mask
            back = nt(solved_h, states_ref[hh, c]) * carry
            outer = jnp.where(equal & strict, nt(solved_h, pseudo), 0.0)
            overlap = nt(keys, keys)
            rate = jnp.sum(solved * values.astype(f32) - back * keys_f - outer * overlap, -1, keepdims=True)
            dlgt = jnp.where(lane == hh, rate * mask * gate * (1.0 - gate), dlgt)
            mixed = (outer * beta).astype(bf16)
            dqkv[at, 256 + hh * 128 : 256 + (hh + 1) * 128] = (
                dk_ref[hh, at, :] + nt(pseudo, packed) * to_last - beta * back - nn(mixed, keys) - tn(mixed, keys)
            )
            dqkv[at, 512 + hh * 128 : 512 + (hh + 1) * 128] = beta * solved
            dqkv[at, hh * 128 : (hh + 1) * 128] = dq_ref[hh, at, :]
        gp_ref[at, 768:896] = dlgt.astype(bf16)
    rows = CHUNK
    length = chunks * CHUNK
    for b in range(6):
        part, hh = b // 2, b % 2
        cols = slice(b * 128, (b + 1) * 128)
        taps = [cw_ref[(part * 4 + j) * 2 + hh : (part * 4 + j) * 2 + hh + 1, :] for j in range(4)]
        pad[0:HALO, :] = jnp.zeros((HALO, 128), f32)
        pad[HALO + length : 2 * HALO + length, :] = jnp.zeros((HALO, 128), f32)
        sums = [jnp.zeros((1, 128), f32) for _ in range(4)]
        for c in range(chunks):
            at = slice(c * rows, (c + 1) * rows)
            base = HALO + c * rows
            u = sum_ref[at, cols]
            sig = 1.0 / (1.0 + jnp.exp(-u))
            grad = dqkv[at, cols]
            if part < 2:
                mixed = u * sig
                r = lax.rsqrt(jnp.sum(mixed * mixed, -1, keepdims=True) + epsilon)
                grad = r * grad - mixed * ((r * r * r) * jnp.sum(mixed * grad, -1, keepdims=True))
            grad = grad * (sig * (1.0 + u * (1.0 - sig)))
            pad[base : base + rows, :] = grad
            own = idc_ref[base : base + rows, :]
            sums[0] = sums[0] + jnp.sum(grad * proj_ref[base : base + rows, cols], 0, keepdims=True)
            for j in range(1, 4):
                prior = idc_ref[base - j : base - j + rows, :]
                sums[j] = sums[j] + jnp.sum(
                    jnp.where(prior == own, proj_ref[base - j : base - j + rows, cols], 0.0) * grad, 0, keepdims=True
                )
        for j in range(4):
            spot = 2 + (part * 4 + j) * 2 + hh
            spread[spot : spot + 1, :] = sums[j]
        for start, size in [(0, HALO)] + [(HALO + c * rows, rows) for c in range(chunks)]:
            own = idc_ref[start : start + size, :]
            acc = pad[start : start + size, :] * taps[0]
            for j in range(1, 4):
                later = idc_ref[start + j : start + j + size, :]
                acc = acc + jnp.where(later == own, pad[start + j : start + j + size, :], 0.0) * taps[j]
            if start == 0:
                first_ref[:, cols] = jnp.concatenate([acc, jnp.zeros((HALO, 128), f32)], 0).astype(bf16)
            else:
                gp_ref[start - HALO : start - HALO + size, cols] = acc.astype(bf16)
    first_ref[:, 768:896] = jnp.zeros((2 * HALO, 128), bf16)

    @pl.when(step == 0)
    def _():
        spread[0:2, :] = jnp.zeros((2, 128), f32)
        spread[26:128, :] = jnp.zeros((102, 128), f32)
        extra[...] = jnp.zeros(extra.shape, f32)

    pad[0:128, :] = jnp.transpose(spread[...])
    part, lanes = 1024 // n_seq, 128 // n_seq
    for i in range(n_seq):
        if n_seq == 8:
            piece = pad[pl.ds(pl.multiple_of(table_ref[i] * lanes, lanes), lanes), :]
        else:
            piece = pad[i * lanes : (i + 1) * lanes, :]
        extra[i * part : i * part + lanes, :] = piece
    grads, edge = gp_ref[...], first_ref[...]

    def back(pieces, fresh):
        weights = jnp.concatenate([w[...] for w in pieces], 0)
        if fresh:
            gn_ref[...] = nt(grads, weights)
            gh_ref[...] = nt(edge, weights)
        else:
            gn_ref[...] += nt(grads, weights)
            gh_ref[...] += nt(edge, weights)

    @pl.when(step == 0)
    def _():
        if last:
            gn_ref[...] = gn_in[...]
            gh_ref[...] = gh_in[...]
        back(first_w, not last)

    @pl.when(step == 1)
    def _():
        back(second_w, False)

    half = own_ref.shape[0]
    for target, into in ((own_ref, slice(0, half)), (other_ref, slice(half, 2 * half))):
        total = nn(turned_ref[into, :], grads) + tn(edge_ref[:, into], edge)
        target[:, 0:768] = total[:, :768].astype(bf16)
        target[:, 768:896] = (total[:, 768:] + extra[into, :]).astype(bf16)

    if not last:
        for i, target in enumerate((own_ref, other_ref)):
            target[:, 896:1152] = outs_w[i][...]
            target[:, 1152:1408] = outs_w[2 + i][...]

    if last:

        @pl.when(step == 1)
        def _():
            for i in range(8):
                here = pl.ds(pl.multiple_of(table_ref[i] * 128, 128), 128)
                in_ref[:, here] = gn_ref[:, i * 128 : (i + 1) * 128]
                hin_ref[:, here] = gh_ref[0:HALO, i * 128 : (i + 1) * 128]

            def through(x, normed_grad):
                r1 = lax.rsqrt(jnp.mean(x * x, -1, keepdims=True) + epsilon)
                scaled = gain_ref[...] * normed_grad
                moved = r1 * scaled - x * ((r1 * r1 * r1) * jnp.mean(x * scaled, -1, keepdims=True))
                return moved, jnp.sum(normed_grad * x * r1, 0, keepdims=True)

            moved, sums_one = through(x_ref[...].astype(f32), in_ref[...])
            in_ref[...] = gres_ref[...] + moved
            moved, sums_two = through(halo_ref[...], hin_ref[...])
            hin_ref[...] = moved
            gone_ref[...] = jnp.broadcast_to(sums_one + sums_two, gone_ref.shape)


def core_first(n_seq):
    return [2 if i % 2 == 0 else 4 for i in range(n_seq)], [4 if i % 2 == 0 else 2 for i in range(n_seq)]


def seq_permute(array, steps):
    return lax.ppermute(array, "seq", [(i, i ^ k) for i, k in enumerate(steps)])


def ring(array, by=1):
    count = lax.axis_size("head")
    return lax.ppermute(array, "head", [(i, (i + by) % count) for i in range(count)])


def slot_table(s, n_seq):
    if n_seq != 8:
        return jnp.arange(8, dtype=jnp.int32)
    odd = s & 1
    f = jnp.where(odd == 0, 2, 4)
    g = 6 - f
    masks = jnp.stack([0 * f, f, g, 0 * f + 6, 0 * f + 1, 1 ^ g, 1 ^ f, 0 * f + 7])
    return (s ^ masks).astype(jnp.int32)


def gather_plane(pieces, n_seq):
    if n_seq != 8:
        full = lax.all_gather(pieces, "seq", axis=1, tiled=True)
        quarter = full.shape[1] // 4
        return [full[:, i * quarter : (i + 1) * quarter] for i in range(4)]
    near, wide = core_first(n_seq)
    pair = jnp.concatenate([pieces, seq_permute(pieces, near)], 1)
    pair_two = seq_permute(pair, wide)
    swap = [1] * n_seq
    return [pair, pair_two, seq_permute(pair, swap), seq_permute(pair_two, swap)]


def plus(a, b):
    return (a.astype(f32) + b.astype(f32)).astype(bf16)


def tie(value, *others):
    return lax.optimization_barrier((value,) + others)[0]


def after_core(own, got):
    return plus(own[:, own.shape[1] // 2 :], got[:, own.shape[1] // 2 :])


def after_wide(own, got, more):
    quarter = own.shape[1] // 4
    at = slice(quarter, 2 * quarter)
    return (own[:, at].astype(f32) + got[:, at].astype(f32) + more[:, quarter:].astype(f32)).astype(bf16)


def after_near(own, got, more, last):
    quarter = own.shape[1] // 4
    total = own[:, :quarter].astype(f32) + got[:, :quarter].astype(f32) + more[:, :quarter].astype(f32)
    return (total + last.astype(f32)).astype(bf16)


def reduce_whole(own, other):
    return lax.psum_scatter(jnp.concatenate([own, other], 1), "seq", scatter_dimension=1, tiled=True)


def reduce_ring(parts):
    groups = len(parts)
    moving = parts[1]
    for k in range(2, groups + 1):
        moving = ring(moving).astype(f32) + parts[k % groups].astype(f32)
        if k < groups:
            moving = moving.astype(bf16)
    return moving


def apply(a, x):
    return jnp.einsum("hij,hjk->hik", a.astype(bf16), x.astype(bf16), preferred_element_type=f32)


def pull(a, g):
    return jnp.einsum("hij,hik->hjk", a.astype(bf16), g.astype(bf16), preferred_element_type=f32)


def to_groups(slots, z):
    groups = len(slots)
    arrived = jnp.stack([slots[0]] + [ring(slots[k], -k) for k in range(1, groups)])
    return lax.dynamic_slice_in_dim(jnp.concatenate([arrived, arrived], 0), (groups - z) % groups, groups, 0)


def from_groups(blocks, z):
    groups = len(blocks)
    stacked = jnp.stack(blocks)
    turned = lax.dynamic_slice_in_dim(jnp.concatenate([stacked, stacked], 0), z, groups, 0)
    return jnp.stack([turned[0]] + [ring(turned[k], k) for k in range(1, groups)])


def exchange_forward(tot, n_seq, s, z, beside):
    groups = len(tot)
    got = tie(to_groups(tot, z), beside)

    def after(second, first):
        moved = apply(second[..., :128], first)
        return jnp.concatenate([moved[..., :128], moved[..., 128:] + second[..., 128:].astype(f32)], -1)

    whole = got[0].astype(f32)
    for j in range(1, groups):
        whole = after(got[j], whole)
    eye = jnp.broadcast_to(jnp.eye(128, dtype=f32), (2, 128, 128))
    prefix = jnp.concatenate([eye, jnp.zeros((2, 128, 128), f32)], -1)
    suffix = eye
    kept = []
    k = 1
    while k < n_seq:
        mine = whole.astype(bf16)
        other = lax.ppermute(mine, "seq", [(i, i ^ k) for i in range(n_seq)])
        upper = (s & k) != 0
        first = jnp.where(upper, other, mine)
        second = jnp.where(upper, mine, other)
        kept.append((first[..., :128], suffix.astype(bf16)))
        prefix = jnp.where(upper, after(prefix, other), prefix)
        suffix = jnp.where(upper, suffix, apply(other[..., :128], suffix))
        whole = after(second, first)
        k *= 2
    state = prefix[..., 128:]
    states = [state.astype(bf16)]
    for j in range(groups - 1):
        state = apply(got[j][..., :128], state) + got[j][..., 128:].astype(f32)
        states.append(state.astype(bf16))
    return from_groups(states, z), got, kept


def exchange_backward(local, got, kept, n_seq, s, z, beside):
    groups = len(local)
    grads = tie(to_groups(local, z), *beside)
    whole = grads[groups - 1].astype(f32)
    for j in range(groups - 2, -1, -1):
        whole = pull(got[j][..., :128], whole) + grads[j].astype(f32)
    later = jnp.zeros_like(whole)
    k = 1
    for first_a, suffix in kept:
        mine = whole.astype(bf16)
        other = lax.ppermute(mine, "seq", [(i, i ^ k) for i in range(n_seq)])
        upper = (s & k) != 0
        later = jnp.where(upper, later, pull(suffix, other) + later)
        first = jnp.where(upper, other, mine)
        second = jnp.where(upper, mine, other)
        whole = pull(first_a, second) + first.astype(f32)
        k *= 2
    outs = [later.astype(bf16)]
    for j in range(groups - 1, 0, -1):
        later = pull(got[j][..., :128], later) + grads[j].astype(f32)
        outs.append(later.astype(bf16))
    return from_groups(outs[::-1], z), outs[0]


def gain_steps(n_seq, n_head):
    if n_seq == 8:
        near, wide = core_first(n_seq)
        steps = [("seq", [1] * n_seq), ("seq", wide), ("seq", near)]
    else:
        steps = [("seq", [1 << i] * n_seq) for i in range(n_seq.bit_length() - 1)]
    return [("head", [1 << i] * n_head) for i in range(n_head.bit_length() - 1)] + steps


def swap_add(array, step):
    axis, partner = step
    return array + lax.ppermute(array, axis, [(i, i ^ k) for i, k in enumerate(partner)])


def local(
    inputs, norm1_gain, w_query, w_key, w_value, w_beta, conv_weight, head_gain, w_out, norm2_gain, w_gate, w_up, w_down,
    seq_ids, cotangent,
):
    n_seq, n_head = lax.axis_size("seq"), lax.axis_size("head")
    s, z = lax.axis_index("seq"), lax.axis_index("head")
    rows, width = inputs.shape
    ff = w_gate.shape[1]
    chunks = rows // CHUNK
    ext = rows + HALO
    count = n_seq * n_head
    part = width // n_seq
    quarter = width // 4
    table = slot_table(s, n_seq)
    smem = pl.BlockSpec(memory_space=pltpu.SMEM)

    before = lax.ppermute(inputs[-HALO:], WHOLE, [(i, i + 1) for i in range(count - 1)])
    ids_before = lax.ppermute(seq_ids[-HALO:], "seq", [(i, i + 1) for i in range(n_seq - 1)])
    taps = conv_weight.reshape(24, 128).T
    high = lax.reduce_precision(taps, 8, 7)
    middle = lax.reduce_precision(taps - high, 8, 7)
    coded = jnp.stack([high, middle, taps - high - middle], -1).reshape(128, 72).astype(bf16)
    coded = jnp.tile(coded, (width // 128, 1))
    more = jnp.concatenate([w_beta, coded, jnp.zeros((width, 54), bf16)], 1)

    def by_row(columns):
        return pl.BlockSpec((128, columns), lambda i, table: (table[i], 0))

    def by_column(size):
        return pl.BlockSpec((size, 128), lambda i, table: (0, table[i]))

    columns = 3 * FFP + 256

    def packed_proj(blocks, name):
        return pl.pallas_call(
            pack_proj_kernel,
            grid_spec=pltpu.PrefetchScalarGridSpec(
                num_scalar_prefetch=1,
                grid=(blocks,),
                in_specs=[by_row(256)] * 3 + [by_row(128)],
                out_specs=pl.BlockSpec((128, 896), lambda i, table: (i, 0)),
            ),
            out_shape=sds((blocks * 128, 896), bf16),
            compiler_params=params(),
            cost_estimate=cost(0.8 * blocks),
            name=name,
        )(table, w_query, w_key, w_value, more)

    proj_local = packed_proj(8, "pack_proj")
    if n_seq == 8:
        own_proj = packed_proj(1, "pack_proj_own")
        own_ffn = pl.pallas_call(
            pack_ffn_kernel,
            grid_spec=pltpu.PrefetchScalarGridSpec(
                num_scalar_prefetch=1,
                grid=(1,),
                in_specs=[by_column(ff), by_column(ff), by_column(ff), by_column(256)],
                out_specs=pl.BlockSpec((128, columns), lambda i, table: (i, 0)),
                scratch_shapes=[pltpu.VMEM((FFP, 128), f32)],
            ),
            out_shape=sds((128, columns), bf16),
            compiler_params=params(),
            cost_estimate=cost(2),
            name="pack_ffn",
        )(table, w_gate.T, w_up.T, w_down, w_out)
    else:
        own_proj = lax.dynamic_slice_in_dim(proj_local, s * part, part, 0)

        def padded(array):
            return jnp.pad(array, ((0, 0), (0, FFP - ff)))

        whole_ffn = jnp.concatenate([padded(w_gate), padded(w_up), padded(w_down.T), w_out.T], 1)
        own_ffn = lax.dynamic_slice_in_dim(whole_ffn, s * part, part, 0)
    ffn_all = lax.all_gather(own_ffn, BY_HEAD, axis=0, tiled=True).reshape(n_head, width, columns)
    ring_pieces = [own_proj]
    for _ in range(n_head - 1):
        ring_pieces.append(ring(ring_pieces[-1]))
    proj_one = gather_plane(ring_pieces[1][None], n_seq)
    proj_far = gather_plane(jnp.stack(ring_pieces[2:]), n_seq)

    ids_before = jnp.where(s == 0, -1, ids_before)
    ids = lax.dynamic_slice_in_dim(jnp.concatenate([ids_before, seq_ids]), z * rows, ext)
    ids_pad = jnp.concatenate([ids, jnp.full((HALO,), -2, jnp.int32)])
    idc = jnp.broadcast_to(ids_pad[:, None], (ext + HALO, 128))
    idr = jnp.broadcast_to(ids[None, :], (8, ext))
    halo = before.astype(f32)
    normed_ext, turned = pl.pallas_call(
        prep_kernel,
        grid=(1,),
        in_specs=[smem, same(HALO, width), same(rows, width), same(1, width)],
        out_specs=[same(ext, width), same(width, rows)],
        out_shape=[sds((ext, width), bf16), sds((width, rows), bf16)],
        scratch_shapes=[pltpu.VMEM((ext, width), f32)],
        compiler_params=params(),
        cost_estimate=cost(5),
        name="prep",
    )(table, halo, inputs, norm1_gain[None])

    idc_spec, idr_spec = same(ext + HALO, 128), same(8, ext)
    hidden_spec = pl.BlockSpec(memory_space=pl.ANY)
    shapes = [
        ((ext, 768), f32), ((rows, 128), f32), ((24, 128), f32), ((rows, 768), bf16), ((rows, 768), f32), ((2, rows, 256), bf16),
        ((2, rows, 128), bf16), ((2, chunks, 128, 256), bf16),
    ]

    def shifted(by, *shape):
        zeros = (0,) * len(shape)
        return pl.BlockSpec((None,) + shape, lambda i: (i + by,) + zeros)

    def local_pieces(columns, at=0):
        return [pl.BlockSpec((quarter, columns), lambda k, i=i: (i, at)) for i in range(4)]

    first = pl.pallas_call(
        functools.partial(front_kernel, chunks, 0),
        grid=(1,),
        in_specs=[same(ext, width)] + local_pieces(896) + [idc_spec, idr_spec],
        out_specs=[lead(*shape) for shape, _ in shapes] + [lead(2, 128, 256)],
        out_shape=[sds((n_head,) + shape, kind) for shape, kind in shapes] + [sds((1, 2, 128, 256), bf16)],
        compiler_params=params(),
        cost_estimate=cost(9),
        name="front_near",
    )(normed_ext, *[proj_local] * 4, idc, idr)
    def front_more(pieces, by, before_it, name):
        size = pieces[0].shape[0]
        return pl.pallas_call(
            functools.partial(front_kernel, chunks, len(shapes)),
            grid=(size,),
            in_specs=[same(ext, width)] + [lead(quarter, 896)] * 4 + [idc_spec, idr_spec] + [hidden_spec] * len(shapes),
            out_specs=[shifted(by, *shape) for shape, _ in shapes] + [lead(2, 128, 256)],
            out_shape=[sds((n_head,) + shape, kind) for shape, kind in shapes] + [sds((size, 2, 128, 256), bf16)],
            input_output_aliases={7 + i: i for i in range(len(shapes))},
            compiler_params=params(),
            cost_estimate=cost(7 * size + 1),
            name=name,
        )(normed_ext, *pieces, idc, idr, *before_it[:-1])

    second = front_more(proj_one, 1, first, "front_one")
    filled = front_more(proj_far, 2, second, "front_far")
    projected, logits, taps_all, qkv, summed, uw, inverse, prefixes, totals = filled
    every_total = [first[-1][0], second[-1][0]] + [totals[k] for k in range(n_head - 2)]
    score, reach, base, far = pl.pallas_call(
        functools.partial(reach_kernel, chunks),
        grid=(n_head,),
        in_specs=[lead(rows, 768), lead(2, rows, 256), lead(2, chunks, 128, 256), idc_spec, idr_spec],
        out_specs=[lead(2, rows, 128)] * 4,
        out_shape=[sds((n_head, 2, rows, 128), kind) for kind in (bf16, bf16, f32, bf16)],
        compiler_params=params(),
        cost_estimate=cost(9),
        name="reach",
    )(qkv, uw, prefixes, idc, idr)
    state_in, got, kept = exchange_forward(every_total, n_seq, s, z, score)
    gain_rows = jnp.broadcast_to(head_gain[None, :], (8, 128))
    attended, head_out = pl.pallas_call(
        attend_kernel,
        grid=(n_head,),
        in_specs=[lead(2, rows, 128), lead(2, rows, 128), lead(2, 128, 128), same(8, 128), idc_spec],
        out_specs=[lead(2, rows, 128), pl.BlockSpec((rows, 256), lambda i: (0, i))],
        out_shape=[sds((n_head, 2, rows, 128), f32), sds((rows, n_head * 256), bf16)],
        compiler_params=params(),
        cost_estimate=cost(5),
        name="attend",
    )(base, far, state_in, gain_rows, idc)

    order = ((z - jnp.arange(n_head)) % n_head).astype(jnp.int32)

    def by_slot(columns, at):
        return pl.BlockSpec((None, width, columns), lambda k, order: (order[k], 0, at))

    def fixed(*shape):
        zeros = (0,) * len(shape)
        return pl.BlockSpec(shape, lambda k, *scalars: zeros)

    def led(*shape):
        zeros = (0,) * len(shape)
        return pl.BlockSpec((None,) + shape, lambda k, *scalars: (k,) + zeros)

    head_columns = pl.BlockSpec((rows, 256), lambda k, *scalars: (0, k))
    residual, normed_two = pl.pallas_call(
        functools.partial(mix_kernel, n_head),
        grid_spec=pltpu.PrefetchScalarGridSpec(
            num_scalar_prefetch=1,
            grid=(n_head,),
            in_specs=[head_columns, fixed(rows, width), fixed(1, width), by_slot(256, 3 * FFP // 256)],
            out_specs=[fixed(rows, width), fixed(rows, width)],
        ),
        out_shape=[sds((rows, width), f32), sds((rows, width), bf16)],
        compiler_params=params(),
        cost_estimate=cost(5),
        name="mix",
    )(order, head_out, inputs, norm2_gain[None], ffn_all)
    near, wide = core_first(n_seq)
    swap = [1] * n_seq

    def ffn_weight(at):
        return pl.BlockSpec((None, width, FFP), lambda k, table, order: (order[k], 0, at))

    ffn_grads = sds((n_head, width // 2, 3 * FFP), bf16)
    ffn_out, grad_two, *ffn_a = pl.pallas_call(
        functools.partial(ffn_kernel, 0),
        grid_spec=pltpu.PrefetchScalarGridSpec(
            num_scalar_prefetch=2,
            grid=(n_head,),
            in_specs=[fixed(rows, width), pl.BlockSpec((rows, width), lambda k, table, order: (order[0], 0))]
            + [ffn_weight(i) for i in range(3)],
            out_specs=[fixed(rows, width), fixed(rows, width)] + [led(width // 2, 3 * FFP)] * 2,
            scratch_shapes=[pltpu.VMEM((width, rows), bf16)] * 2,
        ),
        out_shape=[sds((rows, width), f32), sds((rows, width), f32), ffn_grads, ffn_grads],
        compiler_params=params(60),
        cost_estimate=cost(2),
        name="ffn",
    )(table, order, normed_two, cotangent, ffn_all, ffn_all, ffn_all)
    if n_seq == 8:
        ffn_a = [ffn_a[0], seq_permute(ffn_a[1], swap)]
        send_a = after_core(*ffn_a)

    output, grad_residual, grad_norm_two, out_own, out_other, datt, local_grad, gain_part = pl.pallas_call(
        turn_kernel,
        grid_spec=pltpu.PrefetchScalarGridSpec(
            num_scalar_prefetch=2,
            grid=(n_head,),
            in_specs=[
                fixed(rows, width), fixed(rows, width), fixed(rows, width),
                pl.BlockSpec((rows, width), lambda k, table, order: (order[0], 0)), fixed(1, width), head_columns,
                pl.BlockSpec((None, width, 256), lambda k, table, order: (order[k], 0, 3 * FFP // 256)), led(2, rows, 128),
                led(2, rows, 128), fixed(8, 128), fixed(ext + HALO, 128),
            ],
            out_specs=[
                fixed(rows, width), fixed(rows, width), fixed(8, width),
                led(width // 2, 256), led(width // 2, 256), led(2, rows, 128),
                led(2, 128, 128), led(8, 128),
            ],
            scratch_shapes=[pltpu.VMEM((rows, width), bf16), pltpu.VMEM((width, rows), bf16)],
        ),
        out_shape=[
            sds((rows, width), bf16), sds((rows, width), f32), sds((8, width), f32), sds((n_head, width // 2, 256), bf16),
            sds((n_head, width // 2, 256), bf16), sds((n_head, 2, rows, 128), bf16), sds((n_head, 2, 128, 128), bf16), sds((n_head, 8, 128), f32),
        ],
        compiler_params=params(),
        cost_estimate=cost(0.6),
        name="turn",
    )(
        table, order, ffn_out, grad_two, residual, cotangent, norm2_gain[None], head_out, ffn_all, attended, far, gain_rows, idc,
    )
    grad_out_state, reached = exchange_backward(
        [local_grad[k] for k in range(n_head)], got, kept, n_seq, s, z, [send_a] if n_seq == 8 else []
    )
    if n_seq == 8:
        more_a = seq_permute(tie(send_a, reached), wide)
    inner_shapes = [((2, chunks, 128, 128), bf16)] + [((2, rows, 128), kind) for kind in (bf16, f32, f32, f32)]
    states, pseudo, dq, dk, dp = pl.pallas_call(
        functools.partial(inner_back_kernel, chunks, 0),
        grid=(n_head,),
        in_specs=[
            lead(rows, 768), lead(2, rows, 256), lead(2, chunks, 128, 256), lead(2, rows, 128), lead(2, rows, 128),
            lead(2, 128, 128), idc_spec, idr_spec,
        ],
        out_specs=[lead(*shape) for shape, _ in inner_shapes],
        out_shape=[sds((n_head,) + shape, kind) for shape, kind in inner_shapes],
        compiler_params=params(),
        cost_estimate=cost(1),
        name="inner_back",
    )(qkv, uw, prefixes, score, datt, state_in, idc, idr)
    def tail(slot, pieces, before_it, name):
        last = bool(before_it)
        size = 896 if last else 1408
        grad_size = sds((2, width // 2, size), bf16)

        def at(*shape):
            zeros = (0,) * len(shape)
            return pl.BlockSpec((None,) + shape, lambda i: (slot(i),) + zeros)

        sums = [same(rows, width), same(2 * HALO, width)]
        sum_shapes = [sds((rows, width), f32), sds((2 * HALO, width), f32)]
        given = [out_own, out_other, out_own, out_other]
        given_specs = [pl.BlockSpec((None, width // 2, 256), lambda i: (i + 1, 0, 0))] * 2
        given_specs += [pl.BlockSpec((None, width // 2, 256), lambda i: (3 - 3 * i, 0, 0))] * 2
        outs, out_specs = sum_shapes, sums
        if last:
            given = [*before_it, inputs, halo, norm1_gain[None], grad_residual]
            given_specs = sums + [same(rows, width), same(HALO, width), same(1, width), same(rows, width)]
            outs = [sds((rows, width), f32), sds((HALO, width), f32), sds((8, width), f32)]
            out_specs = [same(rows, width), same(HALO, width), same(8, width)]
        return pl.pallas_call(
            functools.partial(tail_kernel, chunks, n_seq, last),
            grid=(2,),
            in_specs=[
                smem, at(rows, 768), at(2, rows, 256), at(2, rows, 128), at(2, rows, 128), at(2, rows, 128),
                at(2, chunks, 128, 128), at(2, rows, 128), at(2, rows, 128), at(2, rows, 128), at(2, rows, 128),
                at(rows, 768), at(ext, 768), at(rows, 128), at(2, 128, 128), at(24, 128), idc_spec, idr_spec,
                same(width, rows), same(2 * HALO, width),
            ]
            + [spec for spec, _ in pieces]
            + given_specs,
            out_specs=out_specs + [lead(width // 2, size)] * 2,
            out_shape=outs + [grad_size] * 2,
            scratch_shapes=[
                pltpu.VMEM((rows, 896), bf16), pltpu.VMEM((2 * HALO, 896), bf16), pltpu.VMEM((rows, 768), f32),
                pltpu.VMEM((rows + 2 * HALO, 128), f32), pltpu.VMEM((128, 128), f32), pltpu.VMEM((width, 128), f32),
            ]
            + ([pltpu.VMEM((rows, width), f32), pltpu.VMEM((2 * HALO, width), f32)] if last else []),
            compiler_params=params(60),
            cost_estimate=cost(1),
            name=name,
        )(
            table, qkv, uw, inverse, reach, datt, states, pseudo, dq, dk, dp, summed, projected, logits, grad_out_state, taps_all, idc,
            idr, turned, normed_ext, *[piece for _, piece in pieces], *given,
        )

    def picked(arrays, k):
        return [(pl.BlockSpec((None, quarter, 896), lambda i: (k, 0, 0)), array) for array in arrays]

    here = list(zip(local_pieces(896), [proj_local] * 4))
    *partial, one_own, one_other = tail(lambda i: i + 1, picked(proj_one, 0) + picked(proj_far, 0), [], "tail_one")
    if n_seq == 8:
        one_got = seq_permute(one_other, swap)
        one_send = after_core(one_own, one_got)
        next_a = after_wide(*ffn_a, more_a)
        partial[0] = tie(partial[0], next_a, one_send)
        last_a = seq_permute(next_a, near)
        one_more = seq_permute(one_send, wide)
    inputs_grad, halo_grad, grad_norm_one, two_own, two_other = tail(
        lambda i: 3 - 3 * i, picked(proj_far, 1) + here, partial, "tail_two"
    )
    from_next = lax.ppermute(halo_grad, WHOLE, [(i + 1, i) for i in range(count - 1)])
    gains = jnp.concatenate([grad_norm_one[0], grad_norm_two[0], jnp.sum(gain_part[:, 0], 0)]).reshape(-1, 128)
    steps = gain_steps(n_seq, n_head)
    if n_seq == 8:
        two_got = seq_permute(two_other, swap)
        gains = swap_add(gains, steps[0])
        sum_a = after_near(*ffn_a, more_a, last_a)
        gains = swap_add(tie(gains, sum_a), steps[1])
        moved = ring(tie(sum_a[1], gains))
        two_send = after_core(two_own, tie(two_got, sum_a))
        two_more = seq_permute(two_send, wide)
        one_send = after_wide(one_own, one_got, tie(one_more, two_other, gains))
        one_last = seq_permute(one_send, near)
        moved = ring(plus(moved, sum_a[2]))
        two_send = after_wide(two_own, two_got, two_more)
        two_last = seq_permute(two_send, near)
        one_sum = after_near(one_own, one_got, one_more, tie(one_last, sum_a))
        gains = tie(gains, two_send)
        two_sum = after_near(two_own, two_got, two_more, two_last)
        for step in steps[2:]:
            gains = swap_add(gains, step)
        from_next = tie(from_next, two_sum)
        sum_ffn = ring(plus(moved, sum_a[3])).astype(f32) + sum_a[0].astype(f32)
    else:
        one_sum, two_sum, sum_a = (reduce_whole(*pair) for pair in ((one_own, one_other), (two_own, two_other), ffn_a))
        for step in steps:
            gains = swap_add(gains, step)
        sum_ffn = reduce_ring([sum_a[k] for k in range(n_head)])
    third = jnp.concatenate([two_sum[0], one_sum[0, :, 1152:]], 1)
    fourth = jnp.concatenate([two_sum[1], one_sum[1, :, 1152:]], 1)
    sum_proj = reduce_ring([fourth, one_sum[0, :, :1152], one_sum[1, :, :1152], third])
    inputs_grad = inputs_grad.at[rows - HALO :].add(from_next)
    lanes = 128 // n_seq
    gains = gains.reshape(-1)
    return (
        output, inputs_grad, gains[:width], sum_proj[:, :256], sum_proj[:, 256:512], sum_proj[:, 512:768], sum_proj[:, 768:770],
        sum_proj[:lanes, 770:794].T.reshape(3, 4, 2, lanes), gains[2 * width :], sum_proj[:, 896:].T, gains[width : 2 * width],
        sum_ffn[:, :ff], sum_ffn[:, FFP : FFP + ff], sum_ffn[:, 2 * FFP : 2 * FFP + ff].T,
    )


def solution(mesh):
    return jax.shard_map(
        local,
        mesh=mesh,
        in_specs=(
            P(("seq", "head"), None),
            P(),
            P(None, "head"),
            P(None, "head"),
            P(None, "head"),
            P(None, "head"),
            P(None, None, "head", None),
            P(),
            P("head", None),
            P(),
            P(None, "head"),
            P(None, "head"),
            P("head", None),
            P("seq"),
            P("seq", None),
        ),
        out_specs=(
            P(("seq", "head"), None),
            P(("seq", "head"), None),
            P(),
            P("seq", "head"),
            P("seq", "head"),
            P("seq", "head"),
            P("seq", "head"),
            P(None, None, "head", "seq"),
            P(),
            P("head", "seq"),
            P(),
            P("seq", "head"),
            P("seq", "head"),
            P("head", "seq"),
        ),
        check_vma=False,
    )
```

```python
import functools

import jax
import jax.numpy as jnp
from jax import lax
from jax.experimental import pallas as pl
from jax.experimental.pallas import tpu as pltpu
from jax.sharding import PartitionSpec as P

SEQS = 4
CHUNK = 128
HALO = 8
FFP = 768
PAIR = 1408
epsilon = 1e-06
beta_shift = 4.0
f32 = jnp.float32
bf16 = jnp.bfloat16
WHOLE = ("seq", "head")
BY_HEAD = ("head", "seq")


def nn(a, b):
    return lax.dot_general(a, b, (((1,), (0,)), ((), ())), preferred_element_type=f32)


def nt(a, b):
    return lax.dot_general(a, b, (((1,), (1,)), ((), ())), preferred_element_type=f32)


def tn(a, b):
    return lax.dot_general(a, b, (((0,), (0,)), ((), ())), preferred_element_type=f32)


def params(mib=56, grid=1):
    return pltpu.CompilerParams(
        vmem_limit_bytes=mib << 20, dimension_semantics=("arbitrary",) * grid
    )


def lead(*shape):
    zeros = (0,) * len(shape)
    return pl.BlockSpec((None,) + shape, lambda i: (i,) + zeros)


def same(*shape):
    zeros = (0,) * len(shape)
    return pl.BlockSpec(shape, lambda i: zeros)


def cost(us):
    return pl.CostEstimate(flops=int(us * 1.1e9), bytes_accessed=int(us * 1e6), transcendentals=0)


def sds(shape, kind):
    return jax.ShapeDtypeStruct(shape, kind)


def pack_proj_kernel(table_ref, q_ref, k_ref, v_ref, more_ref, out_ref):
    out_ref[:, 0:256] = q_ref[...]
    out_ref[:, 256:512] = k_ref[...]
    out_ref[:, 512:768] = v_ref[...]
    out_ref[:, 768:896] = more_ref[...]


def pack_ffn_kernel(table_ref, gate_ref, up_ref, down_ref, out_w_ref, out_ref, tall):
    ff = gate_ref.shape[0]
    out_ref[:, 0:256] = jnp.transpose(out_w_ref[...].astype(f32)).astype(bf16)
    tall[0:ff, :] = gate_ref[...].astype(f32)
    tall[ff : 2 * ff, :] = up_ref[...].astype(f32)
    out_ref[:, 256 : 256 + PAIR] = jnp.transpose(tall[...]).astype(bf16)
    tall[0:ff, :] = down_ref[...].astype(f32)
    tall[ff:FFP, :] = jnp.zeros((FFP - ff, 128), f32)
    out_ref[:, 256 + PAIR : 256 + PAIR + FFP] = jnp.transpose(tall[0:FFP, :]).astype(bf16)


def prep_kernel(table_ref, halo_ref, x_ref, gain_ref, normed_ref, turned_ref, wide):
    rows = x_ref.shape[0]
    wide[0:HALO, :] = halo_ref[...]
    wide[HALO : HALO + rows, :] = x_ref[...].astype(f32)
    full = wide[...]
    wide[...] = full * lax.rsqrt(jnp.mean(full * full, -1, keepdims=True) + epsilon) * gain_ref[...]
    for i in range(8):
        at = slice(i * 128, (i + 1) * 128)
        here = pl.ds(pl.multiple_of(table_ref[i] * 128, 128), 128)
        block = wide[:, here]
        normed_ref[:, at] = block.astype(bf16)
        turned_ref[at, :] = jnp.transpose(block[HALO:, :]).astype(bf16)


def mix_kernel(groups, order_ref, head_ref, x_ref, gain_ref, weight_ref, res_ref, normed_ref):
    step = pl.program_id(0)
    part = nt(head_ref[...], weight_ref[...])

    @pl.when(step == 0)
    def _():
        res_ref[...] = x_ref[...].astype(f32) + part

    @pl.when(step > 0)
    def _():
        res_ref[...] += part

    @pl.when(step == groups - 1)
    def _():
        full = res_ref[...]
        normed = full * lax.rsqrt(jnp.mean(full * full, -1, keepdims=True) + epsilon) * gain_ref[...]
        normed_ref[...] = normed.astype(bf16)


def turn_kernel(
    table_ref, order_ref, ffn_ref, two_ref, res_ref, dy_ref, gain_two_ref, head_ref, weight_ref, att_ref, far_ref, gain_ref, idc_ref,
    out_ref, gres_ref, gtwo_ref, own_ref, other_ref, datt_ref, local_grad_ref, gain_grad_ref, mixer, turned,
):
    step = pl.program_id(0)
    rows = att_ref.shape[1]

    @pl.when(step == 0)
    def _():
        res = res_ref[...]
        two = two_ref[...]
        r2 = lax.rsqrt(jnp.mean(res * res, -1, keepdims=True) + epsilon)
        scaled = gain_two_ref[...] * two
        grad = dy_ref[...].astype(f32) + r2 * scaled - res * ((r2 * r2 * r2) * jnp.mean(res * scaled, -1, keepdims=True))
        gres_ref[...] = grad
        mixer[...] = grad.astype(bf16)
        for i in range(8):
            here = pl.ds(pl.multiple_of(table_ref[i] * 128, 128), 128)
            turned[i * 128 : (i + 1) * 128, :] = jnp.transpose(gres_ref[:, here]).astype(bf16)
        gtwo_ref[...] = jnp.broadcast_to(jnp.sum(two * res * r2, 0, keepdims=True), gtwo_ref.shape)
        out_ref[...] = (res + ffn_ref[...]).astype(bf16)

    gho = nn(mixer[...], weight_ref[...])
    mask = (idc_ref[HALO : HALO + rows, :] < SEQS).astype(f32)
    gain = gain_ref[0:1, :]
    total = jnp.zeros((1, 128), f32)
    for hh in range(2):
        out = att_ref[hh]
        go = gho[:, hh * 128 : (hh + 1) * 128] * mask
        rh = lax.rsqrt(jnp.mean(out * out, -1, keepdims=True) + epsilon)
        total = total + jnp.sum(go * out * rh, 0, keepdims=True)
        inner = jnp.mean(out * gain * go, -1, keepdims=True)
        grad = (rh * gain * go - out * (rh * rh * rh) * inner).astype(bf16)
        datt_ref[hh] = grad
        local_grad_ref[hh] = tn(far_ref[hh], grad).astype(bf16)
    gain_grad_ref[...] = jnp.broadcast_to(total, (8, 128))
    half = own_ref.shape[0]
    own_ref[...] = nn(turned[0:half, :], head_ref[...]).astype(bf16)
    other_ref[...] = nn(turned[half : 2 * half, :], head_ref[...]).astype(bf16)


def chunk_masks(idc_ref, idr_ref, c):
    base = HALO + c * CHUNK
    own = idc_ref[base : base + CHUNK, :]
    row = idr_ref[0:1, base : base + CHUNK]
    prev = idc_ref[base - 1 : base, :]
    last = idc_ref[base + CHUNK - 1 : base + CHUNK, :]
    equal = own == row
    carry = (own == prev).astype(f32)
    to_last = (own == last).astype(f32)
    carry_last = (last == prev).astype(f32)
    return equal, carry, to_last, carry_last


def positions():
    row = lax.broadcasted_iota(jnp.int32, (CHUNK, CHUNK), 0)
    col = lax.broadcasted_iota(jnp.int32, (CHUNK, CHUNK), 1)
    return row, col


def front_kernel(chunks, skip, normed_ref, w0, w1, w2, w3, idc_ref, idr_ref, *rest):
    proj_ref, lgt_ref, cw_ref, qkv_ref, sum_ref, uw_ref, inv_ref, pre_ref, tot_ref = rest[skip:]
    rows = CHUNK
    quarter = w0.shape[0]
    wide = nn(normed_ref[:, 0:quarter], w0[...])
    for i, w in enumerate((w1, w2, w3)):
        wide = wide + nn(normed_ref[:, (i + 1) * quarter : (i + 2) * quarter], w[...])
    proj_ref[...] = wide[:, :768]
    lgt_ref[...] = wide[HALO:, 768:896]
    turned = jnp.transpose(w0[0:128, 768:896].astype(f32))
    for j in range(24):
        cw_ref[j : j + 1, :] = turned[2 + 3 * j : 3 + 3 * j] + turned[3 + 3 * j : 4 + 3 * j] + turned[4 + 3 * j : 5 + 3 * j]
    for b in range(6):
        part, hh = b // 2, b % 2
        cols = slice(b * 128, (b + 1) * 128)
        taps = [cw_ref[(part * 4 + j) * 2 + hh : (part * 4 + j) * 2 + hh + 1, :] for j in range(4)]
        for c in range(chunks):
            base = HALO + c * rows
            own = idc_ref[base : base + rows, :]
            acc = proj_ref[base : base + rows, cols] * taps[0]
            for j in range(1, 4):
                prior = idc_ref[base - j : base - j + rows, :]
                acc = acc + jnp.where(prior == own, proj_ref[base - j : base - j + rows, cols], 0.0) * taps[j]
            sum_ref[c * rows : (c + 1) * rows, cols] = acc
            mixed = acc / (1.0 + jnp.exp(-acc))
            if part < 2:
                mixed = mixed * lax.rsqrt(jnp.sum(mixed * mixed, -1, keepdims=True) + epsilon)
            qkv_ref[c * rows : (c + 1) * rows, cols] = mixed.astype(bf16)
    row, col = positions()
    differ = row ^ col
    strict = row > col
    units = [(hh, c) for c in range(chunks) for hh in range(2)]
    lower, inv, scaled = {}, {}, {}
    for hh, c in units:
        equal, carry, _, _ = chunk_masks(idc_ref, idr_ref, c)
        at = slice(c * CHUNK, (c + 1) * CHUNK)
        beta = jax.nn.sigmoid(jnp.broadcast_to(lgt_ref[at, hh : hh + 1], (CHUNK, 128)) - beta_shift)
        beta = jnp.where(idc_ref[HALO + c * CHUNK : HALO + (c + 1) * CHUNK, :] < SEQS, beta, 0.0)
        keys = qkv_ref[at, 256 + hh * 128 : 256 + (hh + 1) * 128]
        values = qkv_ref[at, 512 + hh * 128 : 512 + (hh + 1) * 128]
        low = jnp.where(equal & strict, nt(keys, keys), 0.0) * beta
        lower[hh, c] = low
        inv[hh, c] = jnp.where(row == col, 1.0, 0.0) - jnp.where(differ == 1, low, 0.0)
        scaled[hh, c] = jnp.concatenate(
            [(values.astype(f32) * beta).astype(bf16), (keys.astype(f32) * (beta * carry)).astype(bf16)], axis=1
        )
    for k in range(1, 7):
        level = (differ >> k) == 1
        for u in units:
            off = jnp.where(level, lower[u], 0.0).astype(bf16)
            half = inv[u].astype(bf16)
            inv[u] = inv[u] - nn(half, nn(off, half).astype(bf16))
    for hh, c in units:
        at = slice(c * CHUNK, (c + 1) * CHUNK)
        half = inv[hh, c].astype(bf16)
        inv_ref[hh, at, :] = half
        uw_ref[hh, at, :] = nn(half, scaled[hh, c]).astype(bf16)
    eye = jnp.where(row == col, 1.0, 0.0)
    state = [[eye, jnp.zeros((CHUNK, CHUNK), f32)] for _ in range(2)]
    for c in range(chunks):
        at = slice(c * CHUNK, (c + 1) * CHUNK)
        _, _, to_last, carry_last = chunk_masks(idc_ref, idr_ref, c)
        for hh in range(2):
            packed = jnp.concatenate([state[hh][0].astype(bf16), state[hh][1].astype(bf16)], axis=1)
            pre_ref[hh, c] = packed
            moved = nn(uw_ref[hh, at, 128:256], packed)
            change = jnp.concatenate(
                [(-moved[:, :128]).astype(bf16), (uw_ref[hh, at, 0:128].astype(f32) - moved[:, 128:]).astype(bf16)], axis=1
            )
            keys = qkv_ref[at, 256 + hh * 128 : 256 + (hh + 1) * 128]
            kept = (keys.astype(f32) * to_last).astype(bf16)
            step = tn(kept, change)
            state[hh] = [state[hh][0] * carry_last + step[:, :128], state[hh][1] * carry_last + step[:, 128:]]
    for hh in range(2):
        tot_ref[hh] = jnp.concatenate([state[hh][0].astype(bf16), state[hh][1].astype(bf16)], axis=1)


def reach_kernel(chunks, qkv_ref, uw_ref, pre_ref, idc_ref, idr_ref, score_ref, reach_ref, base_ref, far_ref):
    row, col = positions()
    causal = row >= col
    for c in range(chunks):
        at = slice(c * CHUNK, (c + 1) * CHUNK)
        equal, carry, _, _ = chunk_masks(idc_ref, idr_ref, c)
        for hh in range(2):
            queries = qkv_ref[at, hh * 128 : (hh + 1) * 128]
            keys = qkv_ref[at, 256 + hh * 128 : 256 + (hh + 1) * 128]
            score = jnp.where(causal & equal, nt(queries, keys), 0.0).astype(bf16)
            score_ref[hh, at, :] = score
            both = nn(score, uw_ref[hh, at, :])
            reach = (queries.astype(f32) * carry - both[:, 128:]).astype(bf16)
            reach_ref[hh, at, :] = reach
            far = nn(reach, pre_ref[hh, c])
            far_ref[hh, at, :] = far[:, :128].astype(bf16)
            base_ref[hh, at, :] = both[:, :128] + far[:, 128:]


def attend_kernel(base_ref, far_ref, state_ref, gain_ref, idc_ref, out_ref, head_ref):
    rows = base_ref.shape[1]
    mask = (idc_ref[HALO : HALO + rows, :] < SEQS).astype(f32)
    for hh in range(2):
        out = base_ref[hh] + nn(far_ref[hh], state_ref[hh])
        out_ref[hh] = out
        rh = lax.rsqrt(jnp.mean(out * out, -1, keepdims=True) + epsilon)
        head_ref[:, hh * 128 : (hh + 1) * 128] = (out * rh * gain_ref[0:1, :] * mask).astype(bf16)


def ffn_kernel(later, table_ref, order_ref, normed_ref, dy_ref, weight_ref, *rest):
    given, (out_ref, grad_ref, own_ref, other_ref, nturned, dturned) = rest[:later], rest[later:]
    step = pl.program_id(0)
    span = FFP

    @pl.when(step == 0)
    def _():
        for i in range(8):
            at = slice(i * 128, (i + 1) * 128)
            here = pl.ds(pl.multiple_of(table_ref[i] * 128, 128), 128)
            nturned[at, :] = jnp.transpose(normed_ref[:, here].astype(f32)).astype(bf16)
            dturned[at, :] = jnp.transpose(dy_ref[:, here].astype(f32)).astype(bf16)

    pair_w, down_w = weight_ref[:, 256 : 256 + PAIR], weight_ref[:, 256 + PAIR : 256 + PAIR + span]
    ff = PAIR // 2
    pair = nn(normed_ref[...], pair_w)
    inside = lax.broadcasted_iota(jnp.int32, (pair.shape[0], span), 1) < ff
    gate = jnp.where(inside, pair[:, 0:span], 0.0)
    up = jnp.where(inside, pltpu.roll(pair[:, PAIR - span :], ff, 1), 0.0)
    sig = 1.0 / (1.0 + jnp.exp(-gate))
    act = gate * sig
    hidden = (act * up).astype(bf16)
    grad_hidden = nn(dy_ref[...], down_w)
    grad_gate = grad_hidden * up * (sig * (1.0 + gate * (1.0 - sig)))
    grad_up = pltpu.roll(grad_hidden * act, span - ff, 1)
    joint = PAIR - span
    grad_pair = jnp.concatenate(
        [grad_gate[:, :joint], grad_gate[:, joint:] + grad_up[:, : span - joint], grad_up[:, span - joint :]], 1
    ).astype(bf16)
    out = nt(hidden, down_w)
    back = nt(grad_pair, pair_w)

    @pl.when(step == 0)
    def _():
        out_ref[...] = given[0][...] + out if later else out
        grad_ref[...] = given[1][...] + back if later else back

    @pl.when(step > 0)
    def _():
        out_ref[...] += out
        grad_ref[...] += back

    half = own_ref.shape[0]
    for target, into in ((own_ref, slice(0, half)), (other_ref, slice(half, 2 * half))):
        target[:, 0:PAIR] = nn(nturned[into, :], grad_pair).astype(bf16)
        target[:, PAIR : PAIR + span] = nn(dturned[into, :], hidden).astype(bf16)


def inner_back_kernel(chunks, skip, qkv_ref, uw_ref, pre_ref, score_ref, datt_ref, state_ref, idc_ref, idr_ref, *rest):
    states_ref, pseudo_ref, dq_ref, dk_ref, dp_ref = rest[skip:]
    row, col = positions()
    causal = row >= col
    for c in range(chunks):
        at = slice(c * CHUNK, (c + 1) * CHUNK)
        equal, carry, _, _ = chunk_masks(idc_ref, idr_ref, c)
        for hh in range(2):
            queries = qkv_ref[at, hh * 128 : (hh + 1) * 128]
            keys = qkv_ref[at, 256 + hh * 128 : 256 + (hh + 1) * 128]
            grad = datt_ref[hh, at, :]
            state = (nn(pre_ref[hh, c, :, 0:128], state_ref[hh]) + pre_ref[hh, c, :, 128:256].astype(f32)).astype(bf16)
            states_ref[hh, c] = state
            pseudo = (uw_ref[hh, at, 0:128].astype(f32) - nn(uw_ref[hh, at, 128:256], state)).astype(bf16)
            pseudo_ref[hh, at, :] = pseudo
            both = nt(grad, jnp.concatenate([pseudo, state], 0))
            grad_score = jnp.where(causal & equal, both[:, :CHUNK], 0.0).astype(bf16)
            dq_ref[hh, at, :] = both[:, CHUNK:] * carry + nn(grad_score, keys)
            dk_ref[hh, at, :] = tn(grad_score, queries)
            dp_ref[hh, at, :] = tn(score_ref[hh, at, :], grad)


def tail_kernel(
    chunks, n_seq, last, table_ref, qkv_ref, uw_ref, inv_ref, reach_ref, datt_ref, states_ref, pseudo_ref, dq_ref, dk_ref, dp_ref,
    sum_ref, proj_ref, lgt_ref, gout_ref, cw_ref, idc_ref, idr_ref,
    turned_ref, edge_ref, *rest,
):
    first_w, second_w, rest = rest[:4], rest[4:8], rest[8:]
    if last:
        gn_in, gh_in, x_ref, halo_ref, gain_ref, gres_ref = rest[:6]
        in_ref, hin_ref, gone_ref, own_ref, other_ref, gp_ref, first_ref, dqkv, pad, spread, extra, gn_ref, gh_ref = rest[6:]
    else:
        outs_w, (gn_ref, gh_ref, own_ref, other_ref, gp_ref, first_ref, dqkv, pad, spread, extra) = rest[:4], rest[4:]
    step = pl.program_id(0)
    row, col = positions()
    strict = row > col
    lane = lax.broadcasted_iota(jnp.int32, (CHUNK, 128), 1)
    grad_state = [gout_ref[hh].astype(f32) for hh in range(2)]
    for c in range(chunks - 1, -1, -1):
        at = slice(c * CHUNK, (c + 1) * CHUNK)
        equal, carry, to_last, carry_last = chunk_masks(idc_ref, idr_ref, c)
        own = idc_ref[HALO + c * CHUNK : HALO + (c + 1) * CHUNK, :]
        dlgt = jnp.zeros((CHUNK, 128), f32)
        for hh in range(2):
            keys = qkv_ref[at, 256 + hh * 128 : 256 + (hh + 1) * 128]
            keys_f = keys.astype(f32)
            values = qkv_ref[at, 512 + hh * 128 : 512 + (hh + 1) * 128]
            kept = (keys_f * to_last).astype(bf16)
            packed = grad_state[hh].astype(bf16)
            push = nn(kept, packed)
            grad_state[hh] = grad_state[hh] * carry_last + tn(reach_ref[hh, at, :], datt_ref[hh, at, :]) - tn(
                uw_ref[hh, at, 128:256], push.astype(bf16)
            )
            full = (dp_ref[hh, at, :] + push).astype(bf16)
            solved = tn(inv_ref[hh, at, :], full)
            solved_h = solved.astype(bf16)
            pseudo = pseudo_ref[hh, at, :]
            gate = jax.nn.sigmoid(jnp.broadcast_to(lgt_ref[at, hh : hh + 1], (CHUNK, 128)) - beta_shift)
            mask = (own < SEQS).astype(f32)
            beta = gate * mask
            back = nt(solved_h, states_ref[hh, c]) * carry
            outer = jnp.where(equal & strict, nt(solved_h, pseudo), 0.0)
            overlap = nt(keys, keys)
            rate = jnp.sum(solved * values.astype(f32) - back * keys_f - outer * overlap, -1, keepdims=True)
            dlgt = jnp.where(lane == hh, rate * mask * gate * (1.0 - gate), dlgt)
            mixed = (outer * beta).astype(bf16)
            dqkv[at, 256 + hh * 128 : 256 + (hh + 1) * 128] = (
                dk_ref[hh, at, :] + nt(pseudo, packed) * to_last - beta * back - nn(mixed, keys) - tn(mixed, keys)
            )
            dqkv[at, 512 + hh * 128 : 512 + (hh + 1) * 128] = beta * solved
            dqkv[at, hh * 128 : (hh + 1) * 128] = dq_ref[hh, at, :]
        gp_ref[at, 768:896] = dlgt.astype(bf16)
    rows = CHUNK
    length = chunks * CHUNK
    for b in range(6):
        part, hh = b // 2, b % 2
        cols = slice(b * 128, (b + 1) * 128)
        taps = [cw_ref[(part * 4 + j) * 2 + hh : (part * 4 + j) * 2 + hh + 1, :] for j in range(4)]
        pad[0:HALO, :] = jnp.zeros((HALO, 128), f32)
        pad[HALO + length : 2 * HALO + length, :] = jnp.zeros((HALO, 128), f32)
        sums = [jnp.zeros((1, 128), f32) for _ in range(4)]
        for c in range(chunks):
            at = slice(c * rows, (c + 1) * rows)
            base = HALO + c * rows
            u = sum_ref[at, cols]
            sig = 1.0 / (1.0 + jnp.exp(-u))
            grad = dqkv[at, cols]
            if part < 2:
                mixed = u * sig
                r = lax.rsqrt(jnp.sum(mixed * mixed, -1, keepdims=True) + epsilon)
                grad = r * grad - mixed * ((r * r * r) * jnp.sum(mixed * grad, -1, keepdims=True))
            grad = grad * (sig * (1.0 + u * (1.0 - sig)))
            pad[base : base + rows, :] = grad
            own = idc_ref[base : base + rows, :]
            sums[0] = sums[0] + jnp.sum(grad * proj_ref[base : base + rows, cols], 0, keepdims=True)
            for j in range(1, 4):
                prior = idc_ref[base - j : base - j + rows, :]
                sums[j] = sums[j] + jnp.sum(
                    jnp.where(prior == own, proj_ref[base - j : base - j + rows, cols], 0.0) * grad, 0, keepdims=True
                )
        for j in range(4):
            spot = 2 + (part * 4 + j) * 2 + hh
            spread[spot : spot + 1, :] = sums[j]
        for start, size in [(0, HALO)] + [(HALO + c * rows, rows) for c in range(chunks)]:
            own = idc_ref[start : start + size, :]
            acc = pad[start : start + size, :] * taps[0]
            for j in range(1, 4):
                later = idc_ref[start + j : start + j + size, :]
                acc = acc + jnp.where(later == own, pad[start + j : start + j + size, :], 0.0) * taps[j]
            if start == 0:
                first_ref[:, cols] = jnp.concatenate([acc, jnp.zeros((HALO, 128), f32)], 0).astype(bf16)
            else:
                gp_ref[start - HALO : start - HALO + size, cols] = acc.astype(bf16)
    first_ref[:, 768:896] = jnp.zeros((2 * HALO, 128), bf16)

    @pl.when(step == 0)
    def _():
        spread[0:2, :] = jnp.zeros((2, 128), f32)
        spread[26:128, :] = jnp.zeros((102, 128), f32)
        extra[...] = jnp.zeros(extra.shape, f32)

    pad[0:128, :] = jnp.transpose(spread[...])
    part, lanes = 1024 // n_seq, 128 // n_seq
    for i in range(n_seq):
        if n_seq == 8:
            piece = pad[pl.ds(pl.multiple_of(table_ref[i] * lanes, lanes), lanes), :]
        else:
            piece = pad[i * lanes : (i + 1) * lanes, :]
        extra[i * part : i * part + lanes, :] = piece
    grads, edge = gp_ref[...], first_ref[...]

    def back(pieces, fresh):
        weights = jnp.concatenate([w[...] for w in pieces], 0)
        if fresh:
            gn_ref[...] = nt(grads, weights)
            gh_ref[...] = nt(edge, weights)
        else:
            gn_ref[...] += nt(grads, weights)
            gh_ref[...] += nt(edge, weights)

    @pl.when(step == 0)
    def _():
        if last:
            gn_ref[...] = gn_in[...]
            gh_ref[...] = gh_in[...]
        back(first_w, not last)

    @pl.when(step == 1)
    def _():
        back(second_w, False)

    half = own_ref.shape[0]
    for target, into in ((own_ref, slice(0, half)), (other_ref, slice(half, 2 * half))):
        total = nn(turned_ref[into, :], grads) + tn(edge_ref[:, into], edge)
        target[:, 0:768] = total[:, :768].astype(bf16)
        target[:, 768:896] = (total[:, 768:] + extra[into, :]).astype(bf16)

    if not last:
        for i, target in enumerate((own_ref, other_ref)):
            target[:, 896:1152] = outs_w[i][...]
            target[:, 1152:1408] = outs_w[2 + i][...]

    if last:

        @pl.when(step == 1)
        def _():
            for i in range(8):
                here = pl.ds(pl.multiple_of(table_ref[i] * 128, 128), 128)
                in_ref[:, here] = gn_ref[:, i * 128 : (i + 1) * 128]
                hin_ref[:, here] = gh_ref[0:HALO, i * 128 : (i + 1) * 128]

            def through(x, normed_grad):
                r1 = lax.rsqrt(jnp.mean(x * x, -1, keepdims=True) + epsilon)
                scaled = gain_ref[...] * normed_grad
                moved = r1 * scaled - x * ((r1 * r1 * r1) * jnp.mean(x * scaled, -1, keepdims=True))
                return moved, jnp.sum(normed_grad * x * r1, 0, keepdims=True)

            moved, sums_one = through(x_ref[...].astype(f32), in_ref[...])
            in_ref[...] = gres_ref[...] + moved
            moved, sums_two = through(halo_ref[...], hin_ref[...])
            hin_ref[...] = moved
            gone_ref[...] = jnp.broadcast_to(sums_one + sums_two, gone_ref.shape)


def core_first(n_seq):
    return [2 if i % 2 == 0 else 4 for i in range(n_seq)], [4 if i % 2 == 0 else 2 for i in range(n_seq)]


def seq_permute(array, steps):
    return lax.ppermute(array, "seq", [(i, i ^ k) for i, k in enumerate(steps)])


def ring(array, by=1):
    count = lax.axis_size("head")
    return lax.ppermute(array, "head", [(i, (i + by) % count) for i in range(count)])


def slot_table(s, n_seq):
    if n_seq != 8:
        return jnp.arange(8, dtype=jnp.int32)
    odd = s & 1
    f = jnp.where(odd == 0, 2, 4)
    g = 6 - f
    masks = jnp.stack([0 * f, f, g, 0 * f + 6, 0 * f + 1, 1 ^ g, 1 ^ f, 0 * f + 7])
    return (s ^ masks).astype(jnp.int32)


def gather_plane(pieces, n_seq):
    if n_seq != 8:
        full = lax.all_gather(pieces, "seq", axis=1, tiled=True)
        quarter = full.shape[1] // 4
        return [full[:, i * quarter : (i + 1) * quarter] for i in range(4)]
    near, wide = core_first(n_seq)
    pair = jnp.concatenate([pieces, seq_permute(pieces, near)], 1)
    pair_two = seq_permute(pair, wide)
    swap = [1] * n_seq
    return [pair, pair_two, seq_permute(pair, swap), seq_permute(pair_two, swap)]


def plus(a, b):
    return (a.astype(f32) + b.astype(f32)).astype(bf16)


def tie(value, *others):
    return lax.optimization_barrier((value,) + others)[0]


def after_core(own, got):
    return plus(own[:, own.shape[1] // 2 :], got[:, own.shape[1] // 2 :])


def after_wide(own, got, more):
    quarter = own.shape[1] // 4
    at = slice(quarter, 2 * quarter)
    return (own[:, at].astype(f32) + got[:, at].astype(f32) + more[:, quarter:].astype(f32)).astype(bf16)


def after_near(own, got, more, last):
    quarter = own.shape[1] // 4
    total = own[:, :quarter].astype(f32) + got[:, :quarter].astype(f32) + more[:, :quarter].astype(f32)
    return (total + last.astype(f32)).astype(bf16)


def reduce_whole(own, other):
    return lax.psum_scatter(jnp.concatenate([own, other], 1), "seq", scatter_dimension=1, tiled=True)


def reduce_ring(parts):
    groups = len(parts)
    moving = parts[1]
    for k in range(2, groups + 1):
        moving = ring(moving).astype(f32) + parts[k % groups].astype(f32)
        if k < groups:
            moving = moving.astype(bf16)
    return moving


def apply(a, x):
    return jnp.einsum("hij,hjk->hik", a.astype(bf16), x.astype(bf16), preferred_element_type=f32)


def pull(a, g):
    return jnp.einsum("hij,hik->hjk", a.astype(bf16), g.astype(bf16), preferred_element_type=f32)


def to_groups(slots, z):
    groups = len(slots)
    arrived = jnp.stack([slots[0]] + [ring(slots[k], -k) for k in range(1, groups)])
    return lax.dynamic_slice_in_dim(jnp.concatenate([arrived, arrived], 0), (groups - z) % groups, groups, 0)


def from_groups(blocks, z):
    groups = len(blocks)
    stacked = jnp.stack(blocks)
    turned = lax.dynamic_slice_in_dim(jnp.concatenate([stacked, stacked], 0), z, groups, 0)
    return jnp.stack([turned[0]] + [ring(turned[k], k) for k in range(1, groups)])


def exchange_forward(tot, n_seq, s, z, beside):
    groups = len(tot)
    got = tie(to_groups(tot, z), beside)

    def after(second, first):
        moved = apply(second[..., :128], first)
        return jnp.concatenate([moved[..., :128], moved[..., 128:] + second[..., 128:].astype(f32)], -1)

    whole = got[0].astype(f32)
    for j in range(1, groups):
        whole = after(got[j], whole)
    eye = jnp.broadcast_to(jnp.eye(128, dtype=f32), (2, 128, 128))
    prefix = jnp.concatenate([eye, jnp.zeros((2, 128, 128), f32)], -1)
    suffix = eye
    kept = []
    k = 1
    while k < n_seq:
        mine = whole.astype(bf16)
        other = lax.ppermute(mine, "seq", [(i, i ^ k) for i in range(n_seq)])
        upper = (s & k) != 0
        first = jnp.where(upper, other, mine)
        second = jnp.where(upper, mine, other)
        kept.append((first[..., :128], suffix.astype(bf16)))
        prefix = jnp.where(upper, after(prefix, other), prefix)
        suffix = jnp.where(upper, suffix, apply(other[..., :128], suffix))
        whole = after(second, first)
        k *= 2
    state = prefix[..., 128:]
    states = [state.astype(bf16)]
    for j in range(groups - 1):
        state = apply(got[j][..., :128], state) + got[j][..., 128:].astype(f32)
        states.append(state.astype(bf16))
    return from_groups(states, z), got, kept


def exchange_backward(local, got, kept, n_seq, s, z, beside):
    groups = len(local)
    grads = tie(to_groups(local, z), *beside)
    whole = grads[groups - 1].astype(f32)
    for j in range(groups - 2, -1, -1):
        whole = pull(got[j][..., :128], whole) + grads[j].astype(f32)
    later = jnp.zeros_like(whole)
    k = 1
    for first_a, suffix in kept:
        mine = whole.astype(bf16)
        other = lax.ppermute(mine, "seq", [(i, i ^ k) for i in range(n_seq)])
        upper = (s & k) != 0
        later = jnp.where(upper, later, pull(suffix, other) + later)
        first = jnp.where(upper, other, mine)
        second = jnp.where(upper, mine, other)
        whole = pull(first_a, second) + first.astype(f32)
        k *= 2
    outs = [later.astype(bf16)]
    for j in range(groups - 1, 0, -1):
        later = pull(got[j][..., :128], later) + grads[j].astype(f32)
        outs.append(later.astype(bf16))
    return from_groups(outs[::-1], z), outs[0]


def gain_steps(n_seq, n_head):
    if n_seq == 8:
        near, wide = core_first(n_seq)
        steps = [("seq", [1] * n_seq), ("seq", wide), ("seq", near)]
    else:
        steps = [("seq", [1 << i] * n_seq) for i in range(n_seq.bit_length() - 1)]
    return [("head", [1 << i] * n_head) for i in range(n_head.bit_length() - 1)] + steps


def swap_add(array, step):
    axis, partner = step
    return array + lax.ppermute(array, axis, [(i, i ^ k) for i, k in enumerate(partner)])


def local(
    inputs, norm1_gain, w_query, w_key, w_value, w_beta, conv_weight, head_gain, w_out, norm2_gain, w_gate, w_up, w_down,
    seq_ids, cotangent,
):
    n_seq, n_head = lax.axis_size("seq"), lax.axis_size("head")
    s, z = lax.axis_index("seq"), lax.axis_index("head")
    rows, width = inputs.shape
    ff = w_gate.shape[1]
    chunks = rows // CHUNK
    ext = rows + HALO
    count = n_seq * n_head
    part = width // n_seq
    quarter = width // 4
    table = slot_table(s, n_seq)
    smem = pl.BlockSpec(memory_space=pltpu.SMEM)

    before = lax.ppermute(inputs[-HALO:], WHOLE, [(i, i + 1) for i in range(count - 1)])
    ids_before = lax.ppermute(seq_ids[-HALO:], "seq", [(i, i + 1) for i in range(n_seq - 1)])
    taps = conv_weight.reshape(24, 128).T
    high = lax.reduce_precision(taps, 8, 7)
    middle = lax.reduce_precision(taps - high, 8, 7)
    coded = jnp.stack([high, middle, taps - high - middle], -1).reshape(128, 72).astype(bf16)
    coded = jnp.tile(coded, (width // 128, 1))
    more = jnp.concatenate([w_beta, coded, jnp.zeros((width, 54), bf16)], 1)

    def by_row(columns):
        return pl.BlockSpec((128, columns), lambda i, table: (table[i], 0))

    def by_column(size):
        return pl.BlockSpec((size, 128), lambda i, table: (0, table[i]))

    columns = 256 + PAIR + FFP

    def packed_proj(blocks, name):
        return pl.pallas_call(
            pack_proj_kernel,
            grid_spec=pltpu.PrefetchScalarGridSpec(
                num_scalar_prefetch=1,
                grid=(blocks,),
                in_specs=[by_row(256)] * 3 + [by_row(128)],
                out_specs=pl.BlockSpec((128, 896), lambda i, table: (i, 0)),
            ),
            out_shape=sds((blocks * 128, 896), bf16),
            compiler_params=params(),
            cost_estimate=cost(0.8 * blocks),
            name=name,
        )(table, w_query, w_key, w_value, more)

    proj_local = packed_proj(8, "pack_proj")
    if n_seq == 8:
        own_proj = packed_proj(1, "pack_proj_own")
        own_ffn = pl.pallas_call(
            pack_ffn_kernel,
            grid_spec=pltpu.PrefetchScalarGridSpec(
                num_scalar_prefetch=1,
                grid=(1,),
                in_specs=[by_column(ff), by_column(ff), by_column(ff), by_column(256)],
                out_specs=pl.BlockSpec((128, columns), lambda i, table: (i, 0)),
                scratch_shapes=[pltpu.VMEM((PAIR, 128), f32)],
            ),
            out_shape=sds((128, columns), bf16),
            compiler_params=params(),
            cost_estimate=cost(2),
            name="pack_ffn",
        )(table, w_gate.T, w_up.T, w_down, w_out)
    else:
        own_proj = lax.dynamic_slice_in_dim(proj_local, s * part, part, 0)

        down = jnp.pad(w_down.T, ((0, 0), (0, FFP - ff)))
        whole_ffn = jnp.concatenate([w_out.T, w_gate, w_up, down], 1)
        own_ffn = lax.dynamic_slice_in_dim(whole_ffn, s * part, part, 0)
    ffn_all = lax.all_gather(own_ffn, BY_HEAD, axis=0, tiled=True).reshape(n_head, width, columns)
    ring_pieces = [own_proj]
    for _ in range(n_head - 1):
        ring_pieces.append(ring(ring_pieces[-1]))
    proj_one = gather_plane(ring_pieces[1][None], n_seq)
    proj_far = gather_plane(jnp.stack(ring_pieces[2:]), n_seq)

    ids_before = jnp.where(s == 0, -1, ids_before)
    ids = lax.dynamic_slice_in_dim(jnp.concatenate([ids_before, seq_ids]), z * rows, ext)
    ids_pad = jnp.concatenate([ids, jnp.full((HALO,), -2, jnp.int32)])
    idc = jnp.broadcast_to(ids_pad[:, None], (ext + HALO, 128))
    idr = jnp.broadcast_to(ids[None, :], (8, ext))
    halo = before.astype(f32)
    normed_ext, turned = pl.pallas_call(
        prep_kernel,
        grid=(1,),
        in_specs=[smem, same(HALO, width), same(rows, width), same(1, width)],
        out_specs=[same(ext, width), same(width, rows)],
        out_shape=[sds((ext, width), bf16), sds((width, rows), bf16)],
        scratch_shapes=[pltpu.VMEM((ext, width), f32)],
        compiler_params=params(),
        cost_estimate=cost(5),
        name="prep",
    )(table, halo, inputs, norm1_gain[None])

    idc_spec, idr_spec = same(ext + HALO, 128), same(8, ext)
    hidden_spec = pl.BlockSpec(memory_space=pl.ANY)
    shapes = [
        ((ext, 768), f32), ((rows, 128), f32), ((24, 128), f32), ((rows, 768), bf16), ((rows, 768), f32), ((2, rows, 256), bf16),
        ((2, rows, 128), bf16), ((2, chunks, 128, 256), bf16),
    ]

    def shifted(by, *shape):
        zeros = (0,) * len(shape)
        return pl.BlockSpec((None,) + shape, lambda i: (i + by,) + zeros)

    def local_pieces(columns, at=0):
        return [pl.BlockSpec((quarter, columns), lambda k, i=i: (i, at)) for i in range(4)]

    first = pl.pallas_call(
        functools.partial(front_kernel, chunks, 0),
        grid=(1,),
        in_specs=[same(ext, width)] + local_pieces(896) + [idc_spec, idr_spec],
        out_specs=[lead(*shape) for shape, _ in shapes] + [lead(2, 128, 256)],
        out_shape=[sds((n_head,) + shape, kind) for shape, kind in shapes] + [sds((1, 2, 128, 256), bf16)],
        compiler_params=params(),
        cost_estimate=cost(9),
        name="front_near",
    )(normed_ext, *[proj_local] * 4, idc, idr)
    def front_more(pieces, by, before_it, name):
        size = pieces[0].shape[0]
        return pl.pallas_call(
            functools.partial(front_kernel, chunks, len(shapes)),
            grid=(size,),
            in_specs=[same(ext, width)] + [lead(quarter, 896)] * 4 + [idc_spec, idr_spec] + [hidden_spec] * len(shapes),
            out_specs=[shifted(by, *shape) for shape, _ in shapes] + [lead(2, 128, 256)],
            out_shape=[sds((n_head,) + shape, kind) for shape, kind in shapes] + [sds((size, 2, 128, 256), bf16)],
            input_output_aliases={7 + i: i for i in range(len(shapes))},
            compiler_params=params(),
            cost_estimate=cost(7 * size + 1),
            name=name,
        )(normed_ext, *pieces, idc, idr, *before_it[:-1])

    second = front_more(proj_one, 1, first, "front_one")
    filled = front_more(proj_far, 2, second, "front_far")
    projected, logits, taps_all, qkv, summed, uw, inverse, prefixes, totals = filled
    every_total = [first[-1][0], second[-1][0]] + [totals[k] for k in range(n_head - 2)]
    score, reach, base, far = pl.pallas_call(
        functools.partial(reach_kernel, chunks),
        grid=(n_head,),
        in_specs=[lead(rows, 768), lead(2, rows, 256), lead(2, chunks, 128, 256), idc_spec, idr_spec],
        out_specs=[lead(2, rows, 128)] * 4,
        out_shape=[sds((n_head, 2, rows, 128), kind) for kind in (bf16, bf16, f32, bf16)],
        compiler_params=params(),
        cost_estimate=cost(9),
        name="reach",
    )(qkv, uw, prefixes, idc, idr)
    state_in, got, kept = exchange_forward(every_total, n_seq, s, z, score)
    gain_rows = jnp.broadcast_to(head_gain[None, :], (8, 128))
    attended, head_out = pl.pallas_call(
        attend_kernel,
        grid=(n_head,),
        in_specs=[lead(2, rows, 128), lead(2, rows, 128), lead(2, 128, 128), same(8, 128), idc_spec],
        out_specs=[lead(2, rows, 128), pl.BlockSpec((rows, 256), lambda i: (0, i))],
        out_shape=[sds((n_head, 2, rows, 128), f32), sds((rows, n_head * 256), bf16)],
        compiler_params=params(),
        cost_estimate=cost(5),
        name="attend",
    )(base, far, state_in, gain_rows, idc)

    order = ((z - jnp.arange(n_head)) % n_head).astype(jnp.int32)

    def by_slot(columns, at):
        return pl.BlockSpec((None, width, columns), lambda k, order: (order[k], 0, at))

    def fixed(*shape):
        zeros = (0,) * len(shape)
        return pl.BlockSpec(shape, lambda k, *scalars: zeros)

    def led(*shape):
        zeros = (0,) * len(shape)
        return pl.BlockSpec((None,) + shape, lambda k, *scalars: (k,) + zeros)

    head_columns = pl.BlockSpec((rows, 256), lambda k, *scalars: (0, k))
    residual, normed_two = pl.pallas_call(
        functools.partial(mix_kernel, n_head),
        grid_spec=pltpu.PrefetchScalarGridSpec(
            num_scalar_prefetch=1,
            grid=(n_head,),
            in_specs=[head_columns, fixed(rows, width), fixed(1, width), by_slot(256, 0)],
            out_specs=[fixed(rows, width), fixed(rows, width)],
        ),
        out_shape=[sds((rows, width), f32), sds((rows, width), bf16)],
        compiler_params=params(),
        cost_estimate=cost(5),
        name="mix",
    )(order, head_out, inputs, norm2_gain[None], ffn_all)
    near, wide = core_first(n_seq)
    swap = [1] * n_seq

    ffn_weights = pl.BlockSpec((None, width, columns), lambda k, table, order: (order[k], 0, 0))
    ffn_grads = sds((n_head, width // 2, PAIR + FFP), bf16)
    ffn_out, grad_two, *ffn_a = pl.pallas_call(
        functools.partial(ffn_kernel, 0),
        grid_spec=pltpu.PrefetchScalarGridSpec(
            num_scalar_prefetch=2,
            grid=(n_head,),
            in_specs=[fixed(rows, width), pl.BlockSpec((rows, width), lambda k, table, order: (order[0], 0))]
            + [ffn_weights],
            out_specs=[fixed(rows, width), fixed(rows, width)] + [led(width // 2, PAIR + FFP)] * 2,
            scratch_shapes=[pltpu.VMEM((width, rows), bf16)] * 2,
        ),
        out_shape=[sds((rows, width), f32), sds((rows, width), f32), ffn_grads, ffn_grads],
        compiler_params=params(60),
        cost_estimate=cost(2),
        name="ffn",
    )(table, order, normed_two, cotangent, ffn_all)
    if n_seq == 8:
        ffn_a = [ffn_a[0], seq_permute(ffn_a[1], swap)]
        send_a = after_core(*ffn_a)

    output, grad_residual, grad_norm_two, out_own, out_other, datt, local_grad, gain_part = pl.pallas_call(
        turn_kernel,
        grid_spec=pltpu.PrefetchScalarGridSpec(
            num_scalar_prefetch=2,
            grid=(n_head,),
            in_specs=[
                fixed(rows, width), fixed(rows, width), fixed(rows, width),
                pl.BlockSpec((rows, width), lambda k, table, order: (order[0], 0)), fixed(1, width), head_columns,
                pl.BlockSpec((None, width, 256), lambda k, table, order: (order[k], 0, 0)), led(2, rows, 128),
                led(2, rows, 128), fixed(8, 128), fixed(ext + HALO, 128),
            ],
            out_specs=[
                fixed(rows, width), fixed(rows, width), fixed(8, width),
                led(width // 2, 256), led(width // 2, 256), led(2, rows, 128),
                led(2, 128, 128), led(8, 128),
            ],
            scratch_shapes=[pltpu.VMEM((rows, width), bf16), pltpu.VMEM((width, rows), bf16)],
        ),
        out_shape=[
            sds((rows, width), bf16), sds((rows, width), f32), sds((8, width), f32), sds((n_head, width // 2, 256), bf16),
            sds((n_head, width // 2, 256), bf16), sds((n_head, 2, rows, 128), bf16), sds((n_head, 2, 128, 128), bf16), sds((n_head, 8, 128), f32),
        ],
        compiler_params=params(),
        cost_estimate=cost(0.6),
        name="turn",
    )(
        table, order, ffn_out, grad_two, residual, cotangent, norm2_gain[None], head_out, ffn_all, attended, far, gain_rows, idc,
    )
    grad_out_state, reached = exchange_backward(
        [local_grad[k] for k in range(n_head)], got, kept, n_seq, s, z, [send_a] if n_seq == 8 else []
    )
    if n_seq == 8:
        more_a = seq_permute(tie(send_a, reached), wide)
    inner_shapes = [((2, chunks, 128, 128), bf16)] + [((2, rows, 128), kind) for kind in (bf16, f32, f32, f32)]
    states, pseudo, dq, dk, dp = pl.pallas_call(
        functools.partial(inner_back_kernel, chunks, 0),
        grid=(n_head,),
        in_specs=[
            lead(rows, 768), lead(2, rows, 256), lead(2, chunks, 128, 256), lead(2, rows, 128), lead(2, rows, 128),
            lead(2, 128, 128), idc_spec, idr_spec,
        ],
        out_specs=[lead(*shape) for shape, _ in inner_shapes],
        out_shape=[sds((n_head,) + shape, kind) for shape, kind in inner_shapes],
        compiler_params=params(),
        cost_estimate=cost(1),
        name="inner_back",
    )(qkv, uw, prefixes, score, datt, state_in, idc, idr)
    def tail(slot, pieces, before_it, name):
        last = bool(before_it)
        size = 896 if last else 1408
        grad_size = sds((2, width // 2, size), bf16)

        def at(*shape):
            zeros = (0,) * len(shape)
            return pl.BlockSpec((None,) + shape, lambda i: (slot(i),) + zeros)

        sums = [same(rows, width), same(2 * HALO, width)]
        sum_shapes = [sds((rows, width), f32), sds((2 * HALO, width), f32)]
        given = [out_own, out_other, out_own, out_other]
        given_specs = [pl.BlockSpec((None, width // 2, 256), lambda i: (i + 1, 0, 0))] * 2
        given_specs += [pl.BlockSpec((None, width // 2, 256), lambda i: (3 - 3 * i, 0, 0))] * 2
        outs, out_specs = sum_shapes, sums
        if last:
            given = [*before_it, inputs, halo, norm1_gain[None], grad_residual]
            given_specs = sums + [same(rows, width), same(HALO, width), same(1, width), same(rows, width)]
            outs = [sds((rows, width), f32), sds((HALO, width), f32), sds((8, width), f32)]
            out_specs = [same(rows, width), same(HALO, width), same(8, width)]
        return pl.pallas_call(
            functools.partial(tail_kernel, chunks, n_seq, last),
            grid=(2,),
            in_specs=[
                smem, at(rows, 768), at(2, rows, 256), at(2, rows, 128), at(2, rows, 128), at(2, rows, 128),
                at(2, chunks, 128, 128), at(2, rows, 128), at(2, rows, 128), at(2, rows, 128), at(2, rows, 128),
                at(rows, 768), at(ext, 768), at(rows, 128), at(2, 128, 128), at(24, 128), idc_spec, idr_spec,
                same(width, rows), same(2 * HALO, width),
            ]
            + [spec for spec, _ in pieces]
            + given_specs,
            out_specs=out_specs + [lead(width // 2, size)] * 2,
            out_shape=outs + [grad_size] * 2,
            scratch_shapes=[
                pltpu.VMEM((rows, 896), bf16), pltpu.VMEM((2 * HALO, 896), bf16), pltpu.VMEM((rows, 768), f32),
                pltpu.VMEM((rows + 2 * HALO, 128), f32), pltpu.VMEM((128, 128), f32), pltpu.VMEM((width, 128), f32),
            ]
            + ([pltpu.VMEM((rows, width), f32), pltpu.VMEM((2 * HALO, width), f32)] if last else []),
            compiler_params=params(60),
            cost_estimate=cost(1),
            name=name,
        )(
            table, qkv, uw, inverse, reach, datt, states, pseudo, dq, dk, dp, summed, projected, logits, grad_out_state, taps_all, idc,
            idr, turned, normed_ext, *[piece for _, piece in pieces], *given,
        )

    def picked(arrays, k):
        return [(pl.BlockSpec((None, quarter, 896), lambda i: (k, 0, 0)), array) for array in arrays]

    here = list(zip(local_pieces(896), [proj_local] * 4))
    *partial, one_own, one_other = tail(lambda i: i + 1, picked(proj_one, 0) + picked(proj_far, 0), [], "tail_one")
    if n_seq == 8:
        one_got = seq_permute(one_other, swap)
        one_send = after_core(one_own, one_got)
        next_a = after_wide(*ffn_a, more_a)
        partial[0] = tie(partial[0], next_a, one_send)
        last_a = seq_permute(next_a, near)
        one_more = seq_permute(one_send, wide)
    inputs_grad, halo_grad, grad_norm_one, two_own, two_other = tail(
        lambda i: 3 - 3 * i, picked(proj_far, 1) + here, partial, "tail_two"
    )
    from_next = lax.ppermute(halo_grad, WHOLE, [(i + 1, i) for i in range(count - 1)])
    gains = jnp.concatenate([grad_norm_one[0], grad_norm_two[0], jnp.sum(gain_part[:, 0], 0)]).reshape(-1, 128)
    steps = gain_steps(n_seq, n_head)
    if n_seq == 8:
        two_got = seq_permute(two_other, swap)
        gains = swap_add(gains, steps[0])
        sum_a = after_near(*ffn_a, more_a, last_a)
        gains = swap_add(tie(gains, sum_a), steps[1])
        moved = ring(tie(sum_a[1], gains))
        two_send = after_core(two_own, tie(two_got, sum_a))
        two_more = seq_permute(two_send, wide)
        one_send = after_wide(one_own, one_got, tie(one_more, two_other, gains))
        one_last = seq_permute(one_send, near)
        moved = ring(plus(moved, sum_a[2]))
        two_send = after_wide(two_own, two_got, two_more)
        two_last = seq_permute(two_send, near)
        one_sum = after_near(one_own, one_got, one_more, tie(one_last, sum_a))
        gains = tie(gains, two_send)
        two_sum = after_near(two_own, two_got, two_more, two_last)
        for step in steps[2:]:
            gains = swap_add(gains, step)
        from_next = tie(from_next, two_sum)
        sum_ffn = ring(plus(moved, sum_a[3])).astype(f32) + sum_a[0].astype(f32)
    else:
        one_sum, two_sum, sum_a = (reduce_whole(*pair) for pair in ((one_own, one_other), (two_own, two_other), ffn_a))
        for step in steps:
            gains = swap_add(gains, step)
        sum_ffn = reduce_ring([sum_a[k] for k in range(n_head)])
    third = jnp.concatenate([two_sum[0], one_sum[0, :, 1152:]], 1)
    fourth = jnp.concatenate([two_sum[1], one_sum[1, :, 1152:]], 1)
    sum_proj = reduce_ring([fourth, one_sum[0, :, :1152], one_sum[1, :, :1152], third])
    inputs_grad = inputs_grad.at[rows - HALO :].add(from_next)
    lanes = 128 // n_seq
    gains = gains.reshape(-1)
    return (
        output, inputs_grad, gains[:width], sum_proj[:, :256], sum_proj[:, 256:512], sum_proj[:, 512:768], sum_proj[:, 768:770],
        sum_proj[:lanes, 770:794].T.reshape(3, 4, 2, lanes), gains[2 * width :], sum_proj[:, 896:].T, gains[width : 2 * width],
        sum_ffn[:, :ff], sum_ffn[:, ff : 2 * ff], sum_ffn[:, PAIR : PAIR + ff].T,
    )


def solution(mesh):
    return jax.shard_map(
        local,
        mesh=mesh,
        in_specs=(
            P(("seq", "head"), None),
            P(),
            P(None, "head"),
            P(None, "head"),
            P(None, "head"),
            P(None, "head"),
            P(None, None, "head", None),
            P(),
            P("head", None),
            P(),
            P(None, "head"),
            P(None, "head"),
            P("head", None),
            P("seq"),
            P("seq", None),
        ),
        out_specs=(
            P(("seq", "head"), None),
            P(("seq", "head"), None),
            P(),
            P("seq", "head"),
            P("seq", "head"),
            P("seq", "head"),
            P("seq", "head"),
            P(None, None, "head", "seq"),
            P(),
            P("head", "seq"),
            P(),
            P("seq", "head"),
            P("seq", "head"),
            P("head", "seq"),
        ),
        check_vma=False,
    )
```

```python
import functools

import jax
import jax.numpy as jnp
from jax import lax
from jax.experimental import pallas as pl
from jax.experimental.pallas import tpu as pltpu
from jax.sharding import PartitionSpec as P

SEQS = 4
CHUNK = 128
HALO = 8
FFP = 768
PAIR = 1408
epsilon = 1e-06
beta_shift = 4.0
f32 = jnp.float32
bf16 = jnp.bfloat16
WHOLE = ("seq", "head")
BY_HEAD = ("head", "seq")


def nn(a, b):
    return lax.dot_general(a, b, (((1,), (0,)), ((), ())), preferred_element_type=f32)


def nt(a, b):
    return lax.dot_general(a, b, (((1,), (1,)), ((), ())), preferred_element_type=f32)


def tn(a, b):
    return lax.dot_general(a, b, (((0,), (0,)), ((), ())), preferred_element_type=f32)


def params(mib=56, grid=1):
    return pltpu.CompilerParams(
        vmem_limit_bytes=mib << 20, dimension_semantics=("arbitrary",) * grid
    )


def lead(*shape):
    zeros = (0,) * len(shape)
    return pl.BlockSpec((None,) + shape, lambda i: (i,) + zeros)


def same(*shape):
    zeros = (0,) * len(shape)
    return pl.BlockSpec(shape, lambda i: zeros)


def cost(us):
    return pl.CostEstimate(flops=int(us * 1.1e9), bytes_accessed=int(us * 1e6), transcendentals=0)


def sds(shape, kind):
    return jax.ShapeDtypeStruct(shape, kind)


def pack_proj_kernel(table_ref, q_ref, k_ref, v_ref, more_ref, out_ref):
    out_ref[:, 0:256] = q_ref[...]
    out_ref[:, 256:512] = k_ref[...]
    out_ref[:, 512:768] = v_ref[...]
    out_ref[:, 768:896] = more_ref[...]


def pack_ffn_kernel(table_ref, gate_ref, up_ref, down_ref, out_w_ref, out_ref, tall):
    ff = gate_ref.shape[0]
    out_ref[:, 0:256] = jnp.transpose(out_w_ref[...].astype(f32)).astype(bf16)
    tall[0:ff, :] = gate_ref[...].astype(f32)
    tall[ff : 2 * ff, :] = up_ref[...].astype(f32)
    out_ref[:, 256 : 256 + PAIR] = jnp.transpose(tall[...]).astype(bf16)
    tall[0:ff, :] = down_ref[...].astype(f32)
    tall[ff:FFP, :] = jnp.zeros((FFP - ff, 128), f32)
    out_ref[:, 256 + PAIR : 256 + PAIR + FFP] = jnp.transpose(tall[0:FFP, :]).astype(bf16)


def prep_kernel(table_ref, halo_ref, x_ref, gain_ref, normed_ref, turned_ref, wide):
    rows = x_ref.shape[0]
    wide[0:HALO, :] = halo_ref[...]
    wide[HALO : HALO + rows, :] = x_ref[...].astype(f32)
    full = wide[...]
    wide[...] = full * lax.rsqrt(jnp.mean(full * full, -1, keepdims=True) + epsilon) * gain_ref[...]
    for i in range(8):
        at = slice(i * 128, (i + 1) * 128)
        here = pl.ds(pl.multiple_of(table_ref[i] * 128, 128), 128)
        block = wide[:, here]
        normed_ref[:, at] = block.astype(bf16)
        turned_ref[at, :] = jnp.transpose(block[HALO:, :]).astype(bf16)


def mix_kernel(groups, order_ref, head_ref, x_ref, gain_ref, weight_ref, res_ref, normed_ref):
    for i in range(4):
        at = slice(i * 256, (i + 1) * 256)
        weights = jnp.concatenate([weight_ref[order_ref[k], at, :] for k in range(groups)], 1)
        res_ref[:, at] = x_ref[:, at].astype(f32) + nt(head_ref[...], weights)
    full = res_ref[...]
    normed = full * lax.rsqrt(jnp.mean(full * full, -1, keepdims=True) + epsilon) * gain_ref[...]
    normed_ref[...] = normed.astype(bf16)


def turn_kernel(
    table_ref, order_ref, ffn_ref, two_ref, res_ref, dy_ref, gain_two_ref, head_ref, weight_ref, att_ref, far_ref, gain_ref, idc_ref,
    out_ref, gres_ref, gtwo_ref, own_ref, other_ref, datt_ref, local_grad_ref, gain_grad_ref, mixer, turned,
):
    step = pl.program_id(0)
    rows = att_ref.shape[1]

    @pl.when(step == 0)
    def _():
        res = res_ref[...]
        two = two_ref[...]
        r2 = lax.rsqrt(jnp.mean(res * res, -1, keepdims=True) + epsilon)
        scaled = gain_two_ref[...] * two
        grad = dy_ref[...].astype(f32) + r2 * scaled - res * ((r2 * r2 * r2) * jnp.mean(res * scaled, -1, keepdims=True))
        gres_ref[...] = grad
        mixer[...] = grad.astype(bf16)
        for i in range(8):
            here = pl.ds(pl.multiple_of(table_ref[i] * 128, 128), 128)
            turned[i * 128 : (i + 1) * 128, :] = jnp.transpose(gres_ref[:, here]).astype(bf16)
        gtwo_ref[...] = jnp.broadcast_to(jnp.sum(two * res * r2, 0, keepdims=True), gtwo_ref.shape)
        out_ref[...] = (res + ffn_ref[...]).astype(bf16)

    gho = nn(mixer[...], weight_ref[...])
    mask = (idc_ref[HALO : HALO + rows, :] < SEQS).astype(f32)
    gain = gain_ref[0:1, :]
    total = jnp.zeros((1, 128), f32)
    for hh in range(2):
        out = att_ref[hh]
        go = gho[:, hh * 128 : (hh + 1) * 128] * mask
        rh = lax.rsqrt(jnp.mean(out * out, -1, keepdims=True) + epsilon)
        total = total + jnp.sum(go * out * rh, 0, keepdims=True)
        inner = jnp.mean(out * gain * go, -1, keepdims=True)
        grad = (rh * gain * go - out * (rh * rh * rh) * inner).astype(bf16)
        datt_ref[hh] = grad
        local_grad_ref[hh] = tn(far_ref[hh], grad).astype(bf16)
    gain_grad_ref[...] = jnp.broadcast_to(total, (8, 128))
    half = own_ref.shape[0]
    own_ref[...] = nn(turned[0:half, :], head_ref[...]).astype(bf16)
    other_ref[...] = nn(turned[half : 2 * half, :], head_ref[...]).astype(bf16)


def chunk_masks(idc_ref, idr_ref, c):
    base = HALO + c * CHUNK
    own = idc_ref[base : base + CHUNK, :]
    row = idr_ref[0:1, base : base + CHUNK]
    prev = idc_ref[base - 1 : base, :]
    last = idc_ref[base + CHUNK - 1 : base + CHUNK, :]
    equal = own == row
    carry = (own == prev).astype(f32)
    to_last = (own == last).astype(f32)
    carry_last = (last == prev).astype(f32)
    return equal, carry, to_last, carry_last


def positions():
    row = lax.broadcasted_iota(jnp.int32, (CHUNK, CHUNK), 0)
    col = lax.broadcasted_iota(jnp.int32, (CHUNK, CHUNK), 1)
    return row, col


def front_kernel(chunks, skip, normed_ref, w0, w1, w2, w3, idc_ref, idr_ref, *rest):
    proj_ref, lgt_ref, cw_ref, qkv_ref, sum_ref, uw_ref, inv_ref, pre_ref, tot_ref = rest[skip:]
    rows = CHUNK
    quarter = w0.shape[0]
    wide = nn(normed_ref[:, 0:quarter], w0[...])
    for i, w in enumerate((w1, w2, w3)):
        wide = wide + nn(normed_ref[:, (i + 1) * quarter : (i + 2) * quarter], w[...])
    proj_ref[...] = wide[:, :768]
    lgt_ref[...] = wide[HALO:, 768:896]
    turned = jnp.transpose(w0[0:128, 768:896].astype(f32))
    for j in range(24):
        cw_ref[j : j + 1, :] = turned[2 + 3 * j : 3 + 3 * j] + turned[3 + 3 * j : 4 + 3 * j] + turned[4 + 3 * j : 5 + 3 * j]
    for b in range(6):
        part, hh = b // 2, b % 2
        cols = slice(b * 128, (b + 1) * 128)
        taps = [cw_ref[(part * 4 + j) * 2 + hh : (part * 4 + j) * 2 + hh + 1, :] for j in range(4)]
        for c in range(chunks):
            base = HALO + c * rows
            own = idc_ref[base : base + rows, :]
            acc = proj_ref[base : base + rows, cols] * taps[0]
            for j in range(1, 4):
                prior = idc_ref[base - j : base - j + rows, :]
                acc = acc + jnp.where(prior == own, proj_ref[base - j : base - j + rows, cols], 0.0) * taps[j]
            sum_ref[c * rows : (c + 1) * rows, cols] = acc
            mixed = acc / (1.0 + jnp.exp(-acc))
            if part < 2:
                mixed = mixed * lax.rsqrt(jnp.sum(mixed * mixed, -1, keepdims=True) + epsilon)
            qkv_ref[c * rows : (c + 1) * rows, cols] = mixed.astype(bf16)
    row, col = positions()
    differ = row ^ col
    strict = row > col
    units = [(hh, c) for c in range(chunks) for hh in range(2)]
    lower, inv, scaled = {}, {}, {}
    for hh, c in units:
        equal, carry, _, _ = chunk_masks(idc_ref, idr_ref, c)
        at = slice(c * CHUNK, (c + 1) * CHUNK)
        beta = jax.nn.sigmoid(jnp.broadcast_to(lgt_ref[at, hh : hh + 1], (CHUNK, 128)) - beta_shift)
        beta = jnp.where(idc_ref[HALO + c * CHUNK : HALO + (c + 1) * CHUNK, :] < SEQS, beta, 0.0)
        keys = qkv_ref[at, 256 + hh * 128 : 256 + (hh + 1) * 128]
        values = qkv_ref[at, 512 + hh * 128 : 512 + (hh + 1) * 128]
        low = jnp.where(equal & strict, nt(keys, keys), 0.0) * beta
        lower[hh, c] = low
        inv[hh, c] = jnp.where(row == col, 1.0, 0.0) - jnp.where(differ == 1, low, 0.0)
        scaled[hh, c] = jnp.concatenate(
            [(values.astype(f32) * beta).astype(bf16), (keys.astype(f32) * (beta * carry)).astype(bf16)], axis=1
        )
    for k in range(1, 7):
        level = (differ >> k) == 1
        for u in units:
            off = jnp.where(level, lower[u], 0.0).astype(bf16)
            half = inv[u].astype(bf16)
            inv[u] = inv[u] - nn(half, nn(off, half).astype(bf16))
    for hh, c in units:
        at = slice(c * CHUNK, (c + 1) * CHUNK)
        half = inv[hh, c].astype(bf16)
        inv_ref[hh, at, :] = half
        uw_ref[hh, at, :] = nn(half, scaled[hh, c]).astype(bf16)
    eye = jnp.where(row == col, 1.0, 0.0)
    state = [[eye, jnp.zeros((CHUNK, CHUNK), f32)] for _ in range(2)]
    for c in range(chunks):
        at = slice(c * CHUNK, (c + 1) * CHUNK)
        _, _, to_last, carry_last = chunk_masks(idc_ref, idr_ref, c)
        for hh in range(2):
            packed = jnp.concatenate([state[hh][0].astype(bf16), state[hh][1].astype(bf16)], axis=1)
            pre_ref[hh, c] = packed
            moved = nn(uw_ref[hh, at, 128:256], packed)
            change = jnp.concatenate(
                [(-moved[:, :128]).astype(bf16), (uw_ref[hh, at, 0:128].astype(f32) - moved[:, 128:]).astype(bf16)], axis=1
            )
            keys = qkv_ref[at, 256 + hh * 128 : 256 + (hh + 1) * 128]
            kept = (keys.astype(f32) * to_last).astype(bf16)
            step = tn(kept, change)
            state[hh] = [state[hh][0] * carry_last + step[:, :128], state[hh][1] * carry_last + step[:, 128:]]
    for hh in range(2):
        tot_ref[hh] = jnp.concatenate([state[hh][0].astype(bf16), state[hh][1].astype(bf16)], axis=1)


def reach_kernel(chunks, qkv_ref, uw_ref, pre_ref, idc_ref, idr_ref, score_ref, reach_ref, base_ref, far_ref):
    row, col = positions()
    causal = row >= col
    for c in range(chunks):
        at = slice(c * CHUNK, (c + 1) * CHUNK)
        equal, carry, _, _ = chunk_masks(idc_ref, idr_ref, c)
        for hh in range(2):
            queries = qkv_ref[at, hh * 128 : (hh + 1) * 128]
            keys = qkv_ref[at, 256 + hh * 128 : 256 + (hh + 1) * 128]
            score = jnp.where(causal & equal, nt(queries, keys), 0.0).astype(bf16)
            score_ref[hh, at, :] = score
            both = nn(score, uw_ref[hh, at, :])
            reach = (queries.astype(f32) * carry - both[:, 128:]).astype(bf16)
            reach_ref[hh, at, :] = reach
            far = nn(reach, pre_ref[hh, c])
            far_ref[hh, at, :] = far[:, :128].astype(bf16)
            base_ref[hh, at, :] = both[:, :128] + far[:, 128:]


def attend_kernel(base_ref, far_ref, state_ref, gain_ref, idc_ref, out_ref, head_ref):
    rows = base_ref.shape[1]
    mask = (idc_ref[HALO : HALO + rows, :] < SEQS).astype(f32)
    for hh in range(2):
        out = base_ref[hh] + nn(far_ref[hh], state_ref[hh])
        out_ref[hh] = out
        rh = lax.rsqrt(jnp.mean(out * out, -1, keepdims=True) + epsilon)
        head_ref[:, hh * 128 : (hh + 1) * 128] = (out * rh * gain_ref[0:1, :] * mask).astype(bf16)


def ffn_kernel(later, table_ref, order_ref, normed_ref, dy_ref, weight_ref, *rest):
    given, (out_ref, grad_ref, own_ref, other_ref, nturned, dturned) = rest[:later], rest[later:]
    step = pl.program_id(0)
    span = FFP

    @pl.when(step == 0)
    def _():
        for i in range(8):
            at = slice(i * 128, (i + 1) * 128)
            here = pl.ds(pl.multiple_of(table_ref[i] * 128, 128), 128)
            nturned[at, :] = jnp.transpose(normed_ref[:, here].astype(f32)).astype(bf16)
            dturned[at, :] = jnp.transpose(dy_ref[:, here].astype(f32)).astype(bf16)

    pair_w, down_w = weight_ref[:, 256 : 256 + PAIR], weight_ref[:, 256 + PAIR : 256 + PAIR + span]
    ff = PAIR // 2
    pair = nn(normed_ref[...], pair_w)
    inside = lax.broadcasted_iota(jnp.int32, (pair.shape[0], span), 1) < ff
    gate = jnp.where(inside, pair[:, 0:span], 0.0)
    up = jnp.where(inside, pltpu.roll(pair[:, PAIR - span :], ff, 1), 0.0)
    sig = 1.0 / (1.0 + jnp.exp(-gate))
    act = gate * sig
    hidden = (act * up).astype(bf16)
    grad_hidden = nn(dy_ref[...], down_w)
    grad_gate = grad_hidden * up * (sig * (1.0 + gate * (1.0 - sig)))
    grad_up = pltpu.roll(grad_hidden * act, span - ff, 1)
    joint = PAIR - span
    grad_pair = jnp.concatenate(
        [grad_gate[:, :joint], grad_gate[:, joint:] + grad_up[:, : span - joint], grad_up[:, span - joint :]], 1
    ).astype(bf16)
    out = nt(hidden, down_w)
    back = nt(grad_pair, pair_w)

    @pl.when(step == 0)
    def _():
        out_ref[...] = given[0][...] + out if later else out
        grad_ref[...] = given[1][...] + back if later else back

    @pl.when(step > 0)
    def _():
        out_ref[...] += out
        grad_ref[...] += back

    half = own_ref.shape[0]
    for target, into in ((own_ref, slice(0, half)), (other_ref, slice(half, 2 * half))):
        target[:, 0:PAIR] = nn(nturned[into, :], grad_pair).astype(bf16)
        target[:, PAIR : PAIR + span] = nn(dturned[into, :], hidden).astype(bf16)


def inner_back_kernel(chunks, skip, qkv_ref, uw_ref, pre_ref, score_ref, datt_ref, state_ref, idc_ref, idr_ref, *rest):
    states_ref, pseudo_ref, dq_ref, dk_ref, dp_ref = rest[skip:]
    row, col = positions()
    causal = row >= col
    for c in range(chunks):
        at = slice(c * CHUNK, (c + 1) * CHUNK)
        equal, carry, _, _ = chunk_masks(idc_ref, idr_ref, c)
        for hh in range(2):
            queries = qkv_ref[at, hh * 128 : (hh + 1) * 128]
            keys = qkv_ref[at, 256 + hh * 128 : 256 + (hh + 1) * 128]
            grad = datt_ref[hh, at, :]
            state = (nn(pre_ref[hh, c, :, 0:128], state_ref[hh]) + pre_ref[hh, c, :, 128:256].astype(f32)).astype(bf16)
            states_ref[hh, c] = state
            pseudo = (uw_ref[hh, at, 0:128].astype(f32) - nn(uw_ref[hh, at, 128:256], state)).astype(bf16)
            pseudo_ref[hh, at, :] = pseudo
            both = nt(grad, jnp.concatenate([pseudo, state], 0))
            grad_score = jnp.where(causal & equal, both[:, :CHUNK], 0.0).astype(bf16)
            dq_ref[hh, at, :] = both[:, CHUNK:] * carry + nn(grad_score, keys)
            dk_ref[hh, at, :] = tn(grad_score, queries)
            dp_ref[hh, at, :] = tn(score_ref[hh, at, :], grad)


def tail_kernel(
    chunks, n_seq, last, table_ref, qkv_ref, uw_ref, inv_ref, reach_ref, datt_ref, states_ref, pseudo_ref, dq_ref, dk_ref, dp_ref,
    sum_ref, proj_ref, lgt_ref, gout_ref, cw_ref, idc_ref, idr_ref,
    turned_ref, edge_ref, *rest,
):
    first_w, second_w, rest = rest[:4], rest[4:8], rest[8:]
    if last:
        gn_in, gh_in, x_ref, halo_ref, gain_ref, gres_ref = rest[:6]
        in_ref, hin_ref, gone_ref, own_ref, other_ref, gp_ref, first_ref, dqkv, pad, spread, extra, gn_ref, gh_ref = rest[6:]
    else:
        outs_w, (gn_ref, gh_ref, own_ref, other_ref, gp_ref, first_ref, dqkv, pad, spread, extra) = rest[:4], rest[4:]
    step = pl.program_id(0)
    row, col = positions()
    strict = row > col
    lane = lax.broadcasted_iota(jnp.int32, (CHUNK, 128), 1)
    grad_state = [gout_ref[hh].astype(f32) for hh in range(2)]
    for c in range(chunks - 1, -1, -1):
        at = slice(c * CHUNK, (c + 1) * CHUNK)
        equal, carry, to_last, carry_last = chunk_masks(idc_ref, idr_ref, c)
        own = idc_ref[HALO + c * CHUNK : HALO + (c + 1) * CHUNK, :]
        dlgt = jnp.zeros((CHUNK, 128), f32)
        for hh in range(2):
            keys = qkv_ref[at, 256 + hh * 128 : 256 + (hh + 1) * 128]
            keys_f = keys.astype(f32)
            values = qkv_ref[at, 512 + hh * 128 : 512 + (hh + 1) * 128]
            kept = (keys_f * to_last).astype(bf16)
            packed = grad_state[hh].astype(bf16)
            push = nn(kept, packed)
            grad_state[hh] = grad_state[hh] * carry_last + tn(reach_ref[hh, at, :], datt_ref[hh, at, :]) - tn(
                uw_ref[hh, at, 128:256], push.astype(bf16)
            )
            full = (dp_ref[hh, at, :] + push).astype(bf16)
            solved = tn(inv_ref[hh, at, :], full)
            solved_h = solved.astype(bf16)
            pseudo = pseudo_ref[hh, at, :]
            gate = jax.nn.sigmoid(jnp.broadcast_to(lgt_ref[at, hh : hh + 1], (CHUNK, 128)) - beta_shift)
            mask = (own < SEQS).astype(f32)
            beta = gate * mask
            back = nt(solved_h, states_ref[hh, c]) * carry
            outer = jnp.where(equal & strict, nt(solved_h, pseudo), 0.0)
            overlap = nt(keys, keys)
            rate = jnp.sum(solved * values.astype(f32) - back * keys_f - outer * overlap, -1, keepdims=True)
            dlgt = jnp.where(lane == hh, rate * mask * gate * (1.0 - gate), dlgt)
            mixed = (outer * beta).astype(bf16)
            dqkv[at, 256 + hh * 128 : 256 + (hh + 1) * 128] = (
                dk_ref[hh, at, :] + nt(pseudo, packed) * to_last - beta * back - nn(mixed, keys) - tn(mixed, keys)
            )
            dqkv[at, 512 + hh * 128 : 512 + (hh + 1) * 128] = beta * solved
            dqkv[at, hh * 128 : (hh + 1) * 128] = dq_ref[hh, at, :]
        gp_ref[at, 768:896] = dlgt.astype(bf16)
    rows = CHUNK
    length = chunks * CHUNK
    for b in range(6):
        part, hh = b // 2, b % 2
        cols = slice(b * 128, (b + 1) * 128)
        taps = [cw_ref[(part * 4 + j) * 2 + hh : (part * 4 + j) * 2 + hh + 1, :] for j in range(4)]
        pad[0:HALO, :] = jnp.zeros((HALO, 128), f32)
        pad[HALO + length : 2 * HALO + length, :] = jnp.zeros((HALO, 128), f32)
        sums = [jnp.zeros((1, 128), f32) for _ in range(4)]
        for c in range(chunks):
            at = slice(c * rows, (c + 1) * rows)
            base = HALO + c * rows
            u = sum_ref[at, cols]
            sig = 1.0 / (1.0 + jnp.exp(-u))
            grad = dqkv[at, cols]
            if part < 2:
                mixed = u * sig
                r = lax.rsqrt(jnp.sum(mixed * mixed, -1, keepdims=True) + epsilon)
                grad = r * grad - mixed * ((r * r * r) * jnp.sum(mixed * grad, -1, keepdims=True))
            grad = grad * (sig * (1.0 + u * (1.0 - sig)))
            pad[base : base + rows, :] = grad
            own = idc_ref[base : base + rows, :]
            sums[0] = sums[0] + jnp.sum(grad * proj_ref[base : base + rows, cols], 0, keepdims=True)
            for j in range(1, 4):
                prior = idc_ref[base - j : base - j + rows, :]
                sums[j] = sums[j] + jnp.sum(
                    jnp.where(prior == own, proj_ref[base - j : base - j + rows, cols], 0.0) * grad, 0, keepdims=True
                )
        for j in range(4):
            spot = 2 + (part * 4 + j) * 2 + hh
            spread[spot : spot + 1, :] = sums[j]
        for start, size in [(0, HALO)] + [(HALO + c * rows, rows) for c in range(chunks)]:
            own = idc_ref[start : start + size, :]
            acc = pad[start : start + size, :] * taps[0]
            for j in range(1, 4):
                later = idc_ref[start + j : start + j + size, :]
                acc = acc + jnp.where(later == own, pad[start + j : start + j + size, :], 0.0) * taps[j]
            if start == 0:
                first_ref[:, cols] = jnp.concatenate([acc, jnp.zeros((HALO, 128), f32)], 0).astype(bf16)
            else:
                gp_ref[start - HALO : start - HALO + size, cols] = acc.astype(bf16)
    first_ref[:, 768:896] = jnp.zeros((2 * HALO, 128), bf16)

    @pl.when(step == 0)
    def _():
        spread[0:2, :] = jnp.zeros((2, 128), f32)
        spread[26:128, :] = jnp.zeros((102, 128), f32)
        extra[...] = jnp.zeros(extra.shape, f32)

    pad[0:128, :] = jnp.transpose(spread[...])
    part, lanes = 1024 // n_seq, 128 // n_seq
    for i in range(n_seq):
        if n_seq == 8:
            piece = pad[pl.ds(pl.multiple_of(table_ref[i] * lanes, lanes), lanes), :]
        else:
            piece = pad[i * lanes : (i + 1) * lanes, :]
        extra[i * part : i * part + lanes, :] = piece
    grads, edge = gp_ref[...], first_ref[...]

    def back(pieces, fresh):
        weights = jnp.concatenate([w[...] for w in pieces], 0)
        if fresh:
            gn_ref[...] = nt(grads, weights)
            gh_ref[...] = nt(edge, weights)
        else:
            gn_ref[...] += nt(grads, weights)
            gh_ref[...] += nt(edge, weights)

    @pl.when(step == 0)
    def _():
        if last:
            gn_ref[...] = gn_in[...]
            gh_ref[...] = gh_in[...]
        back(first_w, not last)

    @pl.when(step == 1)
    def _():
        back(second_w, False)

    half = own_ref.shape[0]
    for target, into in ((own_ref, slice(0, half)), (other_ref, slice(half, 2 * half))):
        total = nn(turned_ref[into, :], grads) + tn(edge_ref[:, into], edge)
        target[:, 0:768] = total[:, :768].astype(bf16)
        target[:, 768:896] = (total[:, 768:] + extra[into, :]).astype(bf16)

    if not last:
        for i, target in enumerate((own_ref, other_ref)):
            target[:, 896:1152] = outs_w[i][...]
            target[:, 1152:1408] = outs_w[2 + i][...]

    if last:

        @pl.when(step == 1)
        def _():
            for i in range(8):
                here = pl.ds(pl.multiple_of(table_ref[i] * 128, 128), 128)
                in_ref[:, here] = gn_ref[:, i * 128 : (i + 1) * 128]
                hin_ref[:, here] = gh_ref[0:HALO, i * 128 : (i + 1) * 128]

            def through(x, normed_grad):
                r1 = lax.rsqrt(jnp.mean(x * x, -1, keepdims=True) + epsilon)
                scaled = gain_ref[...] * normed_grad
                moved = r1 * scaled - x * ((r1 * r1 * r1) * jnp.mean(x * scaled, -1, keepdims=True))
                return moved, jnp.sum(normed_grad * x * r1, 0, keepdims=True)

            moved, sums_one = through(x_ref[...].astype(f32), in_ref[...])
            in_ref[...] = gres_ref[...] + moved
            moved, sums_two = through(halo_ref[...], hin_ref[...])
            hin_ref[...] = moved
            gone_ref[...] = jnp.broadcast_to(sums_one + sums_two, gone_ref.shape)


def core_first(n_seq):
    return [2 if i % 2 == 0 else 4 for i in range(n_seq)], [4 if i % 2 == 0 else 2 for i in range(n_seq)]


def seq_permute(array, steps):
    return lax.ppermute(array, "seq", [(i, i ^ k) for i, k in enumerate(steps)])


def ring(array, by=1):
    count = lax.axis_size("head")
    return lax.ppermute(array, "head", [(i, (i + by) % count) for i in range(count)])


def slot_table(s, n_seq):
    if n_seq != 8:
        return jnp.arange(8, dtype=jnp.int32)
    odd = s & 1
    f = jnp.where(odd == 0, 2, 4)
    g = 6 - f
    masks = jnp.stack([0 * f, f, g, 0 * f + 6, 0 * f + 1, 1 ^ g, 1 ^ f, 0 * f + 7])
    return (s ^ masks).astype(jnp.int32)


def gather_plane(pieces, n_seq):
    if n_seq != 8:
        full = lax.all_gather(pieces, "seq", axis=1, tiled=True)
        quarter = full.shape[1] // 4
        return [full[:, i * quarter : (i + 1) * quarter] for i in range(4)]
    near, wide = core_first(n_seq)
    pair = jnp.concatenate([pieces, seq_permute(pieces, near)], 1)
    pair_two = seq_permute(pair, wide)
    swap = [1] * n_seq
    return [pair, pair_two, seq_permute(pair, swap), seq_permute(pair_two, swap)]


def plus(a, b):
    return (a.astype(f32) + b.astype(f32)).astype(bf16)


def tie(value, *others):
    return lax.optimization_barrier((value,) + others)[0]


def after_core(own, got):
    return plus(own[:, own.shape[1] // 2 :], got[:, own.shape[1] // 2 :])


def after_wide(own, got, more):
    quarter = own.shape[1] // 4
    at = slice(quarter, 2 * quarter)
    return (own[:, at].astype(f32) + got[:, at].astype(f32) + more[:, quarter:].astype(f32)).astype(bf16)


def after_near(own, got, more, last):
    quarter = own.shape[1] // 4
    total = own[:, :quarter].astype(f32) + got[:, :quarter].astype(f32) + more[:, :quarter].astype(f32)
    return (total + last.astype(f32)).astype(bf16)


def reduce_whole(own, other):
    return lax.psum_scatter(jnp.concatenate([own, other], 1), "seq", scatter_dimension=1, tiled=True)


def reduce_ring(parts):
    groups = len(parts)
    moving = parts[1]
    for k in range(2, groups + 1):
        moving = ring(moving).astype(f32) + parts[k % groups].astype(f32)
        if k < groups:
            moving = moving.astype(bf16)
    return moving


def apply(a, x):
    return jnp.einsum("hij,hjk->hik", a.astype(bf16), x.astype(bf16), preferred_element_type=f32)


def pull(a, g):
    return jnp.einsum("hij,hik->hjk", a.astype(bf16), g.astype(bf16), preferred_element_type=f32)


def to_groups(slots, z):
    groups = len(slots)
    arrived = jnp.stack([slots[0]] + [ring(slots[k], -k) for k in range(1, groups)])
    return lax.dynamic_slice_in_dim(jnp.concatenate([arrived, arrived], 0), (groups - z) % groups, groups, 0)


def from_groups(blocks, z):
    groups = len(blocks)
    stacked = jnp.stack(blocks)
    turned = lax.dynamic_slice_in_dim(jnp.concatenate([stacked, stacked], 0), z, groups, 0)
    return jnp.stack([turned[0]] + [ring(turned[k], k) for k in range(1, groups)])


def exchange_forward(tot, n_seq, s, z, beside):
    groups = len(tot)
    got = tie(to_groups(tot, z), beside)

    def after(second, first):
        moved = apply(second[..., :128], first)
        return jnp.concatenate([moved[..., :128], moved[..., 128:] + second[..., 128:].astype(f32)], -1)

    whole = got[0].astype(f32)
    for j in range(1, groups):
        whole = after(got[j], whole)
    eye = jnp.broadcast_to(jnp.eye(128, dtype=f32), (2, 128, 128))
    prefix = jnp.concatenate([eye, jnp.zeros((2, 128, 128), f32)], -1)
    suffix = eye
    kept = []
    k = 1
    while k < n_seq:
        mine = whole.astype(bf16)
        other = lax.ppermute(mine, "seq", [(i, i ^ k) for i in range(n_seq)])
        upper = (s & k) != 0
        first = jnp.where(upper, other, mine)
        second = jnp.where(upper, mine, other)
        kept.append((first[..., :128], suffix.astype(bf16)))
        prefix = jnp.where(upper, after(prefix, other), prefix)
        suffix = jnp.where(upper, suffix, apply(other[..., :128], suffix))
        whole = after(second, first)
        k *= 2
    state = prefix[..., 128:]
    states = [state.astype(bf16)]
    for j in range(groups - 1):
        state = apply(got[j][..., :128], state) + got[j][..., 128:].astype(f32)
        states.append(state.astype(bf16))
    return from_groups(states, z), got, kept


def exchange_backward(local, got, kept, n_seq, s, z, beside):
    groups = len(local)
    grads = tie(to_groups(local, z), *beside)
    whole = grads[groups - 1].astype(f32)
    for j in range(groups - 2, -1, -1):
        whole = pull(got[j][..., :128], whole) + grads[j].astype(f32)
    later = jnp.zeros_like(whole)
    k = 1
    for first_a, suffix in kept:
        mine = whole.astype(bf16)
        other = lax.ppermute(mine, "seq", [(i, i ^ k) for i in range(n_seq)])
        upper = (s & k) != 0
        later = jnp.where(upper, later, pull(suffix, other) + later)
        first = jnp.where(upper, other, mine)
        second = jnp.where(upper, mine, other)
        whole = pull(first_a, second) + first.astype(f32)
        k *= 2
    outs = [later.astype(bf16)]
    for j in range(groups - 1, 0, -1):
        later = pull(got[j][..., :128], later) + grads[j].astype(f32)
        outs.append(later.astype(bf16))
    return from_groups(outs[::-1], z), outs[0]


def gain_steps(n_seq, n_head):
    if n_seq == 8:
        near, wide = core_first(n_seq)
        steps = [("seq", [1] * n_seq), ("seq", wide), ("seq", near)]
    else:
        steps = [("seq", [1 << i] * n_seq) for i in range(n_seq.bit_length() - 1)]
    return [("head", [1 << i] * n_head) for i in range(n_head.bit_length() - 1)] + steps


def swap_add(array, step):
    axis, partner = step
    return array + lax.ppermute(array, axis, [(i, i ^ k) for i, k in enumerate(partner)])


def local(
    inputs, norm1_gain, w_query, w_key, w_value, w_beta, conv_weight, head_gain, w_out, norm2_gain, w_gate, w_up, w_down,
    seq_ids, cotangent,
):
    n_seq, n_head = lax.axis_size("seq"), lax.axis_size("head")
    s, z = lax.axis_index("seq"), lax.axis_index("head")
    rows, width = inputs.shape
    ff = w_gate.shape[1]
    chunks = rows // CHUNK
    ext = rows + HALO
    count = n_seq * n_head
    part = width // n_seq
    quarter = width // 4
    table = slot_table(s, n_seq)
    smem = pl.BlockSpec(memory_space=pltpu.SMEM)

    before = lax.ppermute(inputs[-HALO:], WHOLE, [(i, i + 1) for i in range(count - 1)])
    ids_before = lax.ppermute(seq_ids[-HALO:], "seq", [(i, i + 1) for i in range(n_seq - 1)])
    taps = conv_weight.reshape(24, 128).T
    high = lax.reduce_precision(taps, 8, 7)
    middle = lax.reduce_precision(taps - high, 8, 7)
    coded = jnp.stack([high, middle, taps - high - middle], -1).reshape(128, 72).astype(bf16)
    coded = jnp.tile(coded, (width // 128, 1))
    more = jnp.concatenate([w_beta, coded, jnp.zeros((width, 54), bf16)], 1)

    def by_row(columns):
        return pl.BlockSpec((128, columns), lambda i, table: (table[i], 0))

    def by_column(size):
        return pl.BlockSpec((size, 128), lambda i, table: (0, table[i]))

    columns = 256 + PAIR + FFP

    def packed_proj(blocks, name):
        return pl.pallas_call(
            pack_proj_kernel,
            grid_spec=pltpu.PrefetchScalarGridSpec(
                num_scalar_prefetch=1,
                grid=(blocks,),
                in_specs=[by_row(256)] * 3 + [by_row(128)],
                out_specs=pl.BlockSpec((128, 896), lambda i, table: (i, 0)),
            ),
            out_shape=sds((blocks * 128, 896), bf16),
            compiler_params=params(),
            cost_estimate=cost(0.8 * blocks),
            name=name,
        )(table, w_query, w_key, w_value, more)

    proj_local = packed_proj(8, "pack_proj")
    if n_seq == 8:
        own_proj = packed_proj(1, "pack_proj_own")
        own_ffn = pl.pallas_call(
            pack_ffn_kernel,
            grid_spec=pltpu.PrefetchScalarGridSpec(
                num_scalar_prefetch=1,
                grid=(1,),
                in_specs=[by_column(ff), by_column(ff), by_column(ff), by_column(256)],
                out_specs=pl.BlockSpec((128, columns), lambda i, table: (i, 0)),
                scratch_shapes=[pltpu.VMEM((PAIR, 128), f32)],
            ),
            out_shape=sds((128, columns), bf16),
            compiler_params=params(),
            cost_estimate=cost(2),
            name="pack_ffn",
        )(table, w_gate.T, w_up.T, w_down, w_out)
    else:
        own_proj = lax.dynamic_slice_in_dim(proj_local, s * part, part, 0)

        down = jnp.pad(w_down.T, ((0, 0), (0, FFP - ff)))
        whole_ffn = jnp.concatenate([w_out.T, w_gate, w_up, down], 1)
        own_ffn = lax.dynamic_slice_in_dim(whole_ffn, s * part, part, 0)
    ffn_all = lax.all_gather(own_ffn, BY_HEAD, axis=0, tiled=True).reshape(n_head, width, columns)
    ring_pieces = [own_proj]
    for _ in range(n_head - 1):
        ring_pieces.append(ring(ring_pieces[-1]))
    proj_one = gather_plane(ring_pieces[1][None], n_seq)
    proj_far = gather_plane(jnp.stack(ring_pieces[2:]), n_seq)

    ids_before = jnp.where(s == 0, -1, ids_before)
    ids = lax.dynamic_slice_in_dim(jnp.concatenate([ids_before, seq_ids]), z * rows, ext)
    ids_pad = jnp.concatenate([ids, jnp.full((HALO,), -2, jnp.int32)])
    idc = jnp.broadcast_to(ids_pad[:, None], (ext + HALO, 128))
    idr = jnp.broadcast_to(ids[None, :], (8, ext))
    halo = before.astype(f32)
    normed_ext, turned = pl.pallas_call(
        prep_kernel,
        grid=(1,),
        in_specs=[smem, same(HALO, width), same(rows, width), same(1, width)],
        out_specs=[same(ext, width), same(width, rows)],
        out_shape=[sds((ext, width), bf16), sds((width, rows), bf16)],
        scratch_shapes=[pltpu.VMEM((ext, width), f32)],
        compiler_params=params(),
        cost_estimate=cost(5),
        name="prep",
    )(table, halo, inputs, norm1_gain[None])

    idc_spec, idr_spec = same(ext + HALO, 128), same(8, ext)
    hidden_spec = pl.BlockSpec(memory_space=pl.ANY)
    shapes = [
        ((ext, 768), f32), ((rows, 128), f32), ((24, 128), f32), ((rows, 768), bf16), ((rows, 768), f32), ((2, rows, 256), bf16),
        ((2, rows, 128), bf16), ((2, chunks, 128, 256), bf16),
    ]

    def shifted(by, *shape):
        zeros = (0,) * len(shape)
        return pl.BlockSpec((None,) + shape, lambda i: (i + by,) + zeros)

    def local_pieces(columns, at=0):
        return [pl.BlockSpec((quarter, columns), lambda k, i=i: (i, at)) for i in range(4)]

    first = pl.pallas_call(
        functools.partial(front_kernel, chunks, 0),
        grid=(1,),
        in_specs=[same(ext, width)] + local_pieces(896) + [idc_spec, idr_spec],
        out_specs=[lead(*shape) for shape, _ in shapes] + [lead(2, 128, 256)],
        out_shape=[sds((n_head,) + shape, kind) for shape, kind in shapes] + [sds((1, 2, 128, 256), bf16)],
        compiler_params=params(),
        cost_estimate=cost(9),
        name="front_near",
    )(normed_ext, *[proj_local] * 4, idc, idr)
    def front_more(pieces, by, before_it, name):
        size = pieces[0].shape[0]
        return pl.pallas_call(
            functools.partial(front_kernel, chunks, len(shapes)),
            grid=(size,),
            in_specs=[same(ext, width)] + [lead(quarter, 896)] * 4 + [idc_spec, idr_spec] + [hidden_spec] * len(shapes),
            out_specs=[shifted(by, *shape) for shape, _ in shapes] + [lead(2, 128, 256)],
            out_shape=[sds((n_head,) + shape, kind) for shape, kind in shapes] + [sds((size, 2, 128, 256), bf16)],
            input_output_aliases={7 + i: i for i in range(len(shapes))},
            compiler_params=params(),
            cost_estimate=cost(7 * size + 1),
            name=name,
        )(normed_ext, *pieces, idc, idr, *before_it[:-1])

    second = front_more(proj_one, 1, first, "front_one")
    filled = front_more(proj_far, 2, second, "front_far")
    projected, logits, taps_all, qkv, summed, uw, inverse, prefixes, totals = filled
    every_total = [first[-1][0], second[-1][0]] + [totals[k] for k in range(n_head - 2)]
    score, reach, base, far = pl.pallas_call(
        functools.partial(reach_kernel, chunks),
        grid=(n_head,),
        in_specs=[lead(rows, 768), lead(2, rows, 256), lead(2, chunks, 128, 256), idc_spec, idr_spec],
        out_specs=[lead(2, rows, 128)] * 4,
        out_shape=[sds((n_head, 2, rows, 128), kind) for kind in (bf16, bf16, f32, bf16)],
        compiler_params=params(),
        cost_estimate=cost(9),
        name="reach",
    )(qkv, uw, prefixes, idc, idr)
    state_in, got, kept = exchange_forward(every_total, n_seq, s, z, score)
    gain_rows = jnp.broadcast_to(head_gain[None, :], (8, 128))
    attended, head_out = pl.pallas_call(
        attend_kernel,
        grid=(n_head,),
        in_specs=[lead(2, rows, 128), lead(2, rows, 128), lead(2, 128, 128), same(8, 128), idc_spec],
        out_specs=[lead(2, rows, 128), pl.BlockSpec((rows, 256), lambda i: (0, i))],
        out_shape=[sds((n_head, 2, rows, 128), f32), sds((rows, n_head * 256), bf16)],
        compiler_params=params(),
        cost_estimate=cost(5),
        name="attend",
    )(base, far, state_in, gain_rows, idc)

    order = ((z - jnp.arange(n_head)) % n_head).astype(jnp.int32)

    def by_slot(columns, at):
        return pl.BlockSpec((None, width, columns), lambda k, order: (order[k], 0, at))

    def fixed(*shape):
        zeros = (0,) * len(shape)
        return pl.BlockSpec(shape, lambda k, *scalars: zeros)

    def led(*shape):
        zeros = (0,) * len(shape)
        return pl.BlockSpec((None,) + shape, lambda k, *scalars: (k,) + zeros)

    head_columns = pl.BlockSpec((rows, 256), lambda k, *scalars: (0, k))
    residual, normed_two = pl.pallas_call(
        functools.partial(mix_kernel, n_head),
        grid_spec=pltpu.PrefetchScalarGridSpec(
            num_scalar_prefetch=1,
            grid=(1,),
            in_specs=[
                fixed(rows, n_head * 256), fixed(rows, width), fixed(1, width),
                pl.BlockSpec((n_head, width, 256), lambda k, *scalars: (0, 0, 0)),
            ],
            out_specs=[fixed(rows, width), fixed(rows, width)],
        ),
        out_shape=[sds((rows, width), f32), sds((rows, width), bf16)],
        compiler_params=params(),
        cost_estimate=cost(5),
        name="mix",
    )(order, head_out, inputs, norm2_gain[None], ffn_all)
    near, wide = core_first(n_seq)
    swap = [1] * n_seq

    ffn_weights = pl.BlockSpec((None, width, columns), lambda k, table, order: (order[k], 0, 0))
    ffn_grads = sds((n_head, width // 2, PAIR + FFP), bf16)
    ffn_out, grad_two, *ffn_a = pl.pallas_call(
        functools.partial(ffn_kernel, 0),
        grid_spec=pltpu.PrefetchScalarGridSpec(
            num_scalar_prefetch=2,
            grid=(n_head,),
            in_specs=[fixed(rows, width), pl.BlockSpec((rows, width), lambda k, table, order: (order[0], 0))]
            + [ffn_weights],
            out_specs=[fixed(rows, width), fixed(rows, width)] + [led(width // 2, PAIR + FFP)] * 2,
            scratch_shapes=[pltpu.VMEM((width, rows), bf16)] * 2,
        ),
        out_shape=[sds((rows, width), f32), sds((rows, width), f32), ffn_grads, ffn_grads],
        compiler_params=params(60),
        cost_estimate=cost(2),
        name="ffn",
    )(table, order, normed_two, cotangent, ffn_all)
    if n_seq == 8:
        ffn_a = [ffn_a[0], seq_permute(ffn_a[1], swap)]
        send_a = after_core(*ffn_a)

    output, grad_residual, grad_norm_two, out_own, out_other, datt, local_grad, gain_part = pl.pallas_call(
        turn_kernel,
        grid_spec=pltpu.PrefetchScalarGridSpec(
            num_scalar_prefetch=2,
            grid=(n_head,),
            in_specs=[
                fixed(rows, width), fixed(rows, width), fixed(rows, width),
                pl.BlockSpec((rows, width), lambda k, table, order: (order[0], 0)), fixed(1, width), head_columns,
                pl.BlockSpec((None, width, 256), lambda k, table, order: (order[k], 0, 0)), led(2, rows, 128),
                led(2, rows, 128), fixed(8, 128), fixed(ext + HALO, 128),
            ],
            out_specs=[
                fixed(rows, width), fixed(rows, width), fixed(8, width),
                led(width // 2, 256), led(width // 2, 256), led(2, rows, 128),
                led(2, 128, 128), led(8, 128),
            ],
            scratch_shapes=[pltpu.VMEM((rows, width), bf16), pltpu.VMEM((width, rows), bf16)],
        ),
        out_shape=[
            sds((rows, width), bf16), sds((rows, width), f32), sds((8, width), f32), sds((n_head, width // 2, 256), bf16),
            sds((n_head, width // 2, 256), bf16), sds((n_head, 2, rows, 128), bf16), sds((n_head, 2, 128, 128), bf16), sds((n_head, 8, 128), f32),
        ],
        compiler_params=params(),
        cost_estimate=cost(0.6),
        name="turn",
    )(
        table, order, ffn_out, grad_two, residual, cotangent, norm2_gain[None], head_out, ffn_all, attended, far, gain_rows, idc,
    )
    grad_out_state, reached = exchange_backward(
        [local_grad[k] for k in range(n_head)], got, kept, n_seq, s, z, [send_a] if n_seq == 8 else []
    )
    if n_seq == 8:
        more_a = seq_permute(tie(send_a, reached), wide)
    inner_shapes = [((2, chunks, 128, 128), bf16)] + [((2, rows, 128), kind) for kind in (bf16, f32, f32, f32)]
    states, pseudo, dq, dk, dp = pl.pallas_call(
        functools.partial(inner_back_kernel, chunks, 0),
        grid=(n_head,),
        in_specs=[
            lead(rows, 768), lead(2, rows, 256), lead(2, chunks, 128, 256), lead(2, rows, 128), lead(2, rows, 128),
            lead(2, 128, 128), idc_spec, idr_spec,
        ],
        out_specs=[lead(*shape) for shape, _ in inner_shapes],
        out_shape=[sds((n_head,) + shape, kind) for shape, kind in inner_shapes],
        compiler_params=params(),
        cost_estimate=cost(1),
        name="inner_back",
    )(qkv, uw, prefixes, score, datt, state_in, idc, idr)
    def tail(slot, pieces, before_it, name):
        last = bool(before_it)
        size = 896 if last else 1408
        grad_size = sds((2, width // 2, size), bf16)

        def at(*shape):
            zeros = (0,) * len(shape)
            return pl.BlockSpec((None,) + shape, lambda i: (slot(i),) + zeros)

        sums = [same(rows, width), same(2 * HALO, width)]
        sum_shapes = [sds((rows, width), f32), sds((2 * HALO, width), f32)]
        given = [out_own, out_other, out_own, out_other]
        given_specs = [pl.BlockSpec((None, width // 2, 256), lambda i: (i + 1, 0, 0))] * 2
        given_specs += [pl.BlockSpec((None, width // 2, 256), lambda i: (3 - 3 * i, 0, 0))] * 2
        outs, out_specs = sum_shapes, sums
        if last:
            given = [*before_it, inputs, halo, norm1_gain[None], grad_residual]
            given_specs = sums + [same(rows, width), same(HALO, width), same(1, width), same(rows, width)]
            outs = [sds((rows, width), f32), sds((HALO, width), f32), sds((8, width), f32)]
            out_specs = [same(rows, width), same(HALO, width), same(8, width)]
        return pl.pallas_call(
            functools.partial(tail_kernel, chunks, n_seq, last),
            grid=(2,),
            in_specs=[
                smem, at(rows, 768), at(2, rows, 256), at(2, rows, 128), at(2, rows, 128), at(2, rows, 128),
                at(2, chunks, 128, 128), at(2, rows, 128), at(2, rows, 128), at(2, rows, 128), at(2, rows, 128),
                at(rows, 768), at(ext, 768), at(rows, 128), at(2, 128, 128), at(24, 128), idc_spec, idr_spec,
                same(width, rows), same(2 * HALO, width),
            ]
            + [spec for spec, _ in pieces]
            + given_specs,
            out_specs=out_specs + [lead(width // 2, size)] * 2,
            out_shape=outs + [grad_size] * 2,
            scratch_shapes=[
                pltpu.VMEM((rows, 896), bf16), pltpu.VMEM((2 * HALO, 896), bf16), pltpu.VMEM((rows, 768), f32),
                pltpu.VMEM((rows + 2 * HALO, 128), f32), pltpu.VMEM((128, 128), f32), pltpu.VMEM((width, 128), f32),
            ]
            + ([pltpu.VMEM((rows, width), f32), pltpu.VMEM((2 * HALO, width), f32)] if last else []),
            compiler_params=params(60),
            cost_estimate=cost(1),
            name=name,
        )(
            table, qkv, uw, inverse, reach, datt, states, pseudo, dq, dk, dp, summed, projected, logits, grad_out_state, taps_all, idc,
            idr, turned, normed_ext, *[piece for _, piece in pieces], *given,
        )

    def picked(arrays, k):
        return [(pl.BlockSpec((None, quarter, 896), lambda i: (k, 0, 0)), array) for array in arrays]

    here = list(zip(local_pieces(896), [proj_local] * 4))
    *partial, one_own, one_other = tail(lambda i: i + 1, picked(proj_one, 0) + picked(proj_far, 0), [], "tail_one")
    if n_seq == 8:
        one_got = seq_permute(one_other, swap)
        one_send = after_core(one_own, one_got)
        next_a = after_wide(*ffn_a, more_a)
        partial[0] = tie(partial[0], next_a, one_send)
        last_a = seq_permute(next_a, near)
        one_more = seq_permute(one_send, wide)
    inputs_grad, halo_grad, grad_norm_one, two_own, two_other = tail(
        lambda i: 3 - 3 * i, picked(proj_far, 1) + here, partial, "tail_two"
    )
    from_next = lax.ppermute(halo_grad, WHOLE, [(i + 1, i) for i in range(count - 1)])
    gains = jnp.concatenate([grad_norm_one[0], grad_norm_two[0], jnp.sum(gain_part[:, 0], 0)]).reshape(-1, 128)
    steps = gain_steps(n_seq, n_head)
    if n_seq == 8:
        two_got = seq_permute(two_other, swap)
        gains = swap_add(gains, steps[0])
        sum_a = after_near(*ffn_a, more_a, last_a)
        gains = swap_add(tie(gains, sum_a), steps[1])
        moved = ring(tie(sum_a[1], gains))
        two_send = after_core(two_own, tie(two_got, sum_a))
        two_more = seq_permute(two_send, wide)
        one_send = after_wide(one_own, one_got, tie(one_more, two_other, gains))
        one_last = seq_permute(one_send, near)
        moved = ring(plus(moved, sum_a[2]))
        two_send = after_wide(two_own, two_got, two_more)
        two_last = seq_permute(two_send, near)
        one_sum = after_near(one_own, one_got, one_more, tie(one_last, sum_a))
        gains = tie(gains, two_send)
        two_sum = after_near(two_own, two_got, two_more, two_last)
        for step in steps[2:]:
            gains = swap_add(gains, step)
        from_next = tie(from_next, two_sum)
        sum_ffn = ring(plus(moved, sum_a[3])).astype(f32) + sum_a[0].astype(f32)
    else:
        one_sum, two_sum, sum_a = (reduce_whole(*pair) for pair in ((one_own, one_other), (two_own, two_other), ffn_a))
        for step in steps:
            gains = swap_add(gains, step)
        sum_ffn = reduce_ring([sum_a[k] for k in range(n_head)])
    third = jnp.concatenate([two_sum[0], one_sum[0, :, 1152:]], 1)
    fourth = jnp.concatenate([two_sum[1], one_sum[1, :, 1152:]], 1)
    sum_proj = reduce_ring([fourth, one_sum[0, :, :1152], one_sum[1, :, :1152], third])
    inputs_grad = inputs_grad.at[rows - HALO :].add(from_next)
    lanes = 128 // n_seq
    gains = gains.reshape(-1)
    return (
        output, inputs_grad, gains[:width], sum_proj[:, :256], sum_proj[:, 256:512], sum_proj[:, 512:768], sum_proj[:, 768:770],
        sum_proj[:lanes, 770:794].T.reshape(3, 4, 2, lanes), gains[2 * width :], sum_proj[:, 896:].T, gains[width : 2 * width],
        sum_ffn[:, :ff], sum_ffn[:, ff : 2 * ff], sum_ffn[:, PAIR : PAIR + ff].T,
    )


def solution(mesh):
    return jax.shard_map(
        local,
        mesh=mesh,
        in_specs=(
            P(("seq", "head"), None),
            P(),
            P(None, "head"),
            P(None, "head"),
            P(None, "head"),
            P(None, "head"),
            P(None, None, "head", None),
            P(),
            P("head", None),
            P(),
            P(None, "head"),
            P(None, "head"),
            P("head", None),
            P("seq"),
            P("seq", None),
        ),
        out_specs=(
            P(("seq", "head"), None),
            P(("seq", "head"), None),
            P(),
            P("seq", "head"),
            P("seq", "head"),
            P("seq", "head"),
            P("seq", "head"),
            P(None, None, "head", "seq"),
            P(),
            P("head", "seq"),
            P(),
            P("seq", "head"),
            P("seq", "head"),
            P("head", "seq"),
        ),
        check_vma=False,
    )
```
